32 devices in a mesh: dp: 8 (over y, x, core), tensor: 4 (over z).
Axes of the slice: x: 2, y: 2, z: 4, core: 2. Of those that a mesh axis runs over, the one named last changes fastest.
Arguments:
- latents: float32 [8192, 768], P(('dp', 'tensor')), may hold values from -6 to 6
- inputs: bfloat16 [102400, 768], P(('dp', 'tensor')), may hold values from -6 to 6
- segment: int32 [102400], P(('dp', 'tensor')), may hold values from 0 to 2, as said below
- cross_weights: bfloat16 [3072, 768], P(('dp', 'tensor'))
- self_weights: bfloat16 [3072, 768], P(('dp', 'tensor'))
- vectors: bfloat16 [19, 768], P(None, ('dp', 'tensor'))
- up_weight: bfloat16 [768, 3072], P('dp', 'tensor'), may hold values from -0.21875 to 0.21875
- down_weight: bfloat16 [3072, 768], P('tensor', 'dp'), may hold values from -0.109375 to 0.109375
- cotangent: float32 [8192, 768], P(('dp', 'tensor')), may hold values from -6 to 6
Outputs:
- latents_out: float32 [8192, 768], P(('dp', 'tensor'))
- grad_latents: float32 [8192, 768], P(('dp', 'tensor'))
- grad_inputs: bfloat16 [102400, 768], P(('dp', 'tensor'))
- grad_cross: float32 [3072, 768], P(('dp', 'tensor'))
- grad_self: float32 [3072, 768], P(('dp', 'tensor'))
- grad_vectors: float32 [19, 768], P(None, ('dp', 'tensor'))
- grad_up: float32 [768, 3072], P('dp', 'tensor')
- grad_down: float32 [3072, 768], P('tensor', 'dp')
The draws below stay inside these ranges and needn't reach their ends.
Inputs may be any that keep to these rules, and one draw needn't show every extreme that they name: `segment`: on each device its 3200 tokens hold either one video of 3176 tokens in slot 0, or one to 2 images of 432 tokens each in slots 0, 1, ... in order; each sample's tokens are contiguous and start at the device's first token, slot numbers never fall, and the remaining tokens are padding marked 2. Slots without tokens hold latents that see no token.
All inputs are finite; a program needn't handle non-finite values.
Results may differ from the reference program's by a relative error of at most 0.015.
Values may be sent and summed in bfloat16 or wider, within the bound.
A program may use at most 192 MiB of HBM per device.

```python
import jax
import jax.numpy as jnp
from jax import lax

D = 768
HEADS = 12
HEAD_DIM = 64
FF = 3072
LAT = 128
SLOTS = 2
IMG_PATCHES = 392
VIDEO_PATCHES = 3136
TEXT_LEN = 40
TOK_DEV = 3200
TOKENS = 102400
SAMPLES = 64
VEC_ROWS = 19
N_DP = 8
N_TENSOR = 4


def block_weights(key, out_scale):
    normal_base = jax.random.normal(key, (4 * D, D), jnp.float32)
    block_index = jnp.arange(4 * D, dtype=jnp.int32) // D
    scales = jnp.where(block_index < 2, 1.3, jnp.where(block_index == 2, 1.0, out_scale))
    return normal_base * scales[:, None] * D ** (-0.5)


def draw_cross_weights(key, part):
    key = jax.random.fold_in(key, 1)
    return block_weights(key, 3.0).astype(jnp.bfloat16)


def draw_self_weights(key, part):
    key = jax.random.fold_in(key, 2)
    return block_weights(key, 2.0).astype(jnp.bfloat16)


def draw_vectors(key, part):
    key = jax.random.fold_in(key, 3)
    key_gain, key_bias = jax.random.split(key)
    row_index = jnp.arange(VEC_ROWS, dtype=jnp.int32)[:, None]
    gain_mask = (row_index == 0) | (row_index == 2) | (row_index == 7) | (row_index == 12)
    gains = 1.0 + 0.4 * jax.random.uniform(key_gain, (VEC_ROWS, D), jnp.float32, -1.0, 1.0)
    biases = 0.5 * jax.random.normal(key_bias, (VEC_ROWS, D), jnp.float32)
    return jnp.where(gain_mask, gains, biases).astype(jnp.bfloat16)


def draw_segment(key, part):
    key = jax.random.fold_in(key, 4)
    key_video, key_images = jax.random.split(key)
    device_count = TOKENS // TOK_DEV
    video_flag = jax.random.randint(key_video, (device_count, 1), 0, 2)
    image_count = jax.random.randint(key_images, (device_count, 1), 1, SLOTS + 1)
    position = jnp.arange(TOK_DEV, dtype=jnp.int32)[None, :]
    image_slot = position // (IMG_PATCHES + TEXT_LEN)
    image_segment = jnp.where(image_slot < image_count, image_slot, SLOTS)
    video_segment = jnp.where(position < VIDEO_PATCHES + TEXT_LEN, 0, SLOTS)
    segment_all = jnp.where(video_flag == 1, video_segment, image_segment)
    return segment_all.reshape(-1).astype(jnp.int32)


def steps_of(stream_key, dims, pieces, low, top_value):
    gain, own = 1.0, jax.random.fold_in(stream_key, 6)
    for axis_at, blocks in pieces:
        steps = jnp.exp(jax.random.uniform(jax.random.fold_in(own, axis_at), (blocks,), jnp.float32, low / len(pieces), top_value / len(pieces)))
        gain = gain * jnp.repeat(steps, dims[axis_at] // blocks).reshape([-1 if axis == axis_at else 1 for axis in range(len(dims))])
    return gain


def bell_draw(key, shape, width, reach, cuts=(), kind=jnp.bfloat16):
    entries = width * jax.random.normal(key, shape, jnp.float32)
    if cuts:
        entries = entries * steps_of(key, shape, cuts, -0.22, 0.18)
    return jnp.clip(entries, -reach, reach).astype(kind)


def setup_inputs(seed: int = 0) -> dict:
    key_list = jax.random.split(jax.random.key(seed), 10)
    return {
        "latents": bell_draw(key_list[0], (SAMPLES * LAT, D), 1.0, 6.0, ((0, 32),), jnp.float32),
        "inputs": bell_draw(key_list[1], (TOKENS, D), 1.0, 6.0, ((0, 32),)),
        "segment": draw_segment(jax.random.fold_in(key_list[9], 71), 0),
        "cross_weights": draw_cross_weights(jax.random.fold_in(key_list[9], 71), 0),
        "self_weights": draw_self_weights(jax.random.fold_in(key_list[9], 71), 0),
        "vectors": draw_vectors(jax.random.fold_in(key_list[9], 71), 0),
        "up_weight": bell_draw(key_list[6], (D, FF), D ** -0.5, 0.21875, ((0, 8), (1, 4))),
        "down_weight": bell_draw(key_list[7], (FF, D), FF ** -0.5, 0.109375, ((0, 4), (1, 8))),
        "cotangent": bell_draw(key_list[8], (SAMPLES * LAT, D), 1.0, 6.0, ((0, 32),), jnp.float32),
    }


@jax.custom_vjp
def low(v):
    return lax.optimization_barrier(v.astype(jnp.bfloat16)).astype(jnp.float32)

@jax.custom_vjp
def low_back(v):
    return v

def low_keep(v):
    return (low(v), None)

def low_pass(kept, grad):
    return (grad,)

def back_keep(v):
    return (v, None)

def back_low(kept, grad):
    return (low(grad),)
low.defvjp(low_keep, low_pass)
low_back.defvjp(back_keep, back_low)

def matmul(left, right):
    return jnp.dot(left, right, precision=lax.Precision.HIGHEST)

def both_ways(values):
    return low_back(low(values))

def layer_norm(values, gain_row, shift_row):
    average = lax.optimization_barrier(jnp.mean(values, axis=-1, keepdims=True))
    centred = values - average
    variance = lax.optimization_barrier(jnp.mean(centred * centred, axis=-1, keepdims=True))
    return centred * lax.rsqrt(variance + 1e-05) * gain_row + shift_row

def attention(queries, keys_in, values_in, visible):
    row_count = queries.shape[0]
    key_count = keys_in.shape[0]
    head_queries = queries.reshape(row_count, HEADS, HEAD_DIM)
    head_keys = keys_in.reshape(key_count, HEADS, HEAD_DIM)
    head_values = values_in.reshape(key_count, HEADS, HEAD_DIM)
    score_scale = HEAD_DIM ** (-0.5)
    scores = low_back(jnp.einsum('qhd,khd->hqk', head_queries, head_keys, precision=lax.Precision.HIGHEST) * score_scale)
    has_keys = jnp.any(visible, axis=-1, keepdims=True)
    peak_score = lax.optimization_barrier(jnp.max(jnp.where(visible, scores, -1000000000.0), axis=-1, keepdims=True))
    peak_score = jnp.where(has_keys, peak_score, 0.0)
    seen_float = visible.astype(jnp.float32)
    exponent = jnp.exp(jnp.where(visible, scores - peak_score, -200.0)) * seen_float
    denominator = lax.optimization_barrier(jnp.sum(exponent, axis=-1, keepdims=True)) + 1.0 - has_keys.astype(jnp.float32)
    attn_probs = low(exponent / denominator)
    outputs = both_ways(jnp.einsum('hqk,khd->qhd', attn_probs, head_values, precision=lax.Precision.HIGHEST))
    return outputs.reshape(row_count, HEADS * HEAD_DIM)

def device_forward(latent_rows, input_rows, segment_rows, cross_full, self_full, vector_rows, up_full, down_full):
    row_count = latent_rows.shape[0]
    slot_row = jnp.arange(row_count, dtype=jnp.int32) // LAT
    normed = low(layer_norm(latent_rows, vector_rows[0], vector_rows[1]))
    context = low(layer_norm(input_rows, vector_rows[2], vector_rows[3]))
    queries = both_ways(matmul(normed, cross_full[:D]) + vector_rows[4])
    keys_in = both_ways(matmul(context, cross_full[D:2 * D]))
    values_in = both_ways(matmul(context, cross_full[2 * D:3 * D]) + vector_rows[5])
    cross_seen = slot_row[:, None] == segment_rows[None, :]
    cross_read = attention(queries, keys_in, values_in, cross_seen)
    after_cross = latent_rows + low_back(matmul(cross_read, cross_full[3 * D:]) + vector_rows[6])
    normed_two = low(layer_norm(after_cross, vector_rows[7], vector_rows[8]))
    queries_two = both_ways(matmul(normed_two, self_full[:D]) + vector_rows[9])
    keys_two = both_ways(matmul(normed_two, self_full[D:2 * D]))
    values_two = both_ways(matmul(normed_two, self_full[2 * D:3 * D]) + vector_rows[10])
    self_seen = slot_row[:, None] == slot_row[None, :]
    self_read = attention(queries_two, keys_two, values_two, self_seen)
    after_self = after_cross + low_back(matmul(self_read, self_full[3 * D:]) + vector_rows[11])
    normed_three = low(layer_norm(after_self, vector_rows[12], vector_rows[13]))
    pre_act = low_back(matmul(normed_three, up_full) + vector_rows[15:].reshape(FF))
    hidden = low(jax.nn.gelu(pre_act, approximate=False))
    return after_self + low_back(matmul(hidden, down_full) + vector_rows[14])

def reference(latents, inputs, segment, cross_weights, self_weights, vectors, up_weight, down_weight, cotangent):
    device_count = N_DP * N_TENSOR
    rows_each = SLOTS * LAT
    weights = (cross_weights.astype(jnp.float32), self_weights.astype(jnp.float32), vectors.astype(jnp.float32), up_weight.astype(jnp.float32), down_weight.astype(jnp.float32))

    def per_device(running, device_index):
        latent_rows = lax.dynamic_slice_in_dim(latents, device_index * rows_each, rows_each, 0)
        input_rows = lax.dynamic_slice_in_dim(inputs, device_index * TOK_DEV, TOK_DEV, 0).astype(jnp.float32)
        segment_rows = lax.dynamic_slice_in_dim(segment, device_index * TOK_DEV, TOK_DEV, 0)
        cot_rows = lax.dynamic_slice_in_dim(cotangent, device_index * rows_each, rows_each, 0)

        def forward(lat_value, inp_value, weight_set):
            return device_forward(lat_value, inp_value, segment_rows, *weight_set)
        result, pullback = jax.vjp(forward, latent_rows, input_rows, weights)
        grad_lat, grad_inp, grad_weights = pullback(cot_rows)
        running = jax.tree.map(jnp.add, running, grad_weights)
        return (running, (result, grad_lat, grad_inp.astype(jnp.bfloat16)))
    start_sums = jax.tree.map(jnp.zeros_like, weights)
    totals, stacked = lax.scan(per_device, start_sums, jnp.arange(device_count, dtype=jnp.int32))
    results, grad_lats, grad_inps = stacked
    return (results.reshape(-1, D), grad_lats.reshape(-1, D), grad_inps.reshape(-1, D), totals[0], totals[1], totals[2], totals[3], totals[4])
```

```python
from functools import partial

import jax
import jax.numpy as jnp
from jax import lax
from jax.experimental import pallas as pl
from jax.experimental.pallas import tpu as pltpu
from jax.sharding import PartitionSpec as P

D = 768
HEAD_DIM = 64
FF = 3072
LAT = 128


def cut_along(x, dim, size):
    before, after = (x.shape[:dim], x.shape[dim + 1 :])
    return jnp.moveaxis(x.reshape(*before, size, -1, *after), dim, 0)


def sent_and_summed(x, axis, dim):
    parts = cut_along(x, dim, lax.axis_size(axis))
    arrived = lax.all_to_all(parts, axis, split_axis=0, concat_axis=0, tiled=True)
    return arrived.astype(jnp.float32).sum(axis=0)


def product(left, right):
    return jnp.dot(left, right, preferred_element_type=jnp.float32)


def product_tn(left, right):
    return lax.dot_general(
        left, right, (((0,), (0,)), ((), ())), preferred_element_type=jnp.float32
    )


def product_nt(left, right):
    return lax.dot_general(
        left, right, (((1,), (1,)), ((), ())), preferred_element_type=jnp.float32
    )


def layer_norm(values, gain_row, shift_row):
    average = jnp.mean(values, axis=-1, keepdims=True)
    centred = values - average
    variance = jnp.mean(centred * centred, axis=-1, keepdims=True)
    return centred * lax.rsqrt(variance + 1e-05) * gain_row + shift_row


def norm_backward(values, gain_row, shift_row, incoming):
    unused, pullback = jax.vjp(layer_norm, values, gain_row, shift_row)
    return pullback(incoming)


def split_heads(values):
    return values.reshape(values.shape[0], -1, HEAD_DIM).transpose(1, 0, 2)


def merge_heads(values):
    return values.transpose(1, 0, 2).reshape(values.shape[1], -1)


def head_probs(head_query, head_key, visible, peak_score, denominator):
    scores = product_nt(head_query, head_key) * HEAD_DIM ** (-0.5)
    exponent = jnp.exp(jnp.where(visible, scores - peak_score, -200.0)) * visible.astype(
        jnp.float32
    )
    return exponent / denominator


def attend_forward(queries, keys_in, values_in, visible):
    has_keys = jnp.any(visible, axis=-1, keepdims=True)
    seen_float = visible.astype(jnp.float32)

    def one_head(operands):
        head_query, head_key, head_value = operands
        scores = product_nt(head_query, head_key) * HEAD_DIM ** (-0.5)
        peak_score = jnp.max(jnp.where(visible, scores, -1000000000.0), axis=-1, keepdims=True)
        peak_score = jnp.where(has_keys, peak_score, 0.0)
        exponent = jnp.exp(jnp.where(visible, scores - peak_score, -200.0)) * seen_float
        denominator = jnp.sum(exponent, axis=-1, keepdims=True) + 1.0 - has_keys.astype(jnp.float32)
        attn_probs = (exponent / denominator).astype(jnp.bfloat16)
        return (product(attn_probs, head_value), peak_score, denominator)

    outputs, peaks, denominators = lax.map(
        one_head, (split_heads(queries), split_heads(keys_in), split_heads(values_in))
    )
    return (merge_heads(outputs).astype(jnp.bfloat16), peaks, denominators)


def attend_backward(queries, keys_in, values_in, visible, peaks, denominators, grad_read):
    score_scale = HEAD_DIM ** (-0.5)

    def one_head(operands):
        head_query, head_key, head_value, peak_score, denominator, head_grad = operands
        attn_probs = head_probs(head_query, head_key, visible, peak_score, denominator)
        grad_probs = product_nt(head_grad, head_value)
        grad_value = product_tn(attn_probs.astype(jnp.bfloat16), head_grad)
        inner_sum = jnp.sum(grad_probs * attn_probs, axis=-1, keepdims=True)
        grad_scores = (attn_probs * (grad_probs - inner_sum)).astype(jnp.bfloat16)
        grad_query = product(grad_scores, head_key) * score_scale
        grad_key = product_tn(grad_scores, head_query) * score_scale
        return (grad_query, grad_key, grad_value)

    grad_q, grad_k, grad_v = lax.map(
        one_head,
        (
            split_heads(queries),
            split_heads(keys_in),
            split_heads(values_in),
            peaks,
            denominators,
            split_heads(grad_read),
        ),
    )
    return (
        merge_heads(grad_q).astype(jnp.bfloat16),
        merge_heads(grad_k).astype(jnp.bfloat16),
        merge_heads(grad_v).astype(jnp.bfloat16),
    )


def column_sum(values):
    return jnp.sum(values.astype(jnp.float32), axis=0)


def local(
    latents,
    inputs,
    segment,
    cross_weights,
    self_weights,
    vectors,
    up_weight,
    down_weight,
    cotangent,
):
    cross_full, self_full, vector_half = (
        lax.all_gather(cross_weights, ("dp", "tensor"), axis=0, tiled=True),
        lax.all_gather(self_weights, ("dp", "tensor"), axis=0, tiled=True),
        lax.all_gather(vectors, ("dp", "tensor"), axis=1, tiled=True),
    )
    up_full, down_full = (
        lax.all_gather(up_weight, "dp", axis=0, tiled=True),
        lax.all_gather(down_weight, "dp", axis=1, tiled=True),
    )
    vector_rows = vector_half.astype(jnp.float32)
    quarter = up_full.shape[1]
    part_index = lax.axis_index("tensor")
    bias_up = lax.dynamic_slice_in_dim(
        vector_rows[15:].reshape(-1), part_index * quarter, quarter, 0
    )
    row_count = latents.shape[0]
    slot_row = jnp.arange(row_count, dtype=jnp.int32) // LAT
    cross_seen = slot_row[:, None] == segment[None, :]
    self_seen = slot_row[:, None] == slot_row[None, :]
    input_float = inputs.astype(jnp.float32)
    normed = layer_norm(latents, vector_rows[0], vector_rows[1]).astype(jnp.bfloat16)
    context = layer_norm(input_float, vector_rows[2], vector_rows[3]).astype(jnp.bfloat16)
    queries = (product(normed, cross_full[:D]) + vector_rows[4]).astype(jnp.bfloat16)
    keys_in = product(context, cross_full[D : 2 * D]).astype(jnp.bfloat16)
    values_in = (product(context, cross_full[2 * D : 3 * D]) + vector_rows[5]).astype(jnp.bfloat16)
    cross_read, cross_peaks, cross_denoms = attend_forward(queries, keys_in, values_in, cross_seen)
    after_cross = latents + (product(cross_read, cross_full[3 * D :]) + vector_rows[6])
    normed_two = layer_norm(after_cross, vector_rows[7], vector_rows[8]).astype(jnp.bfloat16)
    queries_two = (product(normed_two, self_full[:D]) + vector_rows[9]).astype(jnp.bfloat16)
    keys_two = product(normed_two, self_full[D : 2 * D]).astype(jnp.bfloat16)
    values_two = (product(normed_two, self_full[2 * D : 3 * D]) + vector_rows[10]).astype(
        jnp.bfloat16
    )
    self_read, self_peaks, self_denoms = attend_forward(
        queries_two, keys_two, values_two, self_seen
    )
    after_self = after_cross + (product(self_read, self_full[3 * D :]) + vector_rows[11])
    normed_three = layer_norm(after_self, vector_rows[12], vector_rows[13]).astype(jnp.bfloat16)
    gathered = lax.all_gather(normed_three, "tensor", axis=0, tiled=True)
    pre_act = product(gathered, up_full) + bias_up
    hidden = jax.nn.gelu(pre_act, approximate=False).astype(jnp.bfloat16)
    reduced = lax.psum_scatter(
        product(hidden, down_full).astype(jnp.bfloat16), "tensor", scatter_dimension=0, tiled=True
    ).astype(jnp.float32)
    latents_out = after_self + (reduced + vector_rows[14])
    cross_full, self_full, vector_half = (
        lax.all_gather(cross_weights, ("dp", "tensor"), axis=0, tiled=True),
        lax.all_gather(self_weights, ("dp", "tensor"), axis=0, tiled=True),
        lax.all_gather(vectors, ("dp", "tensor"), axis=1, tiled=True),
    )
    up_full, down_full = (
        lax.all_gather(up_weight, "dp", axis=0, tiled=True),
        lax.all_gather(down_weight, "dp", axis=1, tiled=True),
    )
    vector_rows = vector_half.astype(jnp.float32)
    grad_y = cotangent.astype(jnp.bfloat16)
    grad_b2 = column_sum(grad_y)
    grad_rows = lax.all_gather(grad_y, "tensor", axis=0, tiled=True)
    grad_down = product_tn(hidden, grad_rows)
    grad_hidden = product_nt(grad_rows, down_full)
    unused, gelu_pull = jax.vjp(partial(jax.nn.gelu, approximate=False), pre_act)
    grad_pre = gelu_pull(grad_hidden)[0].astype(jnp.bfloat16)
    grad_b1 = column_sum(grad_pre)
    grad_up = product_tn(gathered, grad_pre)
    mlp_sums = (
        sent_and_summed(grad_up.astype(jnp.bfloat16), "dp", 0),
        sent_and_summed(grad_down.astype(jnp.bfloat16), "dp", 1),
    )
    grad_normed_three = lax.psum_scatter(
        product_nt(grad_pre, up_full).astype(jnp.bfloat16),
        "tensor",
        scatter_dimension=0,
        tiled=True,
    ).astype(jnp.float32)
    back_self, grad_gain_three, grad_shift_three = norm_backward(
        after_self, vector_rows[12], vector_rows[13], grad_normed_three
    )
    grad_after_self = cotangent + back_self
    grad_out_two = grad_after_self.astype(jnp.bfloat16)
    grad_bias_out_two = column_sum(grad_out_two)
    grad_wo_two = product_tn(self_read, grad_out_two)
    grad_read_two = product_nt(grad_out_two, self_full[3 * D :]).astype(jnp.bfloat16)
    grad_q_two, grad_k_two, grad_v_two = attend_backward(
        queries_two, keys_two, values_two, self_seen, self_peaks, self_denoms, grad_read_two
    )
    grad_self = jnp.concatenate(
        [
            product_tn(normed_two, grad_q_two),
            product_tn(normed_two, grad_k_two),
            product_tn(normed_two, grad_v_two),
            grad_wo_two,
        ],
        axis=0,
    )
    grad_normed_two = (
        product_nt(grad_q_two, self_full[:D])
        + product_nt(grad_k_two, self_full[D : 2 * D])
        + product_nt(grad_v_two, self_full[2 * D : 3 * D])
    )
    back_cross, grad_gain_two, grad_shift_two = norm_backward(
        after_cross, vector_rows[7], vector_rows[8], grad_normed_two
    )
    grad_after_cross = grad_after_self + back_cross
    grad_out_one = grad_after_cross.astype(jnp.bfloat16)
    grad_bias_out_one = column_sum(grad_out_one)
    grad_wo_one = product_tn(cross_read, grad_out_one)
    grad_read_one = product_nt(grad_out_one, cross_full[3 * D :]).astype(jnp.bfloat16)
    grad_q_one, grad_k_one, grad_v_one = attend_backward(
        queries, keys_in, values_in, cross_seen, cross_peaks, cross_denoms, grad_read_one
    )
    grad_cross = jnp.concatenate(
        [
            product_tn(normed, grad_q_one),
            product_tn(context, grad_k_one),
            product_tn(context, grad_v_one),
            grad_wo_one,
        ],
        axis=0,
    )
    grad_normed = product_nt(grad_q_one, cross_full[:D])
    back_latent, grad_gain_one, grad_shift_one = norm_backward(
        latents, vector_rows[0], vector_rows[1], grad_normed
    )
    grad_latents = grad_after_cross + back_latent
    grad_context = product_nt(grad_k_one, cross_full[D : 2 * D]) + product_nt(
        grad_v_one, cross_full[2 * D : 3 * D]
    )
    back_input, grad_gain_input, grad_shift_input = norm_backward(
        input_float, vector_rows[2], vector_rows[3], grad_context
    )
    grad_inputs = back_input.astype(jnp.bfloat16)
    full_bias = lax.dynamic_update_slice_in_dim(
        jnp.zeros((FF,), jnp.float32), grad_b1, part_index * quarter, 0
    )
    grad_vectors = jnp.concatenate(
        [
            jnp.stack(
                [
                    grad_gain_one,
                    grad_shift_one,
                    grad_gain_input,
                    grad_shift_input,
                    column_sum(grad_q_one),
                    column_sum(grad_v_one),
                    grad_bias_out_one,
                    grad_gain_two,
                    grad_shift_two,
                    column_sum(grad_q_two),
                    column_sum(grad_v_two),
                    grad_bias_out_two,
                    grad_gain_three,
                    grad_shift_three,
                    grad_b2,
                ],
                axis=0,
            ),
            full_bias.reshape(-1, D),
        ],
        axis=0,
    )
    cross_sums, self_sums, vector_sums = (
        lax.psum_scatter(grad_cross, ("dp", "tensor"), scatter_dimension=0, tiled=True),
        lax.psum_scatter(grad_self, ("dp", "tensor"), scatter_dimension=0, tiled=True),
        lax.psum_scatter(grad_vectors, ("dp", "tensor"), scatter_dimension=1, tiled=True),
    )
    return (
        latents_out,
        grad_latents,
        grad_inputs,
        cross_sums,
        self_sums,
        vector_sums,
        mlp_sums[0],
        mlp_sums[1],
    )


BF = jnp.bfloat16
F32 = jnp.float32
MESH = pl.DeviceIdType.MESH
TILE = 256
PAD = 128
GROUP = 256
GROUPS = D // GROUP
GHEADS = GROUP // HEAD_DIM
LANES = 128
HIDE = -1e30
VEC_PAD = 32
NROWS = 4 * D
SLOT1_FIRST = 2
SLOT1_TILES = 2
VMEM_LIMIT = 63 * 1024 * 1024


def nn(left, right):
    return jnp.dot(left, right, preferred_element_type=F32)


def nt(left, right):
    return lax.dot_general(
        left, right, (((1,), (1,)), ((), ())), preferred_element_type=F32
    )


def ln_parts(values):
    average = jnp.mean(values, axis=-1, keepdims=True)
    centred = values - average
    variance = jnp.mean(centred * centred, axis=-1, keepdims=True)
    scale = lax.rsqrt(variance + 1e-05)
    return centred * scale, scale


def ln_rows(values, gain_row, shift_row):
    return ln_parts(values)[0] * gain_row + shift_row


def neighbours(tensor_count):
    dp = lax.axis_index("dp")
    z = lax.axis_index("tensor")
    core = lax.rem(dp, 2)
    flip_x = dp + 2 * (1 - 2 * lax.rem(dp // 2, 2))
    flip_y = dp + 4 * (1 - 2 * (dp // 4))
    other = dp + 1 - 2 * core
    first = (1 - core) * flip_x + core * flip_y
    second = (1 - core) * flip_y + core * flip_x
    both = flip_x + flip_y - dp
    peers = [lax.rem(z + step, tensor_count) for step in range(1, tensor_count)]
    return dp, z, core, other, first, second, both, peers


def meet(dp, z, other, first, second, peers):
    barrier = pltpu.get_barrier_semaphore()
    devices = [(other, z), (first, z), (second, z)] + [(dp, peer) for peer in peers]
    for device in devices:
        pl.semaphore_signal(barrier, inc=1, device_id=device, device_id_type=MESH)
    pl.semaphore_wait(barrier, len(devices))


def head_mask(rows):
    row_head = lax.broadcasted_iota(jnp.int32, (rows, GROUP), 0) // LAT
    col_head = lax.broadcasted_iota(jnp.int32, (rows, GROUP), 1) // HEAD_DIM
    return row_head == col_head


def spread_heads(block, mask):
    wide = jnp.concatenate([block.astype(F32)] * GHEADS, axis=0)
    return jnp.where(mask, wide, 0.0).astype(BF)


def pick_heads(stacked):
    col_head = lax.broadcasted_iota(jnp.int32, (LAT, GROUP), 1) // HEAD_DIM
    total = jnp.zeros((LAT, GROUP), F32)
    for head in range(GHEADS):
        part = stacked[head * LAT : (head + 1) * LAT]
        total = total + jnp.where(col_head == head, part, 0.0)
    return total


def forward_kernel(
    tensor_count,
    lat,
    inp,
    seg,
    cross_shard,
    self_shard,
    up_shard,
    down_shard,
    vec_own,
    cot,
    out_o,
    wc_o,
    ws_o,
    ctx_o,
    key_o,
    val_o,
    prob_o,
    gup_o,
    gdn_o,
    vec_o,
    query_o,
    read_o,
    mid_o,
    query2_o,
    key2_o,
    val2_o,
    prob2_o,
    read2_o,
    late_o,
    gn3_o,
    gb1_o,
    w_cross,
    w_self,
    w_up,
    w_down,
    ctx,
    keys,
    vals,
    scores,
    probs,
    inbuf,
    qbd,
    peak,
    denom,
    oacc,
    norm_t,
    gy_t,
    vec_in,
    vec_sum,
    send_sem,
    recv_sem,
    vec_ssem,
    vec_rsem,
    in_sem,
    out_sem,
):
    dp, z, core, other, first, second, both, peers = neighbours(tensor_count)
    meet(dp, z, other, first, second, peers)
    weights = (w_cross, w_self, w_up, w_down)
    shards = (cross_shard, self_shard, up_shard, down_shard)
    shard_rows = cross_shard.shape[0]
    tiles = ctx.shape[0] // TILE
    chunk_count = 4 * tensor_count
    kinds = 7

    def place(unit, owner, part):
        if unit < 2:
            start = (owner * tensor_count + part) * shard_rows
        else:
            start = part * D + owner * shard_rows
        return pl.ds(pl.multiple_of(start, shard_rows), shard_rows)

    def remote(source, target, number, device):
        return pltpu.make_async_remote_copy(
            src_ref=source,
            dst_ref=target,
            send_sem=send_sem.at[number],
            recv_sem=recv_sem.at[number],
            device_id=device,
            device_id_type=MESH,
        )

    def z_copy(unit, step):
        rows = place(unit, dp, z)
        number = chunk_count * kinds + unit * (tensor_count - 1) + step - 1
        return remote(shards[unit], weights[unit].at[rows], number, (dp, peers[step - 1]))

    def plane_copy(chunk, kind):
        unit, step = divmod(chunk, tensor_count)
        part = lax.rem(z - step + tensor_count, tensor_count)
        owner = (dp, dp, first, dp, first, second, both)[kind]
        target = (first, second, second, other, other, other, other)[kind]
        rows = place(unit, owner, part)
        return remote(
            weights[unit].at[rows], weights[unit].at[rows], chunk * kinds + kind, (target, z)
        )

    def z_start(unit):
        for step in range(1, tensor_count):
            z_copy(unit, step).start()

    def stage0(chunk):
        unit, step = divmod(chunk, tensor_count)
        if step:
            z_copy(unit, step).wait_recv()
        for kind in (0, 1, 3):
            plane_copy(chunk, kind).start()

    def stage1(chunk):
        plane_copy(chunk, 0).wait_recv()
        for kind in (2, 4):
            plane_copy(chunk, kind).start()

    def stage2(chunk):
        plane_copy(chunk, 1).wait_recv()
        plane_copy(chunk, 5).start()
        plane_copy(chunk, 2).wait_recv()
        plane_copy(chunk, 6).start()

    def stage3(chunk):
        for kind in (3, 4, 5, 6):
            plane_copy(chunk, kind).wait_recv()

    def comm(step):
        if step < chunk_count:
            stage0(step)
        for lag, stage in ((1, stage1), (2, stage2), (3, stage3)):
            if 0 <= step - lag < chunk_count:
                stage(step - lag)
        if step % tensor_count == tensor_count - 2 and step // tensor_count < 3:
            z_start(step // tensor_count + 1)

    def vec_copy(hop):
        if hop < tensor_count - 1:
            source, device = vec_own, (dp, peers[hop])
        else:
            level = hop - (tensor_count - 1)
            source, device = vec_sum.at[level], ((first, second, other)[level], z)
        return pltpu.make_async_remote_copy(
            src_ref=source,
            dst_ref=vec_in.at[hop],
            send_sem=vec_ssem.at[hop],
            recv_sem=vec_rsem.at[hop],
            device_id=device,
            device_id_type=MESH,
        )

    def read_in(index):
        rows = inbuf.shape[1]
        start = pl.multiple_of(index * rows, rows)
        slot = lax.rem(index, 2)
        return pltpu.make_async_copy(
            inp.at[pl.ds(start, rows)], inbuf.at[slot], in_sem.at[slot]
        )

    def keep(source, target, number):
        return pltpu.make_async_copy(source, target, out_sem.at[number])

    for hop in range(tensor_count - 1):
        vec_copy(hop).start()
    for unit in range(4):
        weights[unit][place(unit, dp, z), :] = shards[unit][...]
    z_start(0)
    read_in(0).start()
    comm(0)
    for hop in range(tensor_count - 1):
        vec_copy(hop).wait_recv()
    total = vec_own[...].astype(F32)
    for hop in range(tensor_count - 1):
        total = total + vec_in[hop].astype(F32)
    for level in range(3):
        vec_sum[level] = total.astype(BF)
        hop = tensor_count - 1 + level
        vec_copy(hop).start()
        if level == 1:
            comm(1)
        vec_copy(hop).wait_recv()
        total = total + vec_in[hop].astype(F32)
    vec_o[...] = total

    def vec(row):
        return vec_o[row : row + 1, :]

    ctx[0:PAD, :] = jnp.zeros((PAD, D), BF)
    in_rows = inbuf.shape[1]
    reads = inp.shape[0] // in_rows

    def norm_inputs(index, carry):
        @pl.when(index + 1 < reads)
        def _():
            read_in(index + 1).start()

        read_in(index).wait()
        slot = lax.rem(index, 2)

        def rows_of(part, carry2):
            start = pl.multiple_of(part * 64, 64)
            values = inbuf[slot, pl.ds(start, 64), :].astype(F32)
            ctx[pl.ds(pl.multiple_of(PAD + index * in_rows + start, 64), 64), :] = ln_rows(
                values, vec(2), vec(3)
            ).astype(BF)
            return carry2

        lax.fori_loop(0, in_rows // 64, rows_of, 0)

        @pl.when(index == 2)
        def _():
            comm(2)

        @pl.when(index == 7)
        def _():
            comm(3)

        return carry

    lax.fori_loop(0, reads, norm_inputs, 0)
    normed = ln_rows(lat[...], vec(0), vec(1)).astype(BF)
    gy = cot[...].astype(BF)
    gy_t[...] = cot[...].T.astype(BF)
    for step in (4, 5, 6):
        comm(step)
    keep(w_cross, wc_o, 0).start()
    mask = head_mask(GHEADS * LAT)

    query = (nn(normed, w_cross[0:D, :]) + vec(4)).astype(BF)
    scaled = (query.astype(F32) * HEAD_DIM ** (-0.5)).astype(BF)
    query_o[...] = scaled
    for slot in range(2):
        for group in range(GROUPS):
            block = scaled[slot * LAT : (slot + 1) * LAT, group * GROUP : (group + 1) * GROUP]
            qbd[slot * GROUPS + group] = spread_heads(block, mask)

    def project(index, carry):
        rows = pl.ds(pl.multiple_of(index * TILE, TILE), TILE)
        block = ctx[rows, :]
        keys[rows, :] = nn(block, w_cross[D : 2 * D, :]).astype(BF)
        vals[rows, :] = (nn(block, w_cross[2 * D : 3 * D, :]) + vec(5)).astype(BF)

        @pl.when(index == 4)
        def _():
            comm(7)

        @pl.when(index == 9)
        def _():
            comm(8)

        return carry

    lax.fori_loop(0, tiles, project, 0)
    keep(ctx, ctx_o, 1).start()
    keep(keys, key_o, 2).start()
    keep(vals, val_o, 3).start()

    virtual = tiles + SLOT1_TILES

    def slot_and_rows(index):
        slot = index // tiles
        tile = index - slot * (tiles - SLOT1_FIRST)
        return slot, pl.ds(pl.multiple_of(tile * TILE, TILE), TILE)

    def cols_of(index):
        return pl.ds(pl.multiple_of(index * TILE, TILE), TILE)

    seen = []
    for slot in range(2):
        hit = jnp.where(seg[...] == slot, 1.0, 0.0)
        seen.append(jnp.max(hit, axis=1, keepdims=True))

    for group in range(GROUPS):
        gcols = slice(group * GROUP, (group + 1) * GROUP)
        peak[...] = jnp.full(peak.shape, HIDE, F32)
        denom[...] = jnp.zeros(denom.shape, F32)
        oacc[...] = jnp.zeros(oacc.shape, F32)

        def score(index, carry):
            slot, rows = slot_and_rows(index)
            values = nt(qbd[slot * GROUPS + group], keys[rows, gcols])
            visible = seg[:, rows] == slot
            values = jnp.where(visible, values, HIDE)
            scores[:, cols_of(index)] = values
            top = jnp.maximum(values[:, :LANES], values[:, LANES:])
            peak[slot] = jnp.maximum(peak[slot], top)
            return carry

        lax.fori_loop(0, virtual, score, 0)
        for slot in range(2):
            top = jnp.max(peak[slot], axis=1, keepdims=True)
            top = jnp.where(seen[slot] > 0.0, top, 0.0)
            peak[slot] = jnp.broadcast_to(top, (GHEADS * LAT, LANES))
        comm(9 + group)

        def weigh(index, carry):
            slot, rows = slot_and_rows(index)
            for head in range(GHEADS):
                part = slice(head * LAT, (head + 1) * LAT)
                values = scores[part, cols_of(index)]
                top = peak[slot, part, :]
                low = jnp.exp(values[:, :LANES] - top)
                high = jnp.exp(values[:, LANES:] - top)
                scores[part, cols_of(index)] = jnp.concatenate([low, high], axis=1)
                denom[slot, part, :] += low + high
            return carry

        lax.fori_loop(0, virtual, weigh, 0)
        for slot in range(2):
            total = jnp.sum(denom[slot], axis=1, keepdims=True) + 1.0 - seen[slot]
            denom[slot] = jnp.broadcast_to(1.0 / total, (GHEADS * LAT, LANES))
        if group:
            keep(probs, prob_o.at[group - 1], 4).wait()

        def spread(index, carry):
            slot, rows = slot_and_rows(index)
            values = scores[:, cols_of(index)]
            scale = denom[slot]
            values = values * jnp.concatenate([scale, scale], axis=1)
            values = values.astype(BF)
            probs[:, cols_of(index)] = values
            oacc[slot] += nn(values, vals[rows, gcols])
            return carry

        lax.fori_loop(0, virtual, spread, 0)
        keep(probs, prob_o.at[group], 4).start()
        for slot in range(2):
            read_o[slot * LAT : (slot + 1) * LAT, gcols] = pick_heads(oacc[slot])

    mid = lat[...] + (nn(read_o[...].astype(BF), w_cross[3 * D :, :]) + vec(6))
    mid_o[...] = mid
    normed_two = ln_rows(mid, vec(7), vec(8)).astype(BF)
    keep(w_self, ws_o, 5).start()
    query_two = (nn(normed_two, w_self[0:D, :]) + vec(9)).astype(BF)
    query2_o[...] = (query_two.astype(F32) * HEAD_DIM ** (-0.5)).astype(BF)
    key2_o[...] = nn(normed_two, w_self[D : 2 * D, :]).astype(BF)
    val2_o[...] = (nn(normed_two, w_self[2 * D : 3 * D, :]) + vec(10)).astype(BF)
    comm(12)
    for slot in range(2):
        srows = slice(slot * LAT, (slot + 1) * LAT)
        for group in range(GROUPS):
            gcols = slice(group * GROUP, (group + 1) * GROUP)
            wide = spread_heads(query2_o[srows, gcols], mask)
            values = nt(wide, key2_o[srows, gcols])
            values = jnp.exp(values - jnp.max(values, axis=1, keepdims=True))
            values = values / jnp.sum(values, axis=1, keepdims=True)
            values = values.astype(BF)
            prob2_o[slot, group] = values
            read2_o[srows, gcols] = pick_heads(nn(values, val2_o[srows, gcols]))
    late = mid_o[...] + (nn(read2_o[...].astype(BF), w_self[3 * D :, :]) + vec(11))
    late_o[...] = late
    normed_three = ln_rows(late, vec(12), vec(13))
    norm_t[...] = normed_three.T.astype(BF)
    normed_three = normed_three.astype(BF)
    comm(13)
    keep(probs, prob_o.at[GROUPS - 1], 4).wait()
    keep(keys, key_o, 2).wait()
    keep(vals, val_o, 3).wait()

    rows_all = slice(0, 2 * LAT)

    def quarter(step):
        part = lax.rem(z - step + tensor_count, tensor_count)
        return part, pl.ds(pl.multiple_of(part * D, D), D)

    def up_part(step):
        part, rows = quarter(step)
        cols = slice(step * D, (step + 1) * D)
        pre = nn(normed_three, w_up[rows, :]) + vec_o[pl.ds(15 + part, 1), :]
        half = 0.5 * (1.0 + lax.erf(pre * 0.5**0.5))
        slope = half + pre * jnp.exp(-0.5 * pre * pre) * 0.3989422804014327
        hidden = (pre * half).astype(BF)
        probs[rows_all, cols] = hidden
        scores[rows_all, cols] = slope
        vals[rows, :] = nn(gy_t[...], hidden).astype(BF)
        keep(vals.at[rows], gdn_o.at[rows], 6 + step).start()

    def down_part(step):
        part, rows = quarter(step)
        cols = slice(step * D, (step + 1) * D)
        down = w_down[rows, :]
        y_part = nt(probs[rows_all, cols], down)
        grad_pre = (scores[rows_all, cols] * nn(gy, down)).astype(BF)
        keys[rows, :] = nn(norm_t[...], grad_pre).astype(BF)
        keep(keys.at[rows], gup_o.at[rows], 6 + tensor_count + step).start()
        x_part = nt(grad_pre, w_up[rows, :])
        if step == 0:
            out_o[...] = late_o[...] + vec(14) + y_part
            gn3_o[...] = x_part
        else:
            out_o[...] += y_part
            gn3_o[...] += x_part
        gb1_o[pl.ds(part, 1), :] = jnp.sum(grad_pre.astype(F32), axis=0, keepdims=True)

    gb1_o[...] = jnp.zeros(gb1_o.shape, F32)
    up_part(0)
    for step in range(1, tensor_count):
        comm(13 + step)
        up_part(step)
    comm(17)
    down_part(0)
    down_part(1)
    down_part(2)
    comm(18)
    down_part(3)
    keep(w_cross, wc_o, 0).wait()
    keep(ctx, ctx_o, 1).wait()
    keep(w_self, ws_o, 5).wait()
    for step in range(tensor_count):
        part, rows = quarter(step)
        keep(vals.at[rows], gdn_o.at[rows], 6 + step).wait()
        keep(keys.at[rows], gup_o.at[rows], 6 + tensor_count + step).wait()
    for hop in range(tensor_count + 2):
        vec_copy(hop).wait_send()
    for unit in range(4):
        for step in range(1, tensor_count):
            z_copy(unit, step).wait_send()
    for chunk in range(chunk_count):
        for kind in range(kinds):
            plane_copy(chunk, kind).wait_send()


def forward_call(tensor_count, lat, inp, seg, cross_w, self_w, up_w, down_w, vec_own, cot):
    rows = lat.shape[0]
    tokens = inp.shape[0] + PAD
    virtual = (tokens // TILE + SLOT1_TILES) * TILE
    sds = jax.ShapeDtypeStruct
    hbm = pl.BlockSpec(memory_space=pl.ANY)
    vmem = pl.BlockSpec(memory_space=pltpu.VMEM)
    stacked = GHEADS * LAT
    copies = 4 * tensor_count * 7 + 4 * (tensor_count - 1)
    outs = [
        (sds((rows, D), F32), vmem),
        (sds((NROWS, D), BF), hbm),
        (sds((NROWS, D), BF), hbm),
        (sds((tokens, D), BF), hbm),
        (sds((tokens, D), BF), hbm),
        (sds((tokens, D), BF), hbm),
        (sds((GROUPS, stacked, virtual), BF), hbm),
        (sds((NROWS, D), BF), hbm),
        (sds((NROWS, D), BF), hbm),
        (sds((VEC_PAD, D), F32), vmem),
        (sds((rows, D), BF), vmem),
        (sds((rows, D), F32), vmem),
        (sds((rows, D), F32), vmem),
        (sds((rows, D), BF), vmem),
        (sds((rows, D), BF), vmem),
        (sds((rows, D), BF), vmem),
        (sds((2, GROUPS, stacked, LAT), BF), vmem),
        (sds((rows, D), F32), vmem),
        (sds((rows, D), F32), vmem),
        (sds((rows, D), F32), vmem),
        (sds((8, D), F32), vmem),
    ]
    return pl.pallas_call(
        partial(forward_kernel, tensor_count),
        out_shape=[shape for shape, spec in outs],
        out_specs=[spec for shape, spec in outs],
        in_specs=[vmem, hbm, vmem, vmem, vmem, vmem, vmem, vmem, vmem],
        scratch_shapes=[
            pltpu.VMEM((NROWS, D), BF),
            pltpu.VMEM((NROWS, D), BF),
            pltpu.VMEM((NROWS, D), BF),
            pltpu.VMEM((NROWS, D), BF),
            pltpu.VMEM((tokens, D), BF),
            pltpu.VMEM((tokens, D), BF),
            pltpu.VMEM((tokens, D), BF),
            pltpu.VMEM((stacked, virtual), F32),
            pltpu.VMEM((stacked, virtual), BF),
            pltpu.VMEM((2, 320, D), BF),
            pltpu.VMEM((2 * GROUPS, stacked, GROUP), BF),
            pltpu.VMEM((2, stacked, LANES), F32),
            pltpu.VMEM((2, stacked, LANES), F32),
            pltpu.VMEM((2, stacked, GROUP), F32),
            pltpu.VMEM((D, rows), BF),
            pltpu.VMEM((D, rows), BF),
            pltpu.VMEM((tensor_count + 2, VEC_PAD, D), BF),
            pltpu.VMEM((3, VEC_PAD, D), BF),
            pltpu.SemaphoreType.DMA((copies,)),
            pltpu.SemaphoreType.DMA((copies,)),
            pltpu.SemaphoreType.DMA((tensor_count + 2,)),
            pltpu.SemaphoreType.DMA((tensor_count + 2,)),
            pltpu.SemaphoreType.DMA((2,)),
            pltpu.SemaphoreType.DMA((6 + 2 * tensor_count,)),
        ],
        compiler_params=pltpu.CompilerParams(
            collective_id=0, has_side_effects=True, vmem_limit_bytes=VMEM_LIMIT
        ),
        name="gather_forward",
    )(lat, inp, seg, cross_w, self_w, up_w, down_w, vec_own, cot)


def tn(left, right):
    return lax.dot_general(
        left, right, (((0,), (0,)), ((), ())), preferred_element_type=F32
    )


def ln_back(values, gain_row, incoming):
    unit, scale = ln_parts(values)
    scaled = incoming * gain_row
    inner = jnp.mean(scaled * unit, axis=-1, keepdims=True)
    outgoing = scale * (scaled - jnp.mean(scaled, axis=-1, keepdims=True) - unit * inner)
    gain = jnp.sum(incoming * unit, axis=0, keepdims=True)
    return outgoing, gain, jnp.sum(incoming, axis=0, keepdims=True)


def backward_kernel(
    tensor_count,
    lat_h,
    cot_h,
    mid_h,
    late_h,
    gn3_h,
    read_h,
    read2_h,
    query_h,
    query2_h,
    key2_h,
    val2_h,
    prob2_h,
    vecs,
    gb1,
    wc_h,
    ws_h,
    ctx_h,
    key_h,
    val_h,
    prob_h,
    gup_h,
    gdn_h,
    inp,
    glat_o,
    ginp_o,
    gcross_o,
    gself_o,
    gvec_o,
    gup_o,
    gdn_o,
    w_cross,
    g_mlp,
    g_sc,
    rc,
    rb,
    ra,
    rz,
    dwk,
    dwv,
    kt,
    vt,
    ct,
    it,
    pt,
    p1,
    ot,
    dk_t,
    dv_t,
    gbd,
    gbd_t,
    qbd_t,
    row_r,
    dqacc,
    gread,
    dq2,
    dk2,
    dv2,
    gbias,
    gvec,
    vec_in,
    vec_sum,
    c_ssem,
    c_rsem,
    b_ssem,
    b_rsem,
    a_ssem,
    a_rsem,
    z_ssem,
    z_rsem,
    v_ssem,
    v_rsem,
    tile_sem,
    load_sem,
    credit,
):
    dp, z, core, other, first, second, both, peers = neighbours(tensor_count)
    meet(dp, z, other, first, second, peers)
    shard = gcross_o.shape[0]
    quad = 4 * shard
    yy = dp // 4
    xx = lax.rem(dp // 2, 2)
    tiles = ctx_h.shape[0] // TILE
    chunk_count = 4 * tensor_count
    w_self_at = NROWS

    def mult(value, by):
        return pl.multiple_of(value, by)

    def chunk_part(chunk):
        return lax.rem(z + 1 + chunk % tensor_count, tensor_count)

    def own_ref(chunk):
        unit, part = chunk // tensor_count, chunk_part(chunk)
        if unit < 2:
            return g_mlp, (unit * tensor_count + part) * quad
        return g_sc, (((unit - 2) * 2 + core) * tensor_count + part) * quad

    def rows_at(start, count):
        return pl.ds(mult(start, shard), count)

    def remote(source, target, send, recv, device):
        return pltpu.make_async_remote_copy(
            src_ref=source,
            dst_ref=target,
            send_sem=send,
            recv_sem=recv,
            device_id=device,
            device_id_type=MESH,
        )

    def c_slot(chunk):
        return rc.at[chunk % 8]

    def c_whole(chunk):
        return remote(
            c_slot(chunk), c_slot(chunk), c_ssem.at[chunk], c_rsem.at[chunk], (other, z)
        )

    def c_start(chunk):
        unit, part = chunk // tensor_count, chunk_part(chunk)
        if unit < 2:
            source = (gdn_h, gup_h)[unit]
            for q in range(4):
                start = part * D + (2 * q + 1 - core) * shard
                remote(
                    source.at[rows_at(start, shard)],
                    c_slot(chunk).at[pl.ds(q * shard, shard)],
                    c_ssem.at[chunk],
                    c_rsem.at[chunk],
                    (other, z),
                ).start()
        else:
            start = (((unit - 2) * 2 + 1 - core) * tensor_count + part) * quad
            remote(
                g_sc.at[rows_at(start, quad)],
                c_slot(chunk),
                c_ssem.at[chunk],
                c_rsem.at[chunk],
                (other, z),
            ).start()

    def b_copy(chunk, half):
        ref, base = own_ref(chunk)
        q = (1 - core) * ((1 - yy) * 2 + half) + core * (half * 2 + 1 - xx)
        number = chunk * 2 + half
        return remote(
            ref.at[rows_at(base + q * shard, shard)],
            rb.at[chunk % 4, half],
            b_ssem.at[number],
            b_rsem.at[number],
            (second, z),
        )

    def a_copy(chunk):
        ref, base = own_ref(chunk)
        q = (1 - core) * (yy * 2 + 1 - xx) + core * ((1 - yy) * 2 + xx)
        return remote(
            ref.at[rows_at(base + q * shard, shard)],
            ra.at[chunk % 4],
            a_ssem.at[chunk],
            a_rsem.at[chunk],
            (first, z),
        )

    def z_copy(chunk):
        unit, step = divmod(chunk, tensor_count)
        ref, base = own_ref(chunk)
        number = unit * (tensor_count - 1) + step
        return remote(
            ref.at[rows_at(base + (yy * 2 + xx) * shard, shard)],
            rz.at[number],
            z_ssem.at[number],
            z_rsem.at[number],
            (dp, peers[step]),
        )

    piece = 32

    def add_rows(ref, start, source, count):
        def body(index, carry):
            rows = pl.ds(mult(start + index * piece, piece), piece)
            part = source[pl.ds(mult(index * piece, piece), piece), :]
            ref[rows, :] = (ref[rows, :].astype(F32) + part.astype(F32)).astype(BF)
            return carry

        lax.fori_loop(0, count // piece, body, 0)

    def stage1(chunk):
        c_whole(chunk).wait_recv()
        ref, base = own_ref(chunk)
        add_rows(ref, base, c_slot(chunk), quad)
        if chunk in (3, 7):
            pl.semaphore_signal(
                credit, inc=1, device_id=(other, z), device_id_type=MESH
            )
        for half in range(2):
            b_copy(chunk, half).start()

    def stage2(chunk):
        ref, base = own_ref(chunk)
        for half in range(2):
            b_copy(chunk, half).wait_recv()
            q = (1 - core) * (yy * 2 + half) + core * (half * 2 + xx)
            add_rows(ref, base + q * shard, rb.at[chunk % 4, half], shard)
        a_copy(chunk).start()

    def stage3(chunk):
        a_copy(chunk).wait_recv()
        ref, base = own_ref(chunk)
        add_rows(ref, base + (yy * 2 + xx) * shard, ra.at[chunk % 4], shard)
        if chunk % tensor_count < tensor_count - 1:
            z_copy(chunk).start()

    def finish(unit):
        chunk = unit * tensor_count + tensor_count - 1
        ref, base = own_ref(chunk)
        target = (gdn_o, gup_o, gself_o, gcross_o)[unit]
        for step in range(tensor_count - 1):
            z_copy(unit * tensor_count + step).wait_recv()

        def body(index, carry):
            rows = pl.ds(mult(index * piece, piece), piece)
            start = base + (yy * 2 + xx) * shard + index * piece
            total = ref[pl.ds(mult(start, piece), piece), :].astype(F32)
            for step in range(tensor_count - 1):
                total = total + rz[unit * (tensor_count - 1) + step, rows, :].astype(F32)
            target[rows, :] = total
            return carry

        lax.fori_loop(0, shard // piece, body, 0)

    def comm(step):
        for lag, stage in ((0, stage1), (1, stage2), (2, stage3)):
            if 0 <= step - lag < chunk_count:
                stage(step - lag)
        done = step - 3
        if done >= 0 and done % tensor_count == tensor_count - 1:
            finish(done // tensor_count)

    def store_grad(unit, block, values):
        for part in range(8):
            parity, zpart = divmod(part, tensor_count)
            start = (((unit * 2 + parity) * tensor_count + zpart) * 4 + block) * shard
            g_sc[start : start + shard, :] = values[part * shard : (part + 1) * shard].astype(BF)

    def load(source, target, number):
        return pltpu.make_async_copy(source, target, load_sem.at[number])

    w_self = g_sc.at[pl.ds(w_self_at, NROWS)]
    for chunk in range(2 * tensor_count):
        c_start(chunk)
    load(ws_h, w_self, 0).start()
    for unit in range(2):
        source = (gdn_h, gup_h)[unit]
        for part in range(tensor_count):
            for q in range(4):
                pltpu.make_async_copy(
                    source.at[rows_at(part * D + (2 * q + core) * shard, shard)],
                    g_mlp.at[pl.ds(((unit * tensor_count + part) * 4 + q) * shard, shard)],
                    load_sem.at[1 + unit],
                ).start()
    lat_rows = 2 * LAT
    late, gn3, read2 = (dwk.at[pl.ds(third * lat_rows, lat_rows)] for third in range(3))
    read, mid, lat = (dwv.at[pl.ds(third * lat_rows, lat_rows)] for third in range(3))
    prob2 = pt.at[:, :, :, pl.ds(0, LAT)]
    early = [
        (cot_h, glat_o),
        (late_h, late),
        (gn3_h, gn3),
        (read2_h, read2),
        (read_h, read),
        (mid_h, mid),
        (prob2_h, prob2),
        (query2_h, kt.at[0]),
        (key2_h, kt.at[1]),
        (val2_h, vt.at[0]),
        (query_h, vt.at[1]),
    ]
    query2, key2, val2, query = kt.at[0], kt.at[1], vt.at[0], vt.at[1]
    for number, (source, target) in enumerate(early):
        load(source, target, 5 + number).start()
    load(wc_h, w_cross, 3).start()

    def load_p1(extra):
        return load(prob_h.at[:, :, pl.ds((tiles + extra) * TILE, TILE)], p1, 4)

    load_p1(0).start()
    half_mlp = tensor_count * quad
    for unit in range(2):
        whole = g_mlp.at[pl.ds(unit * half_mlp, half_mlp)]
        load(whole, whole, 1 + unit).wait()
    comm(0)

    def vec(row):
        return vecs[row : row + 1, :]

    mask = head_mask(GHEADS * LAT)
    gvec[...] = jnp.zeros(gvec.shape, F32)

    def note(row, values):
        gvec[row : row + 1, :] = values

    def col_sum(values):
        return jnp.sum(values.astype(F32), axis=0, keepdims=True)

    def row_terms(grad_block, read_block):
        wide = jnp.concatenate([grad_block.astype(F32) * read_block] * GHEADS, axis=0)
        return jnp.sum(jnp.where(mask, wide, 0.0), axis=1, keepdims=True)

    for number, (source, target) in enumerate(early):
        load(source, target, 5 + number).wait()
    note(14, col_sum(glat_o[...].astype(BF)))
    gvec[15 : 15 + tensor_count, :] = gb1[0:tensor_count, :]
    back, gain, shift = ln_back(late[...], vec(12), gn3[...])
    note(12, gain)
    note(13, shift)
    gas = glat_o[...] + back
    glat_o[...] = gas
    grad_out = gas.astype(BF)
    note(11, col_sum(grad_out))
    load(ws_h, w_self, 0).wait()

    def self_block(block):
        return g_sc[w_self_at + block * D : w_self_at + (block + 1) * D, :]

    store_grad(0, 3, nn(read2[...].T.astype(BF), grad_out))
    gread[...] = nt(grad_out, self_block(3)).astype(BF)
    comm(1)
    for slot in range(2):
        srows = slice(slot * LAT, (slot + 1) * LAT)
        for group in range(GROUPS):
            gcols = slice(group * GROUP, (group + 1) * GROUP)
            grads = spread_heads(gread[srows, gcols], mask)
            inner = row_terms(gread[srows, gcols], read2[srows, gcols])
            chance = prob2[slot, group]
            dprob = nt(grads, val2[srows, gcols])
            dscore = (chance.astype(F32) * (dprob - inner)).astype(BF)
            dq2[srows, gcols] = (
                pick_heads(nn(dscore, key2[srows, gcols])) * HEAD_DIM ** (-0.5)
            ).astype(BF)
            wide = spread_heads(query2[srows, gcols], mask)
            dk2[srows, gcols] = tn(dscore, wide).astype(BF)
            dv2[srows, gcols] = tn(chance, grads).astype(BF)
    comm(2)
    note(9, col_sum(dq2[...]))
    note(10, col_sum(dv2[...]))
    unit_two, scale_two = ln_parts(mid[...])
    norm_t = (unit_two * vec(7) + vec(8)).T.astype(BF)
    store_grad(0, 0, nn(norm_t, dq2[...]))
    store_grad(0, 1, nn(norm_t, dk2[...]))
    store_grad(0, 2, nn(norm_t, dv2[...]))
    incoming = nt(dq2[...], self_block(0)) + nt(dk2[...], self_block(1))
    incoming = incoming + nt(dv2[...], self_block(2))
    back, gain, shift = ln_back(mid[...], vec(7), incoming)
    note(7, gain)
    note(8, shift)
    total = glat_o[...] + back
    glat_o[...] = total
    grad_out = total.astype(BF)
    note(6, col_sum(grad_out))
    load(wc_h, w_cross, 3).wait()
    store_grad(1, 3, nn(read[...].T.astype(BF), grad_out))
    gread[...] = nt(grad_out, w_cross[3 * D :, :]).astype(BF)
    for slot in range(2):
        srows = slice(slot * LAT, (slot + 1) * LAT)
        for group in range(GROUPS):
            gcols = slice(group * GROUP, (group + 1) * GROUP)
            at = slot * GROUPS + group
            grads = jnp.concatenate([gread[srows, gcols].astype(F32)] * GHEADS, axis=0)
            grads = jnp.where(mask, grads, 0.0)
            gbd[at] = grads.astype(BF)
            gbd_t[at] = grads.T.astype(BF)
            wide = jnp.concatenate([query[srows, gcols].astype(F32)] * GHEADS, axis=0)
            qbd_t[at] = jnp.where(mask, wide, 0.0).T.astype(BF)
            inner = row_terms(gread[srows, gcols], read[srows, gcols])
            row_r[at] = jnp.broadcast_to(inner, (GHEADS * LAT, LANES))
    dqacc[...] = jnp.zeros(dqacc.shape, F32)
    dwk[...] = jnp.zeros(dwk.shape, F32)
    dwv[...] = jnp.zeros(dwv.shape, F32)
    gbias[...] = jnp.zeros(gbias.shape, F32)
    it[0] = jnp.zeros(it.shape[1:], BF)
    comm(3)

    def fetches(index, at_start):
        slot = 0 if at_start else lax.rem(index, 2)
        rows = pl.ds(0, TILE) if at_start else pl.ds(mult(index * TILE, TILE), TILE)
        copies = [
            (key_h.at[rows], kt.at[slot]),
            (val_h.at[rows], vt.at[slot]),
            (ctx_h.at[rows], ct.at[slot]),
            (prob_h.at[:, :, rows], pt.at[slot]),
        ]
        if at_start:
            copies.append((inp.at[pl.ds(0, TILE - PAD)], it.at[0, pl.ds(PAD, TILE - PAD)]))
        else:
            copies.append((inp.at[pl.ds(mult(index * TILE - PAD, PAD), TILE)], it.at[slot]))
        return [
            pltpu.make_async_copy(source, target, tile_sem.at[slot, number])
            for number, (source, target) in enumerate(copies)
        ]

    def put(index, at_start):
        slot = 0 if at_start else lax.rem(index, 2)
        if at_start:
            source, rows = ot.at[0, pl.ds(PAD, TILE - PAD)], pl.ds(0, TILE - PAD)
        else:
            source, rows = ot.at[slot], pl.ds(mult(index * TILE - PAD, PAD), TILE)
        return pltpu.make_async_copy(source, ginp_o.at[rows], tile_sem.at[slot, 5])

    for copy in fetches(0, True):
        copy.start()

    def attend_back(slot, chance_of, buffer, first_time):
        for group in range(GROUPS):
            gcols = slice(group * GROUP, (group + 1) * GROUP)
            at = slot * GROUPS + group
            chance = chance_of(group)
            dprob = nt(gbd[at], vt[buffer, :, gcols])
            inner = row_r[at]
            dscore = chance.astype(F32) * (dprob - jnp.concatenate([inner, inner], axis=1))
            dscore = dscore.astype(BF)
            dk_part = nn(qbd_t[at], dscore)
            dv_part = nn(gbd_t[at], chance)
            if first_time:
                dk_t[gcols, :] = dk_part
                dv_t[gcols, :] = dv_part
            else:
                dk_t[gcols, :] += dk_part
                dv_t[gcols, :] += dv_part
            dqacc[at] += nn(dscore, kt[buffer, :, gcols])

    comm_at = {1: 4, 2: 5, 4: 6, 5: 7, 7: 8, 8: 9, 10: 10, 11: 11}

    def tile_body(index, carry):
        buffer = lax.rem(index, 2)

        @pl.when(index + 1 < tiles)
        def _():
            for copy in fetches(index + 1, False):
                copy.start()

        @pl.when(index == 0)
        def _():
            for copy in fetches(0, True):
                copy.wait()

        @pl.when(index > 0)
        def _():
            for copy in fetches(index, False):
                copy.wait()

        attend_back(0, lambda group: pt[buffer, group], buffer, True)
        for extra in range(SLOT1_TILES):

            @pl.when(index == SLOT1_FIRST + extra)
            def _():
                load_p1(extra).wait()
                attend_back(1, lambda group: p1[group], buffer, False)
                if extra + 1 < SLOT1_TILES:
                    load_p1(extra + 1).start()

        dk = dk_t[...].astype(BF)
        dv = dv_t[...].astype(BF)
        gbias[...] += dv[:, :LANES].astype(F32) + dv[:, LANES:].astype(F32)
        block = ct[buffer]
        dwk[...] += nn(dk, block)
        dwv[...] += nn(dv, block)
        incoming = nn(w_cross[D : 2 * D, :], dk) + nn(w_cross[2 * D : 3 * D, :], dv)
        back, gain, shift = ln_back(it[buffer].astype(F32), vec(2), incoming.T)
        gvec[2:3, :] += gain
        gvec[3:4, :] += shift

        @pl.when(index == 2)
        def _():
            put(0, True).wait()

        @pl.when(index > 2)
        def _():
            put(index - 2, False).wait()

        ot[buffer] = back.astype(BF)

        @pl.when(index == 0)
        def _():
            put(0, True).start()

        @pl.when(index > 0)
        def _():
            put(index, False).start()

        for at, step in comm_at.items():

            @pl.when(index == at)
            def _():
                if step == 7:
                    pl.semaphore_wait(credit, 1)
                    for chunk in range(2 * tensor_count, 3 * tensor_count):
                        c_start(chunk)
                comm(step)

        return carry

    lax.fori_loop(0, tiles, tile_body, 0)
    store_grad(1, 2, dwv[...].T)
    load(lat_h, lat, 16).start()
    store_grad(1, 1, dwk[...].T)
    for slot in range(2):
        srows = slice(slot * LAT, (slot + 1) * LAT)
        for group in range(GROUPS):
            gcols = slice(group * GROUP, (group + 1) * GROUP)
            dq2[srows, gcols] = (
                pick_heads(dqacc[slot * GROUPS + group]) * HEAD_DIM ** (-0.5)
            ).astype(BF)
    load(lat_h, lat, 16).wait()
    unit_one, scale_one = ln_parts(lat[...])
    norm_t = (unit_one * vec(0) + vec(1)).T.astype(BF)
    store_grad(1, 0, nn(norm_t, dq2[...]))
    pl.semaphore_wait(credit, 1)
    for chunk in range(3 * tensor_count, 4 * tensor_count):
        c_start(chunk)
    comm(12)
    note(4, col_sum(dq2[...]))
    note(5, jnp.sum(gbias[...].T, axis=0, keepdims=True))
    incoming = nt(dq2[...], w_cross[0:D, :])
    back, gain, shift = ln_back(lat[...], vec(0), incoming)
    note(0, gain)
    note(1, shift)
    glat_o[...] = glat_o[...] + back

    def vec_copy(hop):
        if hop < 3:
            source, device = vec_sum.at[hop], ((other, second, first)[hop], z)
        else:
            source, device = vec_sum.at[3], (dp, peers[hop - 3])
        return remote(source, vec_in.at[hop], v_ssem.at[hop], v_rsem.at[hop], device)

    total = gvec[...]
    for hop in range(3):
        vec_sum[hop] = total
        vec_copy(hop).start()
        comm(13 + hop)
        vec_copy(hop).wait_recv()
        total = total + vec_in[hop]
    vec_sum[3] = total
    for hop in range(3, 2 + tensor_count):
        vec_copy(hop).start()
    comm(16)
    comm(17)
    comm(18)
    for hop in range(3, 2 + tensor_count):
        vec_copy(hop).wait_recv()
        total = total + vec_in[hop]
    gvec_o[...] = total
    put(tiles - 2, False).wait()
    put(tiles - 1, False).wait()
    for hop in range(2 + tensor_count):
        vec_copy(hop).wait_send()
    for chunk in range(chunk_count):
        c_whole(chunk).wait_send()
        b_copy(chunk, 0).wait_send()
        b_copy(chunk, 1).wait_send()
        a_copy(chunk).wait_send()
        if chunk % tensor_count < tensor_count - 1:
            z_copy(chunk).wait_send()


def backward_call(tensor_count, shard, operands):
    sds = jax.ShapeDtypeStruct
    hbm = pl.BlockSpec(memory_space=pl.ANY)
    vmem = pl.BlockSpec(memory_space=pltpu.VMEM)
    rows = operands[0].shape[0]
    inp = operands[-1]
    stacked = GHEADS * LAT
    chunks = 4 * tensor_count
    zs = 4 * (tensor_count - 1)
    at = 2 * GROUPS
    sem = pltpu.SemaphoreType.DMA
    outs = [
        (sds((rows, D), F32), vmem),
        (sds(inp.shape, BF), hbm),
        (sds((shard, D), F32), vmem),
        (sds((shard, D), F32), vmem),
        (sds((VEC_PAD, D), F32), vmem),
        (sds((shard, D), F32), vmem),
        (sds((shard, D), F32), vmem),
    ]
    return pl.pallas_call(
        partial(backward_kernel, tensor_count),
        out_shape=[shape for shape, spec in outs],
        out_specs=[spec for shape, spec in outs],
        in_specs=[hbm] * 12 + [vmem] * 2 + [hbm] * 9,
        scratch_shapes=[
            pltpu.VMEM((NROWS, D), BF),
            pltpu.VMEM((NROWS, D), BF),
            pltpu.VMEM((2 * NROWS, D), BF),
            pltpu.VMEM((8, 4 * shard, D), BF),
            pltpu.VMEM((4, 2, shard, D), BF),
            pltpu.VMEM((4, shard, D), BF),
            pltpu.VMEM((zs, shard, D), BF),
            pltpu.VMEM((D, D), F32),
            pltpu.VMEM((D, D), F32),
            pltpu.VMEM((2, TILE, D), BF),
            pltpu.VMEM((2, TILE, D), BF),
            pltpu.VMEM((2, TILE, D), BF),
            pltpu.VMEM((2, TILE, D), BF),
            pltpu.VMEM((2, GROUPS, stacked, TILE), BF),
            pltpu.VMEM((GROUPS, stacked, TILE), BF),
            pltpu.VMEM((2, TILE, D), BF),
            pltpu.VMEM((D, TILE), F32),
            pltpu.VMEM((D, TILE), F32),
            pltpu.VMEM((at, stacked, GROUP), BF),
            pltpu.VMEM((at, GROUP, stacked), BF),
            pltpu.VMEM((at, GROUP, stacked), BF),
            pltpu.VMEM((at, stacked, LANES), F32),
            pltpu.VMEM((at, stacked, GROUP), F32),
            pltpu.VMEM((rows, D), BF),
            pltpu.VMEM((rows, D), BF),
            pltpu.VMEM((rows, D), BF),
            pltpu.VMEM((rows, D), BF),
            pltpu.VMEM((D, LANES), F32),
            pltpu.VMEM((VEC_PAD, D), F32),
            pltpu.VMEM((2 + tensor_count, VEC_PAD, D), F32),
            pltpu.VMEM((4, VEC_PAD, D), F32),
            sem((chunks,)),
            sem((chunks,)),
            sem((2 * chunks,)),
            sem((2 * chunks,)),
            sem((chunks,)),
            sem((chunks,)),
            sem((zs,)),
            sem((zs,)),
            sem((2 + tensor_count,)),
            sem((2 + tensor_count,)),
            sem((2, 6)),
            sem((17,)),
            pltpu.SemaphoreType.REGULAR,
        ],
        compiler_params=pltpu.CompilerParams(
            collective_id=1, has_side_effects=True, vmem_limit_bytes=VMEM_LIMIT
        ),
        name="backward_scatter",
    )(*operands)


def local_fused(
    latents,
    inputs,
    segment,
    cross_weights,
    self_weights,
    vectors,
    up_weight,
    down_weight,
    cotangent,
):
    tensor_count = lax.axis_size("tensor")
    shard = cross_weights.shape[0]
    width = vectors.shape[1]
    index = lax.axis_index("dp") * tensor_count + lax.axis_index("tensor")
    own = lax.dynamic_update_slice(
        jnp.zeros((VEC_PAD, D), BF), vectors, (0, index * width)
    )
    seg = jnp.pad(segment, (PAD, 0), constant_values=2)[None, :]
    (
        latents_out,
        wc,
        ws,
        ctx,
        keys,
        vals,
        prob,
        gup,
        gdn,
        vecs,
        query,
        read,
        mid,
        query2,
        key2,
        val2,
        prob2,
        read2,
        late,
        gn3,
        gb1,
    ) = forward_call(
        tensor_count,
        latents,
        inputs,
        seg,
        cross_weights,
        self_weights,
        up_weight,
        down_weight.T,
        own,
        cotangent,
    )
    operands = [latents, cotangent, mid, late, gn3, read, read2, query, query2, key2, val2]
    operands += [prob2, vecs, gb1, wc, ws, ctx, keys, vals, prob, gup, gdn, inputs]
    glat, ginp, gcross, gself, gvec, gup_sum, gdn_sum = backward_call(
        tensor_count, shard, operands
    )
    grad_vectors = lax.dynamic_slice(gvec, (0, index * width), (vectors.shape[0], width))
    return latents_out, glat, ginp, gcross, gself, grad_vectors, gup_sum, gdn_sum.T


def solution(mesh):
    placed = (
        P(("dp", "tensor"), None),
        P(("dp", "tensor"), None),
        P(("dp", "tensor")),
        P(("dp", "tensor"), None),
        P(("dp", "tensor"), None),
        P(None, ("dp", "tensor")),
        P("dp", "tensor"),
        P("tensor", "dp"),
        P(("dp", "tensor"), None),
    )
    shards = mesh.shape["dp"] * mesh.shape["tensor"]
    fused = mesh.shape["dp"] == 8 and mesh.shape["tensor"] == 4 and 4 * D % (32 * shards) == 0
    return jax.shard_map(
        local_fused if fused else local,
        mesh=mesh,
        in_specs=placed,
        out_specs=(
            P(("dp", "tensor"), None),
            P(("dp", "tensor"), None),
            P(("dp", "tensor"), None),
            P(("dp", "tensor"), None),
            P(("dp", "tensor"), None),
            P(None, ("dp", "tensor")),
            P("dp", "tensor"),
            P("tensor", "dp"),
        ),
        check_vma=False,
    )
```

```python
from functools import partial

import jax
import jax.numpy as jnp
from jax import lax
from jax.experimental import pallas as pl
from jax.experimental.pallas import tpu as pltpu
from jax.sharding import PartitionSpec as P

D = 768
HEAD_DIM = 64
FF = 3072
LAT = 128


def cut_along(x, dim, size):
    before, after = (x.shape[:dim], x.shape[dim + 1 :])
    return jnp.moveaxis(x.reshape(*before, size, -1, *after), dim, 0)


def sent_and_summed(x, axis, dim):
    parts = cut_along(x, dim, lax.axis_size(axis))
    arrived = lax.all_to_all(parts, axis, split_axis=0, concat_axis=0, tiled=True)
    return arrived.astype(jnp.float32).sum(axis=0)


def product(left, right):
    return jnp.dot(left, right, preferred_element_type=jnp.float32)


def product_tn(left, right):
    return lax.dot_general(
        left, right, (((0,), (0,)), ((), ())), preferred_element_type=jnp.float32
    )


def product_nt(left, right):
    return lax.dot_general(
        left, right, (((1,), (1,)), ((), ())), preferred_element_type=jnp.float32
    )


def layer_norm(values, gain_row, shift_row):
    average = jnp.mean(values, axis=-1, keepdims=True)
    centred = values - average
    variance = jnp.mean(centred * centred, axis=-1, keepdims=True)
    return centred * lax.rsqrt(variance + 1e-05) * gain_row + shift_row


def norm_backward(values, gain_row, shift_row, incoming):
    unused, pullback = jax.vjp(layer_norm, values, gain_row, shift_row)
    return pullback(incoming)


def split_heads(values):
    return values.reshape(values.shape[0], -1, HEAD_DIM).transpose(1, 0, 2)


def merge_heads(values):
    return values.transpose(1, 0, 2).reshape(values.shape[1], -1)


def head_probs(head_query, head_key, visible, peak_score, denominator):
    scores = product_nt(head_query, head_key) * HEAD_DIM ** (-0.5)
    exponent = jnp.exp(jnp.where(visible, scores - peak_score, -200.0)) * visible.astype(
        jnp.float32
    )
    return exponent / denominator


def attend_forward(queries, keys_in, values_in, visible):
    has_keys = jnp.any(visible, axis=-1, keepdims=True)
    seen_float = visible.astype(jnp.float32)

    def one_head(operands):
        head_query, head_key, head_value = operands
        scores = product_nt(head_query, head_key) * HEAD_DIM ** (-0.5)
        peak_score = jnp.max(jnp.where(visible, scores, -1000000000.0), axis=-1, keepdims=True)
        peak_score = jnp.where(has_keys, peak_score, 0.0)
        exponent = jnp.exp(jnp.where(visible, scores - peak_score, -200.0)) * seen_float
        denominator = jnp.sum(exponent, axis=-1, keepdims=True) + 1.0 - has_keys.astype(jnp.float32)
        attn_probs = (exponent / denominator).astype(jnp.bfloat16)
        return (product(attn_probs, head_value), peak_score, denominator)

    outputs, peaks, denominators = lax.map(
        one_head, (split_heads(queries), split_heads(keys_in), split_heads(values_in))
    )
    return (merge_heads(outputs).astype(jnp.bfloat16), peaks, denominators)


def attend_backward(queries, keys_in, values_in, visible, peaks, denominators, grad_read):
    score_scale = HEAD_DIM ** (-0.5)

    def one_head(operands):
        head_query, head_key, head_value, peak_score, denominator, head_grad = operands
        attn_probs = head_probs(head_query, head_key, visible, peak_score, denominator)
        grad_probs = product_nt(head_grad, head_value)
        grad_value = product_tn(attn_probs.astype(jnp.bfloat16), head_grad)
        inner_sum = jnp.sum(grad_probs * attn_probs, axis=-1, keepdims=True)
        grad_scores = (attn_probs * (grad_probs - inner_sum)).astype(jnp.bfloat16)
        grad_query = product(grad_scores, head_key) * score_scale
        grad_key = product_tn(grad_scores, head_query) * score_scale
        return (grad_query, grad_key, grad_value)

    grad_q, grad_k, grad_v = lax.map(
        one_head,
        (
            split_heads(queries),
            split_heads(keys_in),
            split_heads(values_in),
            peaks,
            denominators,
            split_heads(grad_read),
        ),
    )
    return (
        merge_heads(grad_q).astype(jnp.bfloat16),
        merge_heads(grad_k).astype(jnp.bfloat16),
        merge_heads(grad_v).astype(jnp.bfloat16),
    )


def column_sum(values):
    return jnp.sum(values.astype(jnp.float32), axis=0)


def local(
    latents,
    inputs,
    segment,
    cross_weights,
    self_weights,
    vectors,
    up_weight,
    down_weight,
    cotangent,
):
    cross_full, self_full, vector_half = (
        lax.all_gather(cross_weights, ("dp", "tensor"), axis=0, tiled=True),
        lax.all_gather(self_weights, ("dp", "tensor"), axis=0, tiled=True),
        lax.all_gather(vectors, ("dp", "tensor"), axis=1, tiled=True),
    )
    up_full, down_full = (
        lax.all_gather(up_weight, "dp", axis=0, tiled=True),
        lax.all_gather(down_weight, "dp", axis=1, tiled=True),
    )
    vector_rows = vector_half.astype(jnp.float32)
    quarter = up_full.shape[1]
    part_index = lax.axis_index("tensor")
    bias_up = lax.dynamic_slice_in_dim(
        vector_rows[15:].reshape(-1), part_index * quarter, quarter, 0
    )
    row_count = latents.shape[0]
    slot_row = jnp.arange(row_count, dtype=jnp.int32) // LAT
    cross_seen = slot_row[:, None] == segment[None, :]
    self_seen = slot_row[:, None] == slot_row[None, :]
    input_float = inputs.astype(jnp.float32)
    normed = layer_norm(latents, vector_rows[0], vector_rows[1]).astype(jnp.bfloat16)
    context = layer_norm(input_float, vector_rows[2], vector_rows[3]).astype(jnp.bfloat16)
    queries = (product(normed, cross_full[:D]) + vector_rows[4]).astype(jnp.bfloat16)
    keys_in = product(context, cross_full[D : 2 * D]).astype(jnp.bfloat16)
    values_in = (product(context, cross_full[2 * D : 3 * D]) + vector_rows[5]).astype(jnp.bfloat16)
    cross_read, cross_peaks, cross_denoms = attend_forward(queries, keys_in, values_in, cross_seen)
    after_cross = latents + (product(cross_read, cross_full[3 * D :]) + vector_rows[6])
    normed_two = layer_norm(after_cross, vector_rows[7], vector_rows[8]).astype(jnp.bfloat16)
    queries_two = (product(normed_two, self_full[:D]) + vector_rows[9]).astype(jnp.bfloat16)
    keys_two = product(normed_two, self_full[D : 2 * D]).astype(jnp.bfloat16)
    values_two = (product(normed_two, self_full[2 * D : 3 * D]) + vector_rows[10]).astype(
        jnp.bfloat16
    )
    self_read, self_peaks, self_denoms = attend_forward(
        queries_two, keys_two, values_two, self_seen
    )
    after_self = after_cross + (product(self_read, self_full[3 * D :]) + vector_rows[11])
    normed_three = layer_norm(after_self, vector_rows[12], vector_rows[13]).astype(jnp.bfloat16)
    gathered = lax.all_gather(normed_three, "tensor", axis=0, tiled=True)
    pre_act = product(gathered, up_full) + bias_up
    hidden = jax.nn.gelu(pre_act, approximate=False).astype(jnp.bfloat16)
    reduced = lax.psum_scatter(
        product(hidden, down_full).astype(jnp.bfloat16), "tensor", scatter_dimension=0, tiled=True
    ).astype(jnp.float32)
    latents_out = after_self + (reduced + vector_rows[14])
    cross_full, self_full, vector_half = (
        lax.all_gather(cross_weights, ("dp", "tensor"), axis=0, tiled=True),
        lax.all_gather(self_weights, ("dp", "tensor"), axis=0, tiled=True),
        lax.all_gather(vectors, ("dp", "tensor"), axis=1, tiled=True),
    )
    up_full, down_full = (
        lax.all_gather(up_weight, "dp", axis=0, tiled=True),
        lax.all_gather(down_weight, "dp", axis=1, tiled=True),
    )
    vector_rows = vector_half.astype(jnp.float32)
    grad_y = cotangent.astype(jnp.bfloat16)
    grad_b2 = column_sum(grad_y)
    grad_rows = lax.all_gather(grad_y, "tensor", axis=0, tiled=True)
    grad_down = product_tn(hidden, grad_rows)
    grad_hidden = product_nt(grad_rows, down_full)
    unused, gelu_pull = jax.vjp(partial(jax.nn.gelu, approximate=False), pre_act)
    grad_pre = gelu_pull(grad_hidden)[0].astype(jnp.bfloat16)
    grad_b1 = column_sum(grad_pre)
    grad_up = product_tn(gathered, grad_pre)
    mlp_sums = (
        sent_and_summed(grad_up.astype(jnp.bfloat16), "dp", 0),
        sent_and_summed(grad_down.astype(jnp.bfloat16), "dp", 1),
    )
    grad_normed_three = lax.psum_scatter(
        product_nt(grad_pre, up_full).astype(jnp.bfloat16),
        "tensor",
        scatter_dimension=0,
        tiled=True,
    ).astype(jnp.float32)
    back_self, grad_gain_three, grad_shift_three = norm_backward(
        after_self, vector_rows[12], vector_rows[13], grad_normed_three
    )
    grad_after_self = cotangent + back_self
    grad_out_two = grad_after_self.astype(jnp.bfloat16)
    grad_bias_out_two = column_sum(grad_out_two)
    grad_wo_two = product_tn(self_read, grad_out_two)
    grad_read_two = product_nt(grad_out_two, self_full[3 * D :]).astype(jnp.bfloat16)
    grad_q_two, grad_k_two, grad_v_two = attend_backward(
        queries_two, keys_two, values_two, self_seen, self_peaks, self_denoms, grad_read_two
    )
    grad_self = jnp.concatenate(
        [
            product_tn(normed_two, grad_q_two),
            product_tn(normed_two, grad_k_two),
            product_tn(normed_two, grad_v_two),
            grad_wo_two,
        ],
        axis=0,
    )
    grad_normed_two = (
        product_nt(grad_q_two, self_full[:D])
        + product_nt(grad_k_two, self_full[D : 2 * D])
        + product_nt(grad_v_two, self_full[2 * D : 3 * D])
    )
    back_cross, grad_gain_two, grad_shift_two = norm_backward(
        after_cross, vector_rows[7], vector_rows[8], grad_normed_two
    )
    grad_after_cross = grad_after_self + back_cross
    grad_out_one = grad_after_cross.astype(jnp.bfloat16)
    grad_bias_out_one = column_sum(grad_out_one)
    grad_wo_one = product_tn(cross_read, grad_out_one)
    grad_read_one = product_nt(grad_out_one, cross_full[3 * D :]).astype(jnp.bfloat16)
    grad_q_one, grad_k_one, grad_v_one = attend_backward(
        queries, keys_in, values_in, cross_seen, cross_peaks, cross_denoms, grad_read_one
    )
    grad_cross = jnp.concatenate(
        [
            product_tn(normed, grad_q_one),
            product_tn(context, grad_k_one),
            product_tn(context, grad_v_one),
            grad_wo_one,
        ],
        axis=0,
    )
    grad_normed = product_nt(grad_q_one, cross_full[:D])
    back_latent, grad_gain_one, grad_shift_one = norm_backward(
        latents, vector_rows[0], vector_rows[1], grad_normed
    )
    grad_latents = grad_after_cross + back_latent
    grad_context = product_nt(grad_k_one, cross_full[D : 2 * D]) + product_nt(
        grad_v_one, cross_full[2 * D : 3 * D]
    )
    back_input, grad_gain_input, grad_shift_input = norm_backward(
        input_float, vector_rows[2], vector_rows[3], grad_context
    )
    grad_inputs = back_input.astype(jnp.bfloat16)
    full_bias = lax.dynamic_update_slice_in_dim(
        jnp.zeros((FF,), jnp.float32), grad_b1, part_index * quarter, 0
    )
    grad_vectors = jnp.concatenate(
        [
            jnp.stack(
                [
                    grad_gain_one,
                    grad_shift_one,
                    grad_gain_input,
                    grad_shift_input,
                    column_sum(grad_q_one),
                    column_sum(grad_v_one),
                    grad_bias_out_one,
                    grad_gain_two,
                    grad_shift_two,
                    column_sum(grad_q_two),
                    column_sum(grad_v_two),
                    grad_bias_out_two,
                    grad_gain_three,
                    grad_shift_three,
                    grad_b2,
                ],
                axis=0,
            ),
            full_bias.reshape(-1, D),
        ],
        axis=0,
    )
    cross_sums, self_sums, vector_sums = (
        lax.psum_scatter(grad_cross, ("dp", "tensor"), scatter_dimension=0, tiled=True),
        lax.psum_scatter(grad_self, ("dp", "tensor"), scatter_dimension=0, tiled=True),
        lax.psum_scatter(grad_vectors, ("dp", "tensor"), scatter_dimension=1, tiled=True),
    )
    return (
        latents_out,
        grad_latents,
        grad_inputs,
        cross_sums,
        self_sums,
        vector_sums,
        mlp_sums[0],
        mlp_sums[1],
    )


BF = jnp.bfloat16
F32 = jnp.float32
MESH = pl.DeviceIdType.MESH
TILE = 256
PAD = 128
GROUP = 256
GROUPS = D // GROUP
GHEADS = GROUP // HEAD_DIM
LANES = 128
HIDE = -1e30
VEC_PAD = 32
NROWS = 4 * D
SLOT1_FIRST = 2
SLOT1_TILES = 2
VMEM_LIMIT = 63 * 1024 * 1024


def nn(left, right):
    return jnp.dot(left, right, preferred_element_type=F32)


def nt(left, right):
    return lax.dot_general(
        left, right, (((1,), (1,)), ((), ())), preferred_element_type=F32
    )


def ln_parts(values):
    average = jnp.mean(values, axis=-1, keepdims=True)
    centred = values - average
    variance = jnp.mean(centred * centred, axis=-1, keepdims=True)
    scale = lax.rsqrt(variance + 1e-05)
    return centred * scale, scale


def ln_rows(values, gain_row, shift_row):
    return ln_parts(values)[0] * gain_row + shift_row


def neighbours(tensor_count):
    dp = lax.axis_index("dp")
    z = lax.axis_index("tensor")
    core = lax.rem(dp, 2)
    flip_x = dp + 2 * (1 - 2 * lax.rem(dp // 2, 2))
    flip_y = dp + 4 * (1 - 2 * (dp // 4))
    other = dp + 1 - 2 * core
    first = (1 - core) * flip_x + core * flip_y
    second = (1 - core) * flip_y + core * flip_x
    both = flip_x + flip_y - dp
    peers = [lax.rem(z + step, tensor_count) for step in range(1, tensor_count)]
    return dp, z, core, other, first, second, both, peers


def meet(dp, z, other, first, second, peers):
    barrier = pltpu.get_barrier_semaphore()
    devices = [(other, z), (first, z), (second, z)] + [(dp, peer) for peer in peers]
    for device in devices:
        pl.semaphore_signal(barrier, inc=1, device_id=device, device_id_type=MESH)
    pl.semaphore_wait(barrier, len(devices))


def head_mask(rows):
    row_head = lax.broadcasted_iota(jnp.int32, (rows, GROUP), 0) // LAT
    col_head = lax.broadcasted_iota(jnp.int32, (rows, GROUP), 1) // HEAD_DIM
    return row_head == col_head


def spread_heads(block, mask):
    wide = jnp.concatenate([block.astype(F32)] * GHEADS, axis=0)
    return jnp.where(mask, wide, 0.0).astype(BF)


def pick_heads(stacked):
    col_head = lax.broadcasted_iota(jnp.int32, (LAT, GROUP), 1) // HEAD_DIM
    total = jnp.zeros((LAT, GROUP), F32)
    for head in range(GHEADS):
        part = stacked[head * LAT : (head + 1) * LAT]
        total = total + jnp.where(col_head == head, part, 0.0)
    return total


def forward_kernel(
    tensor_count,
    lat,
    inp,
    seg_in,
    cross_shard,
    self_shard,
    up_shard,
    down_shard,
    vectors,
    cot,
    out_o,
    wc_o,
    ws_o,
    ctx_o,
    key_o,
    val_o,
    prob_o,
    gup_o,
    gdn_o,
    vec_o,
    query_h,
    read_h,
    mid_h,
    query2_h,
    key2_h,
    val2_h,
    prob2_h,
    read2_h,
    late_h,
    gn3_o,
    gb1_o,
    inv_o,
    query_o,
    read,
    mid_o,
    query2_o,
    key2_o,
    val2_o,
    prob2_o,
    read2_o,
    late_o,
    seg,
    vec_own,
    w_cross,
    w_self,
    w_up,
    w_down,
    ctx,
    keys,
    vals,
    scores,
    probs,
    inbuf,
    qbd,
    peak,
    denom,
    oacc,
    norm_t,
    gy_t,
    vec_in,
    vec_sum,
    send_sem,
    recv_sem,
    vec_ssem,
    vec_rsem,
    in_sem,
    out_sem,
):
    dp, z, core, other, first, second, both, peers = neighbours(tensor_count)
    meet(dp, z, other, first, second, peers)
    weights = (w_cross, w_self, w_up, w_down)
    shards = (cross_shard, self_shard, up_shard, down_shard)
    shard_rows = cross_shard.shape[0]
    tiles = ctx.shape[0] // TILE
    chunk_count = 4 * tensor_count
    kinds = 7

    def place(unit, owner, part):
        if unit < 2:
            start = (owner * tensor_count + part) * shard_rows
        else:
            start = part * D + owner * shard_rows
        return pl.ds(pl.multiple_of(start, shard_rows), shard_rows)

    def remote(source, target, number, device):
        return pltpu.make_async_remote_copy(
            src_ref=source,
            dst_ref=target,
            send_sem=send_sem.at[number],
            recv_sem=recv_sem.at[number],
            device_id=device,
            device_id_type=MESH,
        )

    def z_copy(unit, step):
        rows = place(unit, dp, z)
        number = chunk_count * kinds + unit * (tensor_count - 1) + step - 1
        return remote(shards[unit], weights[unit].at[rows], number, (dp, peers[step - 1]))

    def plane_copy(chunk, kind):
        unit, step = divmod(chunk, tensor_count)
        part = lax.rem(z - step + tensor_count, tensor_count)
        owner = (dp, dp, first, dp, first, second, both)[kind]
        target = (first, second, second, other, other, other, other)[kind]
        rows = place(unit, owner, part)
        return remote(
            weights[unit].at[rows], weights[unit].at[rows], chunk * kinds + kind, (target, z)
        )

    def z_start(unit):
        for step in range(1, tensor_count):
            z_copy(unit, step).start()

    def stage0(chunk):
        unit, step = divmod(chunk, tensor_count)
        if step:
            z_copy(unit, step).wait_recv()
        for kind in (0, 1, 3):
            plane_copy(chunk, kind).start()

    def stage1(chunk):
        plane_copy(chunk, 0).wait_recv()
        for kind in (2, 4):
            plane_copy(chunk, kind).start()

    def stage2(chunk):
        plane_copy(chunk, 1).wait_recv()
        plane_copy(chunk, 5).start()
        plane_copy(chunk, 2).wait_recv()
        plane_copy(chunk, 6).start()

    def stage3(chunk):
        for kind in (3, 4, 5, 6):
            plane_copy(chunk, kind).wait_recv()

    ahead = 3
    last = chunk_count - 1

    def begin(chunk):
        if chunk < chunk_count:
            if chunk % tensor_count:
                stage0(chunk)
            if chunk % tensor_count == tensor_count - 2 and chunk // tensor_count < 3:
                z_start(chunk // tensor_count + 1)

    def comm(step):
        begin(step + ahead)
        if step <= last - ahead:
            stage1(step)
        elif step == last - ahead + 1:
            for chunk in range(step, last + 1):
                stage1(chunk)
        for lag, stage in ((1, stage2), (2, stage3)):
            if 0 <= step - lag < chunk_count:
                stage(step - lag)

    def vec_copy(hop):
        if hop < tensor_count - 1:
            source, device = vec_own, (dp, peers[hop])
        else:
            level = hop - (tensor_count - 1)
            source, device = vec_sum.at[level], ((first, second, other)[level], z)
        return pltpu.make_async_remote_copy(
            src_ref=source,
            dst_ref=vec_in.at[hop],
            send_sem=vec_ssem.at[hop],
            recv_sem=vec_rsem.at[hop],
            device_id=device,
            device_id_type=MESH,
        )

    def read_in(index):
        rows = inbuf.shape[1]
        start = pl.multiple_of(index * rows, rows)
        slot = lax.rem(index, 2)
        return pltpu.make_async_copy(
            inp.at[pl.ds(start, rows)], inbuf.at[slot], in_sem.at[slot]
        )

    def keep(source, target, number):
        return pltpu.make_async_copy(source, target, out_sem.at[number])

    width = vectors.shape[1]
    first_col = (dp * tensor_count + z) * width
    row = lax.broadcasted_iota(jnp.int32, (width, D), 0)
    col = lax.broadcasted_iota(jnp.int32, (width, D), 1)
    spot = jnp.where(col == row + first_col, 1.0, 0.0).astype(BF)
    vec_own[...] = jnp.zeros(vec_own.shape, BF)
    vec_own[0 : vectors.shape[0], :] = nn(vectors[...], spot).astype(BF)
    for hop in range(tensor_count - 1):
        vec_copy(hop).start()
    w_cross[place(0, dp, z), :] = cross_shard[...]
    z_start(0)
    read_in(0).start()
    keep(cot, gn3_o, 16).start()
    for unit in range(1, 4):
        weights[unit][place(unit, dp, z), :] = shards[unit][...]
    seg[...] = jnp.full(seg.shape, 2, jnp.int32)
    for row in range(seg_in.shape[0]):
        seg[:, PAD + row * LANES : PAD + (row + 1) * LANES] = seg_in[row : row + 1, :]
    for unit in range(4):
        stage0(unit * tensor_count)
    for hop in range(tensor_count - 1):
        vec_copy(hop).wait_recv()
    total = vec_own[...].astype(F32)
    for hop in range(tensor_count - 1):
        total = total + vec_in[hop].astype(F32)
    for level in range(3):
        vec_sum[level] = total.astype(BF)
        hop = tensor_count - 1 + level
        vec_copy(hop).start()
        if level:
            begin(level)
        vec_copy(hop).wait_recv()
        total = total + vec_in[hop].astype(F32)
    vec_o[...] = total

    def vec(row):
        return vec_o[row : row + 1, :]

    ctx[0:PAD, :] = jnp.zeros((PAD, D), BF)
    in_rows = inbuf.shape[1]
    reads = inp.shape[0] // in_rows

    def norm_inputs(index, carry):
        @pl.when(index + 1 < reads)
        def _():
            read_in(index + 1).start()

        read_in(index).wait()
        slot = lax.rem(index, 2)

        def rows_of(part, carry2):
            start = pl.multiple_of(part * 64, 64)
            values = inbuf[slot, pl.ds(start, 64), :].astype(F32)
            ctx[pl.ds(pl.multiple_of(PAD + index * in_rows + start, 64), 64), :] = ln_rows(
                values, vec(2), vec(3)
            ).astype(BF)
            return carry2

        lax.fori_loop(0, in_rows // 64, rows_of, 0)

        @pl.when(index == 2)
        def _():
            comm(0)

        @pl.when(index == 7)
        def _():
            comm(1)

        return carry

    lax.fori_loop(0, reads, norm_inputs, 0)
    normed = ln_rows(lat[...], vec(0), vec(1)).astype(BF)
    keep(cot, gn3_o, 16).wait()
    gy = gn3_o[...].astype(BF)
    gy_t[...] = gn3_o[...].T.astype(BF)
    for step in (2, 3, 4, 5):
        comm(step)
    keep(w_cross, wc_o, 0).start()
    mask = head_mask(GHEADS * LAT)

    query = (nn(normed, w_cross[0:D, :]) + vec(4)).astype(BF)
    scaled = (query.astype(F32) * HEAD_DIM ** (-0.5)).astype(BF)
    query_o[...] = scaled
    for slot in range(2):
        for group in range(GROUPS):
            block = scaled[slot * LAT : (slot + 1) * LAT, group * GROUP : (group + 1) * GROUP]
            qbd[slot * GROUPS + group] = spread_heads(block, mask)

    def project(index, carry):
        rows = pl.ds(pl.multiple_of(index * TILE, TILE), TILE)
        block = ctx[rows, :]
        keys[rows, :] = nn(block, w_cross[D : 2 * D, :]).astype(BF)
        vals[rows, :] = (nn(block, w_cross[2 * D : 3 * D, :]) + vec(5)).astype(BF)

        @pl.when(index == 4)
        def _():
            comm(6)

        @pl.when(index == 9)
        def _():
            comm(7)

        return carry

    lax.fori_loop(0, tiles, project, 0)
    keep(ctx, ctx_o, 1).start()
    keep(keys, key_o, 2).start()
    keep(vals, val_o, 3).start()

    wide = 3 * TILE
    whole = tiles // 3
    rest = [
        (0, slice(whole * wide, tiles * TILE), slice(whole * wide, tiles * TILE)),
        (
            1,
            slice(SLOT1_FIRST * TILE, (SLOT1_FIRST + SLOT1_TILES) * TILE),
            slice(tiles * TILE, (tiles + SLOT1_TILES) * TILE),
        ),
    ]

    def wide_cols(index):
        return pl.ds(pl.multiple_of(index * wide, wide), wide)

    def fold(values, op):
        parts = [values[:, at : at + LANES] for at in range(0, values.shape[1], LANES)]
        while len(parts) > 1:
            parts = [
                op(parts[at], parts[at + 1]) if at + 1 < len(parts) else parts[at]
                for at in range(0, len(parts), 2)
            ]
        return parts[0]

    seen = []
    for slot in range(2):
        hit = jnp.where(seg[...] == slot, 1.0, 0.0)
        seen.append(jnp.max(hit, axis=1, keepdims=True))

    for group in range(GROUPS):
        gcols = slice(group * GROUP, (group + 1) * GROUP)
        peak[...] = jnp.full(peak.shape, HIDE, F32)
        denom[...] = jnp.zeros(denom.shape, F32)
        oacc[...] = jnp.zeros(oacc.shape, F32)

        def score_part(slot, rows, cols):
            values = nt(qbd[slot * GROUPS + group], keys[rows, gcols])
            values = jnp.where(seg[:, rows] == slot, values, HIDE)
            scores[:, cols] = values
            peak[slot] = jnp.maximum(peak[slot], fold(values, jnp.maximum))

        def score(index, carry):
            score_part(0, wide_cols(index), wide_cols(index))

            @pl.when(index == 2)
            def _():
                comm(8 + group)

            return carry

        lax.fori_loop(0, whole, score, 0)
        for slot, rows, cols in rest:
            score_part(slot, rows, cols)
        for slot in range(2):
            top = jnp.max(peak[slot], axis=1, keepdims=True)
            top = jnp.where(seen[slot] > 0.0, top, 0.0)
            peak[slot] = jnp.broadcast_to(top, (GHEADS * LAT, LANES))
        if group:
            keep(probs, prob_o.at[group - 1], 4).wait()

        def spread_part(slot, rows, cols):
            for head in range(GHEADS):
                part = slice(head * LAT, (head + 1) * LAT)
                values = scores[part, cols]
                count = values.shape[1] // LANES
                top = jnp.concatenate([peak[slot, part, :]] * count, axis=1)
                values = jnp.exp(values - top)
                probs[part, cols] = values.astype(BF)
                denom[slot, part, :] += fold(values, jnp.add)
            oacc[slot] += nn(probs[:, cols], vals[rows, gcols])

        def spread(index, carry):
            spread_part(0, wide_cols(index), wide_cols(index))
            return carry

        lax.fori_loop(0, whole, spread, 0)
        for slot, rows, cols in rest:
            spread_part(slot, rows, cols)
        keep(probs, prob_o.at[group], 4).start()
        for slot in range(2):
            total = jnp.sum(denom[slot], axis=1, keepdims=True) + 1.0 - seen[slot]
            scale = 1.0 / total
            across = jnp.broadcast_to(scale, (GHEADS * LAT, LANES)).T
            at = slot * GROUPS + group
            inv_o[at : at + 1, :] = across[0:1, :]
            read[slot * LAT : (slot + 1) * LAT, gcols] = pick_heads(oacc[slot] * scale)

    mid = lat[...] + (nn(read[...].astype(BF), w_cross[3 * D :, :]) + vec(6))
    mid_o[...] = mid
    normed_two = ln_rows(mid, vec(7), vec(8)).astype(BF)
    keep(w_self, ws_o, 5).start()
    query_two = (nn(normed_two, w_self[0:D, :]) + vec(9)).astype(BF)
    query2_o[...] = (query_two.astype(F32) * HEAD_DIM ** (-0.5)).astype(BF)
    key2_o[...] = nn(normed_two, w_self[D : 2 * D, :]).astype(BF)
    val2_o[...] = (nn(normed_two, w_self[2 * D : 3 * D, :]) + vec(10)).astype(BF)
    for slot in range(2):
        srows = slice(slot * LAT, (slot + 1) * LAT)
        for group in range(GROUPS):
            gcols = slice(group * GROUP, (group + 1) * GROUP)
            wide = spread_heads(query2_o[srows, gcols], mask)
            values = nt(wide, key2_o[srows, gcols])
            values = jnp.exp(values - jnp.max(values, axis=1, keepdims=True))
            values = values / jnp.sum(values, axis=1, keepdims=True)
            values = values.astype(BF)
            prob2_o[slot, group] = values
            read2_o[srows, gcols] = pick_heads(nn(values, val2_o[srows, gcols]))
    late = mid_o[...] + (nn(read2_o[...].astype(BF), w_self[3 * D :, :]) + vec(11))
    late_o[...] = late
    normed_three = ln_rows(late, vec(12), vec(13))
    norm_t[...] = normed_three.T.astype(BF)
    normed_three = normed_three.astype(BF)
    keep(probs, prob_o.at[GROUPS - 1], 4).wait()
    keep(keys, key_o, 2).wait()
    keep(vals, val_o, 3).wait()

    small = [
        (query_o, query_h),
        (read, read_h),
        (mid_o, mid_h),
        (query2_o, query2_h),
        (key2_o, key2_h),
        (val2_o, val2_h),
        (prob2_o, prob2_h),
        (read2_o, read2_h),
        (late_o, late_h),
    ]
    for number, (source, target) in enumerate(small):
        keep(source, target, 17 + number).start()

    rows_all = slice(0, 2 * LAT)

    def quarter(step):
        part = lax.rem(z - step + tensor_count, tensor_count)
        return part, pl.ds(pl.multiple_of(part * D, D), D)

    def up_part(step):
        part, rows = quarter(step)
        cols = slice(step * D, (step + 1) * D)
        pre = nn(normed_three, w_up[rows, :]) + vec_o[pl.ds(15 + part, 1), :]
        half = 0.5 * (1.0 + lax.erf(pre * 0.5**0.5))
        slope = half + pre * jnp.exp(-0.5 * pre * pre) * 0.3989422804014327
        hidden = (pre * half).astype(BF)
        probs[rows_all, cols] = hidden
        scores[rows_all, cols] = slope
        vals[rows, :] = nn(gy_t[...], hidden).astype(BF)
        keep(vals.at[rows], gdn_o.at[rows], 6 + step).start()

    def down_part(step):
        part, rows = quarter(step)
        cols = slice(step * D, (step + 1) * D)
        down = w_down[rows, :]
        y_part = nt(probs[rows_all, cols], down)
        grad_pre = (scores[rows_all, cols] * nn(gy, down)).astype(BF)
        keys[rows, :] = nn(norm_t[...], grad_pre).astype(BF)
        keep(keys.at[rows], gup_o.at[rows], 6 + tensor_count + step).start()
        x_part = nt(grad_pre, w_up[rows, :])
        if step == 0:
            out_o[...] = late_o[...] + vec(14) + y_part
            gn3_o[...] = x_part
        else:
            out_o[...] += y_part
            gn3_o[...] += x_part
        gb1_o[pl.ds(part, 1), :] = jnp.sum(grad_pre.astype(F32), axis=0, keepdims=True)

    gb1_o[...] = jnp.zeros(gb1_o.shape, F32)
    for step in range(tensor_count):
        if step:
            comm(10 + step)
        up_part(step)
    for step in range(tensor_count):
        comm(14 + step)
        down_part(step)
    for number, (source, target) in enumerate(small):
        keep(source, target, 17 + number).wait()
    keep(w_cross, wc_o, 0).wait()
    keep(ctx, ctx_o, 1).wait()
    keep(w_self, ws_o, 5).wait()
    for step in range(tensor_count):
        part, rows = quarter(step)
        keep(vals.at[rows], gdn_o.at[rows], 6 + step).wait()
        keep(keys.at[rows], gup_o.at[rows], 6 + tensor_count + step).wait()
    for hop in range(tensor_count + 2):
        vec_copy(hop).wait_send()
    for unit in range(4):
        for step in range(1, tensor_count):
            z_copy(unit, step).wait_send()
    for chunk in range(chunk_count):
        for kind in range(kinds):
            plane_copy(chunk, kind).wait_send()


def forward_call(tensor_count, lat, inp, seg, cross_w, self_w, up_w, down_w, vectors, cot):
    rows = lat.shape[0]
    tokens = inp.shape[0] + PAD
    virtual = (tokens // TILE + SLOT1_TILES) * TILE
    sds = jax.ShapeDtypeStruct
    hbm = pl.BlockSpec(memory_space=pl.ANY)
    vmem = pl.BlockSpec(memory_space=pltpu.VMEM)
    stacked = GHEADS * LAT
    copies = 4 * tensor_count * 7 + 4 * (tensor_count - 1)
    outs = [
        (sds((rows, D), F32), vmem),
        (sds((NROWS, D), BF), hbm),
        (sds((NROWS, D), BF), hbm),
        (sds((tokens, D), BF), hbm),
        (sds((tokens, D), BF), hbm),
        (sds((tokens, D), BF), hbm),
        (sds((GROUPS, stacked, virtual), BF), hbm),
        (sds((NROWS, D), BF), hbm),
        (sds((NROWS, D), BF), hbm),
        (sds((VEC_PAD, D), F32), vmem),
        (sds((rows, D), BF), hbm),
        (sds((rows, D), F32), hbm),
        (sds((rows, D), F32), hbm),
        (sds((rows, D), BF), hbm),
        (sds((rows, D), BF), hbm),
        (sds((rows, D), BF), hbm),
        (sds((2, GROUPS, stacked, LAT), BF), hbm),
        (sds((rows, D), F32), hbm),
        (sds((rows, D), F32), hbm),
        (sds((rows, D), F32), vmem),
        (sds((8, D), F32), vmem),
        (sds((8, stacked), F32), vmem),
    ]
    return pl.pallas_call(
        partial(forward_kernel, tensor_count),
        out_shape=[shape for shape, spec in outs],
        out_specs=[spec for shape, spec in outs],
        in_specs=[vmem, hbm] + [vmem] * 6 + [hbm],
        scratch_shapes=[
            pltpu.VMEM((rows, D), BF),
            pltpu.VMEM((rows, D), F32),
            pltpu.VMEM((rows, D), F32),
            pltpu.VMEM((rows, D), BF),
            pltpu.VMEM((rows, D), BF),
            pltpu.VMEM((rows, D), BF),
            pltpu.VMEM((2, GROUPS, stacked, LAT), BF),
            pltpu.VMEM((rows, D), F32),
            pltpu.VMEM((rows, D), F32),
            pltpu.VMEM((1, tokens), jnp.int32),
            pltpu.VMEM((VEC_PAD, D), BF),
            pltpu.VMEM((NROWS, D), BF),
            pltpu.VMEM((NROWS, D), BF),
            pltpu.VMEM((NROWS, D), BF),
            pltpu.VMEM((NROWS, D), BF),
            pltpu.VMEM((tokens, D), BF),
            pltpu.VMEM((tokens, D), BF),
            pltpu.VMEM((tokens, D), BF),
            pltpu.VMEM((stacked, virtual), F32),
            pltpu.VMEM((stacked, virtual), BF),
            pltpu.VMEM((2, 320, D), BF),
            pltpu.VMEM((2 * GROUPS, stacked, GROUP), BF),
            pltpu.VMEM((2, stacked, LANES), F32),
            pltpu.VMEM((2, stacked, LANES), F32),
            pltpu.VMEM((2, stacked, GROUP), F32),
            pltpu.VMEM((D, rows), BF),
            pltpu.VMEM((D, rows), BF),
            pltpu.VMEM((tensor_count + 2, VEC_PAD, D), BF),
            pltpu.VMEM((3, VEC_PAD, D), BF),
            pltpu.SemaphoreType.DMA((copies,)),
            pltpu.SemaphoreType.DMA((copies,)),
            pltpu.SemaphoreType.DMA((tensor_count + 2,)),
            pltpu.SemaphoreType.DMA((tensor_count + 2,)),
            pltpu.SemaphoreType.DMA((2,)),
            pltpu.SemaphoreType.DMA((26,)),
        ],
        compiler_params=pltpu.CompilerParams(
            collective_id=0, has_side_effects=True, vmem_limit_bytes=VMEM_LIMIT
        ),
        name="gather_forward",
    )(lat, inp, seg, cross_w, self_w, up_w, down_w, vectors, cot)


def tn(left, right):
    return lax.dot_general(
        left, right, (((0,), (0,)), ((), ())), preferred_element_type=F32
    )


def ln_back(values, gain_row, incoming):
    unit, scale = ln_parts(values)
    scaled = incoming * gain_row
    inner = jnp.mean(scaled * unit, axis=-1, keepdims=True)
    outgoing = scale * (scaled - jnp.mean(scaled, axis=-1, keepdims=True) - unit * inner)
    gain = jnp.sum(incoming * unit, axis=0, keepdims=True)
    return outgoing, gain, jnp.sum(incoming, axis=0, keepdims=True)


def backward_kernel(
    tensor_count,
    lat_h,
    cot_h,
    mid_h,
    late_h,
    gn3_h,
    read_h,
    read2_h,
    query_h,
    query2_h,
    key2_h,
    val2_h,
    prob2_h,
    vecs,
    gb1,
    inv,
    wc_h,
    ws_h,
    ctx_h,
    key_h,
    val_h,
    prob_h,
    gup_h,
    gdn_h,
    inp,
    glat_o,
    ginp_o,
    gcross_o,
    gself_o,
    gvec_o,
    gup_o,
    gdn_o,
    dkv_h,
    w_cross,
    g_mlp,
    g_sc,
    rc,
    rb,
    ra,
    rz,
    dwk,
    dwv,
    kt,
    vt,
    ct,
    it,
    pt,
    p1,
    ot,
    dk_t,
    dv_t,
    dkv,
    gbd,
    gbd_t,
    qbd_t,
    row_r,
    dqacc,
    gread,
    dq2,
    dk2,
    dv2,
    gbias,
    gvec,
    vec_in,
    vec_sum,
    c_ssem,
    c_rsem,
    b_ssem,
    b_rsem,
    a_ssem,
    a_rsem,
    z_ssem,
    z_rsem,
    v_ssem,
    v_rsem,
    tile_sem,
    load_sem,
    credit,
):
    dp, z, core, other, first, second, both, peers = neighbours(tensor_count)
    meet(dp, z, other, first, second, peers)
    shard = gcross_o.shape[0]
    quad = 4 * shard
    yy = dp // 4
    xx = lax.rem(dp // 2, 2)
    tiles = ctx_h.shape[0] // TILE
    chunk_count = 4 * tensor_count
    w_self_at = NROWS

    def mult(value, by):
        return pl.multiple_of(value, by)

    def chunk_part(chunk):
        return lax.rem(z + 1 + chunk % tensor_count, tensor_count)

    def own_ref(chunk):
        unit, part = chunk // tensor_count, chunk_part(chunk)
        if unit < 2:
            return g_mlp, (unit * tensor_count + part) * quad
        return g_sc, (((unit - 2) * 2 + core) * tensor_count + part) * quad

    def rows_at(start, count):
        return pl.ds(mult(start, shard), count)

    def remote(source, target, send, recv, device):
        return pltpu.make_async_remote_copy(
            src_ref=source,
            dst_ref=target,
            send_sem=send,
            recv_sem=recv,
            device_id=device,
            device_id_type=MESH,
        )

    def c_slot(chunk):
        return rc.at[chunk % 8]

    def c_whole(chunk):
        return remote(
            c_slot(chunk), c_slot(chunk), c_ssem.at[chunk], c_rsem.at[chunk], (other, z)
        )

    def c_start(chunk):
        unit, part = chunk // tensor_count, chunk_part(chunk)
        if unit < 2:
            source = (gdn_h, gup_h)[unit]
            for q in range(4):
                start = part * D + (2 * q + 1 - core) * shard
                remote(
                    source.at[rows_at(start, shard)],
                    c_slot(chunk).at[pl.ds(q * shard, shard)],
                    c_ssem.at[chunk],
                    c_rsem.at[chunk],
                    (other, z),
                ).start()
        else:
            start = (((unit - 2) * 2 + 1 - core) * tensor_count + part) * quad
            remote(
                g_sc.at[rows_at(start, quad)],
                c_slot(chunk),
                c_ssem.at[chunk],
                c_rsem.at[chunk],
                (other, z),
            ).start()

    def b_copy(chunk, half):
        ref, base = own_ref(chunk)
        q = (1 - core) * ((1 - yy) * 2 + half) + core * (half * 2 + 1 - xx)
        number = chunk * 2 + half
        return remote(
            ref.at[rows_at(base + q * shard, shard)],
            rb.at[chunk % 6, half],
            b_ssem.at[number],
            b_rsem.at[number],
            (second, z),
        )

    def a_copy(chunk):
        ref, base = own_ref(chunk)
        q = (1 - core) * (yy * 2 + 1 - xx) + core * ((1 - yy) * 2 + xx)
        return remote(
            ref.at[rows_at(base + q * shard, shard)],
            ra.at[chunk % 4],
            a_ssem.at[chunk],
            a_rsem.at[chunk],
            (first, z),
        )

    def z_copy(chunk):
        unit, step = divmod(chunk, tensor_count)
        ref, base = own_ref(chunk)
        number = unit * (tensor_count - 1) + step
        return remote(
            ref.at[rows_at(base + (yy * 2 + xx) * shard, shard)],
            rz.at[number],
            z_ssem.at[number],
            z_rsem.at[number],
            (dp, peers[step]),
        )

    piece = 32

    def add_rows(ref, start, source, count):
        def body(index, carry):
            rows = pl.ds(mult(start + index * piece, piece), piece)
            part = source[pl.ds(mult(index * piece, piece), piece), :]
            ref[rows, :] = (ref[rows, :].astype(F32) + part.astype(F32)).astype(BF)
            return carry

        lax.fori_loop(0, count // piece, body, 0)

    def stage1(chunk):
        c_whole(chunk).wait_recv()
        ref, base = own_ref(chunk)
        add_rows(ref, base, c_slot(chunk), quad)
        if chunk in (3, 7):
            pl.semaphore_signal(
                credit, inc=1, device_id=(other, z), device_id_type=MESH
            )
        for half in range(2):
            b_copy(chunk, half).start()

    def stage2(chunk):
        ref, base = own_ref(chunk)
        for half in range(2):
            b_copy(chunk, half).wait_recv()
            q = (1 - core) * (yy * 2 + half) + core * (half * 2 + xx)
            add_rows(ref, base + q * shard, rb.at[chunk % 6, half], shard)
        a_copy(chunk).start()

    def stage3(chunk):
        a_copy(chunk).wait_recv()
        ref, base = own_ref(chunk)
        add_rows(ref, base + (yy * 2 + xx) * shard, ra.at[chunk % 4], shard)
        if chunk % tensor_count < tensor_count - 1:
            z_copy(chunk).start()

    def finish(unit):
        chunk = unit * tensor_count + tensor_count - 1
        ref, base = own_ref(chunk)
        target = (gdn_o, gup_o, gself_o, gcross_o)[unit]
        for step in range(tensor_count - 1):
            z_copy(unit * tensor_count + step).wait_recv()

        def body(index, carry):
            rows = pl.ds(mult(index * piece, piece), piece)
            start = base + (yy * 2 + xx) * shard + index * piece
            total = ref[pl.ds(mult(start, piece), piece), :].astype(F32)
            for step in range(tensor_count - 1):
                total = total + rz[unit * (tensor_count - 1) + step, rows, :].astype(F32)
            target[rows, :] = total
            return carry

        lax.fori_loop(0, shard // piece, body, 0)

    ahead = 2

    def comm(step):
        if step + ahead < chunk_count:
            stage1(step + ahead)
        if step < chunk_count:
            stage2(step)
        if 0 <= step - 1 < chunk_count:
            stage3(step - 1)
        done = step - 2
        if done >= 0 and done % tensor_count == tensor_count - 1:
            finish(done // tensor_count)

    def send_unit(unit):
        pl.semaphore_wait(credit, 1)
        for chunk in range(unit * tensor_count, (unit + 1) * tensor_count):
            c_start(chunk)

    def store_grad(unit, block, values):
        for part in range(8):
            parity, zpart = divmod(part, tensor_count)
            start = (((unit * 2 + parity) * tensor_count + zpart) * 4 + block) * shard
            g_sc[start : start + shard, :] = values[part * shard : (part + 1) * shard].astype(BF)

    def load(source, target, number):
        return pltpu.make_async_copy(source, target, load_sem.at[number])

    w_self = g_sc.at[pl.ds(w_self_at, NROWS)]
    for chunk in range(2 * tensor_count):
        c_start(chunk)
    load(ws_h, w_self, 0).start()
    for unit in range(2):
        source = (gdn_h, gup_h)[unit]
        for part in range(tensor_count):
            for q in range(4):
                pltpu.make_async_copy(
                    source.at[rows_at(part * D + (2 * q + core) * shard, shard)],
                    g_mlp.at[pl.ds(((unit * tensor_count + part) * 4 + q) * shard, shard)],
                    load_sem.at[1 + unit],
                ).start()
    lat_rows = 2 * LAT
    late, gn3, read2 = (dwk.at[pl.ds(third * lat_rows, lat_rows)] for third in range(3))
    read, mid, lat = (dwv.at[pl.ds(third * lat_rows, lat_rows)] for third in range(3))
    prob2 = pt.at[:, :, :, pl.ds(0, LAT)]
    early = [
        (cot_h, glat_o),
        (late_h, late),
        (gn3_h, gn3),
        (read2_h, read2),
        (read_h, read),
        (mid_h, mid),
        (prob2_h, prob2),
        (query2_h, kt.at[0]),
        (key2_h, kt.at[1]),
        (val2_h, vt.at[0]),
        (query_h, vt.at[1]),
    ]
    query2, key2, val2, query = kt.at[0], kt.at[1], vt.at[0], vt.at[1]
    for number, (source, target) in enumerate(early):
        load(source, target, 5 + number).start()
    load(wc_h, w_cross, 3).start()

    def load_p1(extra):
        return load(prob_h.at[:, :, pl.ds((tiles + extra) * TILE, TILE)], p1, 4)

    load_p1(0).start()
    half_mlp = tensor_count * quad
    for unit in range(2):
        whole = g_mlp.at[pl.ds(unit * half_mlp, half_mlp)]
        load(whole, whole, 1 + unit).wait()
    for chunk in range(ahead):
        stage1(chunk)
    comm(0)

    def vec(row):
        return vecs[row : row + 1, :]

    mask = head_mask(GHEADS * LAT)
    gvec[...] = jnp.zeros(gvec.shape, F32)

    def note(row, values):
        gvec[row : row + 1, :] = values

    def col_sum(values):
        return jnp.sum(values.astype(F32), axis=0, keepdims=True)

    def row_terms(grad_block, read_block):
        wide = jnp.concatenate([grad_block.astype(F32) * read_block] * GHEADS, axis=0)
        return jnp.sum(jnp.where(mask, wide, 0.0), axis=1, keepdims=True)

    for number, (source, target) in enumerate(early):
        load(source, target, 5 + number).wait()
    note(14, col_sum(glat_o[...].astype(BF)))
    gvec[15 : 15 + tensor_count, :] = gb1[0:tensor_count, :]
    back, gain, shift = ln_back(late[...], vec(12), gn3[...])
    note(12, gain)
    note(13, shift)
    gas = glat_o[...] + back
    glat_o[...] = gas
    grad_out = gas.astype(BF)
    note(11, col_sum(grad_out))
    load(ws_h, w_self, 0).wait()

    def self_block(block):
        return g_sc[w_self_at + block * D : w_self_at + (block + 1) * D, :]

    store_grad(0, 3, nn(read2[...].T.astype(BF), grad_out))
    gread[...] = nt(grad_out, self_block(3)).astype(BF)
    comm(1)
    for slot in range(2):
        srows = slice(slot * LAT, (slot + 1) * LAT)
        for group in range(GROUPS):
            gcols = slice(group * GROUP, (group + 1) * GROUP)
            grads = spread_heads(gread[srows, gcols], mask)
            inner = row_terms(gread[srows, gcols], read2[srows, gcols])
            chance = prob2[slot, group]
            dprob = nt(grads, val2[srows, gcols])
            dscore = (chance.astype(F32) * (dprob - inner)).astype(BF)
            dq2[srows, gcols] = (
                pick_heads(nn(dscore, key2[srows, gcols])) * HEAD_DIM ** (-0.5)
            ).astype(BF)
            wide = spread_heads(query2[srows, gcols], mask)
            dk2[srows, gcols] = tn(dscore, wide).astype(BF)
            dv2[srows, gcols] = tn(chance, grads).astype(BF)
    comm(2)
    note(9, col_sum(dq2[...]))
    note(10, col_sum(dv2[...]))
    unit_two, scale_two = ln_parts(mid[...])
    norm_t = (unit_two * vec(7) + vec(8)).T.astype(BF)
    store_grad(0, 0, nn(norm_t, dq2[...]))
    store_grad(0, 1, nn(norm_t, dk2[...]))
    store_grad(0, 2, nn(norm_t, dv2[...]))
    incoming = nt(dq2[...], self_block(0)) + nt(dk2[...], self_block(1))
    incoming = incoming + nt(dv2[...], self_block(2))
    back, gain, shift = ln_back(mid[...], vec(7), incoming)
    note(7, gain)
    note(8, shift)
    total = glat_o[...] + back
    glat_o[...] = total
    grad_out = total.astype(BF)
    note(6, col_sum(grad_out))
    load(wc_h, w_cross, 3).wait()
    store_grad(1, 3, nn(read[...].T.astype(BF), grad_out))
    gread[...] = nt(grad_out, w_cross[3 * D :, :]).astype(BF)
    for slot in range(2):
        srows = slice(slot * LAT, (slot + 1) * LAT)
        for group in range(GROUPS):
            gcols = slice(group * GROUP, (group + 1) * GROUP)
            at = slot * GROUPS + group
            grads = jnp.concatenate([gread[srows, gcols].astype(F32)] * GHEADS, axis=0)
            grads = jnp.where(mask, grads, 0.0).T * inv[at : at + 1, :]
            gbd_t[at] = grads.astype(BF)
            grads = grads.T
            gbd[at] = grads.astype(BF)
            wide = jnp.concatenate([query[srows, gcols].astype(F32)] * GHEADS, axis=0)
            qbd_t[at] = jnp.where(mask, wide, 0.0).T.astype(BF)
            wide = jnp.concatenate([read[srows, gcols]] * GHEADS, axis=0)
            inner = jnp.sum(grads * wide, axis=1, keepdims=True)
            row_r[at] = jnp.broadcast_to(inner, (GHEADS * LAT, LANES))
    dqacc[...] = jnp.zeros(dqacc.shape, F32)
    dwk[...] = jnp.zeros(dwk.shape, F32)
    dwv[...] = jnp.zeros(dwv.shape, F32)
    gbias[...] = jnp.zeros(gbias.shape, F32)
    it[0] = jnp.zeros(it.shape[1:], BF)
    comm(3)

    def fetches(index):
        slot = lax.rem(index, 2)
        rows = pl.ds(mult(index * TILE, TILE), TILE)
        copies = [
            (key_h.at[rows], kt.at[slot]),
            (val_h.at[rows], vt.at[slot]),
            (ctx_h.at[rows], ct.at[slot]),
            (prob_h.at[:, :, rows], pt.at[slot]),
        ]
        return [
            pltpu.make_async_copy(source, target, tile_sem.at[slot, number])
            for number, (source, target) in enumerate(copies)
        ]

    def spill(index):
        slot = lax.rem(index, 2)
        return pltpu.make_async_copy(dkv.at[slot], dkv_h.at[index], tile_sem.at[slot, 4])

    for copy in fetches(jnp.int32(0)):
        copy.start()

    def attend_back(slot, chance_of, buffer, first_time):
        for group in range(GROUPS):
            gcols = slice(group * GROUP, (group + 1) * GROUP)
            at = slot * GROUPS + group
            chance = chance_of(group)
            dprob = nt(gbd[at], vt[buffer, :, gcols])
            inner = row_r[at]
            dscore = chance.astype(F32) * (dprob - jnp.concatenate([inner, inner], axis=1))
            dscore = dscore.astype(BF)
            dk_part = nn(qbd_t[at], dscore)
            dv_part = nn(gbd_t[at], chance)
            if first_time:
                dk_t[gcols, :] = dk_part
                dv_t[gcols, :] = dv_part
            else:
                dk_t[gcols, :] += dk_part
                dv_t[gcols, :] += dv_part
            dqacc[at] += nn(dscore, kt[buffer, :, gcols])

    def between(index, plan):
        for at, action in plan.items():
            pl.when(index == at)(action)

    def tile_body(index, carry):
        buffer = lax.rem(index, 2)

        @pl.when(index + 1 < tiles)
        def _():
            for copy in fetches(index + 1):
                copy.start()

        for copy in fetches(index):
            copy.wait()
        attend_back(0, lambda group: pt[buffer, group], buffer, True)
        for extra in range(SLOT1_TILES):

            @pl.when(index == SLOT1_FIRST + extra)
            def _():
                load_p1(extra).wait()
                attend_back(1, lambda group: p1[group], buffer, False)
                if extra + 1 < SLOT1_TILES:
                    load_p1(extra + 1).start()

        @pl.when(index > 1)
        def _():
            spill(index - 2).wait()

        dk = dk_t[...].astype(BF)
        dv = dv_t[...].astype(BF)
        dkv[buffer, 0] = dk
        dkv[buffer, 1] = dv
        spill(index).start()
        gbias[...] += dv[:, :LANES].astype(F32) + dv[:, LANES:].astype(F32)
        block = ct[buffer]
        dwk[...] += nn(dk, block)
        dwv[...] += nn(dv, block)

        def self_step():
            send_unit(2)
            comm(6)

        plan = {1: partial(comm, 4), 3: partial(comm, 5), 5: self_step}
        plan.update({7: partial(comm, 7), 9: partial(comm, 8), 11: partial(comm, 9)})
        between(index, plan)
        return carry

    lax.fori_loop(0, tiles, tile_body, 0)
    store_grad(1, 2, dwv[...].T)
    load(lat_h, lat, 16).start()
    store_grad(1, 1, dwk[...].T)
    for slot in range(2):
        srows = slice(slot * LAT, (slot + 1) * LAT)
        for group in range(GROUPS):
            gcols = slice(group * GROUP, (group + 1) * GROUP)
            dq2[srows, gcols] = (
                pick_heads(dqacc[slot * GROUPS + group]) * HEAD_DIM ** (-0.5)
            ).astype(BF)
    load(lat_h, lat, 16).wait()
    unit_one, scale_one = ln_parts(lat[...])
    norm_t = (unit_one * vec(0) + vec(1)).T.astype(BF)
    store_grad(1, 0, nn(norm_t, dq2[...]))
    send_unit(3)
    spill(tiles - 2).wait()
    spill(tiles - 1).wait()
    comm(10)

    def fetch_back(index, at_start):
        slot = 0 if at_start else lax.rem(index, 2)
        back_rows = inp.at[pl.ds(0, TILE - PAD)]
        target = it.at[0, pl.ds(PAD, TILE - PAD)]
        if not at_start:
            back_rows = inp.at[pl.ds(mult(index * TILE - PAD, PAD), TILE)]
            target = it.at[slot]
        tile = 0 if at_start else index
        return [
            pltpu.make_async_copy(back_rows, target, tile_sem.at[slot, 0]),
            pltpu.make_async_copy(dkv_h.at[tile], dkv.at[slot], tile_sem.at[slot, 1]),
        ]

    def put(index, at_start):
        slot = 0 if at_start else lax.rem(index, 2)
        if at_start:
            source, rows = ot.at[0, pl.ds(PAD, TILE - PAD)], pl.ds(0, TILE - PAD)
        else:
            source, rows = ot.at[slot], pl.ds(mult(index * TILE - PAD, PAD), TILE)
        return pltpu.make_async_copy(source, ginp_o.at[rows], tile_sem.at[slot, 5])

    for copy in fetch_back(0, True):
        copy.start()

    def token_body(index, carry):
        buffer = lax.rem(index, 2)

        @pl.when(index + 1 < tiles)
        def _():
            for copy in fetch_back(index + 1, False):
                copy.start()

        @pl.when(index == 0)
        def _():
            for copy in fetch_back(0, True):
                copy.wait()

        @pl.when(index > 0)
        def _():
            for copy in fetch_back(index, False):
                copy.wait()

        incoming = nn(w_cross[D : 2 * D, :], dkv[buffer, 0])
        incoming = incoming + nn(w_cross[2 * D : 3 * D, :], dkv[buffer, 1])
        back, gain, shift = ln_back(it[buffer].astype(F32), vec(2), incoming.T)
        gvec[2:3, :] += gain
        gvec[3:4, :] += shift

        @pl.when(index == 2)
        def _():
            put(0, True).wait()

        @pl.when(index > 2)
        def _():
            put(index - 2, False).wait()

        ot[buffer] = back.astype(BF)

        @pl.when(index == 0)
        def _():
            put(0, True).start()

        @pl.when(index > 0)
        def _():
            put(index, False).start()

        between(index, {2: partial(comm, 11), 6: partial(comm, 12), 10: partial(comm, 13)})
        return carry

    lax.fori_loop(0, tiles, token_body, 0)
    note(4, col_sum(dq2[...]))
    note(5, jnp.sum(gbias[...].T, axis=0, keepdims=True))
    incoming = nt(dq2[...], w_cross[0:D, :])
    back, gain, shift = ln_back(lat[...], vec(0), incoming)
    note(0, gain)
    note(1, shift)
    glat_o[...] = glat_o[...] + back

    def vec_copy(hop):
        if hop < 3:
            source, device = vec_sum.at[hop], ((other, second, first)[hop], z)
        else:
            source, device = vec_sum.at[3], (dp, peers[hop - 3])
        return remote(source, vec_in.at[hop], v_ssem.at[hop], v_rsem.at[hop], device)

    total = gvec[...]
    for hop in range(3):
        vec_sum[hop] = total
        vec_copy(hop).start()
        comm(14 + hop)
        vec_copy(hop).wait_recv()
        total = total + vec_in[hop]
    vec_sum[3] = total
    for hop in range(3, 2 + tensor_count):
        vec_copy(hop).start()
    comm(17)
    for hop in range(3, 2 + tensor_count):
        vec_copy(hop).wait_recv()
        total = total + vec_in[hop]
    width = gvec_o.shape[1]
    turn = lax.rem(D - (dp * tensor_count + z) * width, D)
    gvec_o[...] = pltpu.roll(total, turn, 1)[0 : gvec_o.shape[0], 0:width]
    put(tiles - 2, False).wait()
    put(tiles - 1, False).wait()
    for hop in range(2 + tensor_count):
        vec_copy(hop).wait_send()
    for chunk in range(chunk_count):
        c_whole(chunk).wait_send()
        b_copy(chunk, 0).wait_send()
        b_copy(chunk, 1).wait_send()
        a_copy(chunk).wait_send()
        if chunk % tensor_count < tensor_count - 1:
            z_copy(chunk).wait_send()


def backward_call(tensor_count, shard, vec_shape, operands):
    sds = jax.ShapeDtypeStruct
    hbm = pl.BlockSpec(memory_space=pl.ANY)
    vmem = pl.BlockSpec(memory_space=pltpu.VMEM)
    rows = operands[0].shape[0]
    inp = operands[-1]
    stacked = GHEADS * LAT
    chunks = 4 * tensor_count
    zs = 4 * (tensor_count - 1)
    at = 2 * GROUPS
    sem = pltpu.SemaphoreType.DMA
    outs = [
        (sds((rows, D), F32), vmem),
        (sds(inp.shape, BF), hbm),
        (sds((shard, D), F32), vmem),
        (sds((shard, D), F32), vmem),
        (sds(vec_shape, F32), vmem),
        (sds((shard, D), F32), vmem),
        (sds((shard, D), F32), vmem),
        (sds(((inp.shape[0] + PAD) // TILE, 2, D, TILE), BF), hbm),
    ]
    return pl.pallas_call(
        partial(backward_kernel, tensor_count),
        out_shape=[shape for shape, spec in outs],
        out_specs=[spec for shape, spec in outs],
        in_specs=[hbm] * 12 + [vmem] * 3 + [hbm] * 9,
        scratch_shapes=[
            pltpu.VMEM((NROWS, D), BF),
            pltpu.VMEM((NROWS, D), BF),
            pltpu.VMEM((2 * NROWS, D), BF),
            pltpu.VMEM((8, 4 * shard, D), BF),
            pltpu.VMEM((6, 2, shard, D), BF),
            pltpu.VMEM((4, shard, D), BF),
            pltpu.VMEM((zs, shard, D), BF),
            pltpu.VMEM((D, D), F32),
            pltpu.VMEM((D, D), F32),
            pltpu.VMEM((2, TILE, D), BF),
            pltpu.VMEM((2, TILE, D), BF),
            pltpu.VMEM((2, TILE, D), BF),
            pltpu.VMEM((2, TILE, D), BF),
            pltpu.VMEM((2, GROUPS, stacked, TILE), BF),
            pltpu.VMEM((GROUPS, stacked, TILE), BF),
            pltpu.VMEM((2, TILE, D), BF),
            pltpu.VMEM((D, TILE), F32),
            pltpu.VMEM((D, TILE), F32),
            pltpu.VMEM((2, 2, D, TILE), BF),
            pltpu.VMEM((at, stacked, GROUP), BF),
            pltpu.VMEM((at, GROUP, stacked), BF),
            pltpu.VMEM((at, GROUP, stacked), BF),
            pltpu.VMEM((at, stacked, LANES), F32),
            pltpu.VMEM((at, stacked, GROUP), F32),
            pltpu.VMEM((rows, D), BF),
            pltpu.VMEM((rows, D), BF),
            pltpu.VMEM((rows, D), BF),
            pltpu.VMEM((rows, D), BF),
            pltpu.VMEM((D, LANES), F32),
            pltpu.VMEM((VEC_PAD, D), F32),
            pltpu.VMEM((2 + tensor_count, VEC_PAD, D), F32),
            pltpu.VMEM((4, VEC_PAD, D), F32),
            sem((chunks,)),
            sem((chunks,)),
            sem((2 * chunks,)),
            sem((2 * chunks,)),
            sem((chunks,)),
            sem((chunks,)),
            sem((zs,)),
            sem((zs,)),
            sem((2 + tensor_count,)),
            sem((2 + tensor_count,)),
            sem((2, 6)),
            sem((17,)),
            pltpu.SemaphoreType.REGULAR,
        ],
        compiler_params=pltpu.CompilerParams(
            collective_id=1, has_side_effects=True, vmem_limit_bytes=VMEM_LIMIT
        ),
        name="backward_scatter",
    )(*operands)


def local_fused(
    latents,
    inputs,
    segment,
    cross_weights,
    self_weights,
    vectors,
    up_weight,
    down_weight,
    cotangent,
):
    tensor_count = lax.axis_size("tensor")
    shard = cross_weights.shape[0]
    seg = segment.reshape(-1, LANES)
    (
        latents_out,
        wc,
        ws,
        ctx,
        keys,
        vals,
        prob,
        gup,
        gdn,
        vecs,
        query,
        read,
        mid,
        query2,
        key2,
        val2,
        prob2,
        read2,
        late,
        gn3,
        gb1,
        inv,
    ) = forward_call(
        tensor_count,
        latents,
        inputs,
        seg,
        cross_weights,
        self_weights,
        up_weight,
        down_weight.T,
        vectors,
        cotangent,
    )
    operands = [latents, cotangent, mid, late, gn3, read, read2, query, query2, key2, val2]
    operands += [prob2, vecs, gb1, inv, wc, ws, ctx, keys, vals, prob, gup, gdn, inputs]
    glat, ginp, gcross, gself, gvec, gup_sum, gdn_sum, unused = backward_call(
        tensor_count, shard, vectors.shape, operands
    )
    return latents_out, glat, ginp, gcross, gself, gvec, gup_sum, gdn_sum.T


def solution(mesh):
    placed = (
        P(("dp", "tensor"), None),
        P(("dp", "tensor"), None),
        P(("dp", "tensor")),
        P(("dp", "tensor"), None),
        P(("dp", "tensor"), None),
        P(None, ("dp", "tensor")),
        P("dp", "tensor"),
        P("tensor", "dp"),
        P(("dp", "tensor"), None),
    )
    shards = mesh.shape["dp"] * mesh.shape["tensor"]
    fused = mesh.shape["dp"] == 8 and mesh.shape["tensor"] == 4 and 4 * D % (32 * shards) == 0
    return jax.shard_map(
        local_fused if fused else local,
        mesh=mesh,
        in_specs=placed,
        out_specs=(
            P(("dp", "tensor"), None),
            P(("dp", "tensor"), None),
            P(("dp", "tensor"), None),
            P(("dp", "tensor"), None),
            P(("dp", "tensor"), None),
            P(None, ("dp", "tensor")),
            P("dp", "tensor"),
            P("tensor", "dp"),
        ),
        check_vma=False,
    )
```

```python
from functools import partial

import jax
import jax.numpy as jnp
from jax import lax
from jax.experimental import pallas as pl
from jax.experimental.pallas import tpu as pltpu
from jax.sharding import PartitionSpec as P

D = 768
HEAD_DIM = 64
FF = 3072
LAT = 128


def cut_along(x, dim, size):
    before, after = (x.shape[:dim], x.shape[dim + 1 :])
    return jnp.moveaxis(x.reshape(*before, size, -1, *after), dim, 0)


def sent_and_summed(x, axis, dim):
    parts = cut_along(x, dim, lax.axis_size(axis))
    arrived = lax.all_to_all(parts, axis, split_axis=0, concat_axis=0, tiled=True)
    return arrived.astype(jnp.float32).sum(axis=0)


def product(left, right):
    return jnp.dot(left, right, preferred_element_type=jnp.float32)


def product_tn(left, right):
    return lax.dot_general(
        left, right, (((0,), (0,)), ((), ())), preferred_element_type=jnp.float32
    )


def product_nt(left, right):
    return lax.dot_general(
        left, right, (((1,), (1,)), ((), ())), preferred_element_type=jnp.float32
    )


def layer_norm(values, gain_row, shift_row):
    average = jnp.mean(values, axis=-1, keepdims=True)
    centred = values - average
    variance = jnp.mean(centred * centred, axis=-1, keepdims=True)
    return centred * lax.rsqrt(variance + 1e-05) * gain_row + shift_row


def norm_backward(values, gain_row, shift_row, incoming):
    unused, pullback = jax.vjp(layer_norm, values, gain_row, shift_row)
    return pullback(incoming)


def split_heads(values):
    return values.reshape(values.shape[0], -1, HEAD_DIM).transpose(1, 0, 2)


def merge_heads(values):
    return values.transpose(1, 0, 2).reshape(values.shape[1], -1)


def head_probs(head_query, head_key, visible, peak_score, denominator):
    scores = product_nt(head_query, head_key) * HEAD_DIM ** (-0.5)
    exponent = jnp.exp(jnp.where(visible, scores - peak_score, -200.0)) * visible.astype(
        jnp.float32
    )
    return exponent / denominator


def attend_forward(queries, keys_in, values_in, visible):
    has_keys = jnp.any(visible, axis=-1, keepdims=True)
    seen_float = visible.astype(jnp.float32)

    def one_head(operands):
        head_query, head_key, head_value = operands
        scores = product_nt(head_query, head_key) * HEAD_DIM ** (-0.5)
        peak_score = jnp.max(jnp.where(visible, scores, -1000000000.0), axis=-1, keepdims=True)
        peak_score = jnp.where(has_keys, peak_score, 0.0)
        exponent = jnp.exp(jnp.where(visible, scores - peak_score, -200.0)) * seen_float
        denominator = jnp.sum(exponent, axis=-1, keepdims=True) + 1.0 - has_keys.astype(jnp.float32)
        attn_probs = (exponent / denominator).astype(jnp.bfloat16)
        return (product(attn_probs, head_value), peak_score, denominator)

    outputs, peaks, denominators = lax.map(
        one_head, (split_heads(queries), split_heads(keys_in), split_heads(values_in))
    )
    return (merge_heads(outputs).astype(jnp.bfloat16), peaks, denominators)


def attend_backward(queries, keys_in, values_in, visible, peaks, denominators, grad_read):
    score_scale = HEAD_DIM ** (-0.5)

    def one_head(operands):
        head_query, head_key, head_value, peak_score, denominator, head_grad = operands
        attn_probs = head_probs(head_query, head_key, visible, peak_score, denominator)
        grad_probs = product_nt(head_grad, head_value)
        grad_value = product_tn(attn_probs.astype(jnp.bfloat16), head_grad)
        inner_sum = jnp.sum(grad_probs * attn_probs, axis=-1, keepdims=True)
        grad_scores = (attn_probs * (grad_probs - inner_sum)).astype(jnp.bfloat16)
        grad_query = product(grad_scores, head_key) * score_scale
        grad_key = product_tn(grad_scores, head_query) * score_scale
        return (grad_query, grad_key, grad_value)

    grad_q, grad_k, grad_v = lax.map(
        one_head,
        (
            split_heads(queries),
            split_heads(keys_in),
            split_heads(values_in),
            peaks,
            denominators,
            split_heads(grad_read),
        ),
    )
    return (
        merge_heads(grad_q).astype(jnp.bfloat16),
        merge_heads(grad_k).astype(jnp.bfloat16),
        merge_heads(grad_v).astype(jnp.bfloat16),
    )


def column_sum(values):
    return jnp.sum(values.astype(jnp.float32), axis=0)


def local(
    latents,
    inputs,
    segment,
    cross_weights,
    self_weights,
    vectors,
    up_weight,
    down_weight,
    cotangent,
):
    cross_full, self_full, vector_half = (
        lax.all_gather(cross_weights, ("dp", "tensor"), axis=0, tiled=True),
        lax.all_gather(self_weights, ("dp", "tensor"), axis=0, tiled=True),
        lax.all_gather(vectors, ("dp", "tensor"), axis=1, tiled=True),
    )
    up_full, down_full = (
        lax.all_gather(up_weight, "dp", axis=0, tiled=True),
        lax.all_gather(down_weight, "dp", axis=1, tiled=True),
    )
    vector_rows = vector_half.astype(jnp.float32)
    quarter = up_full.shape[1]
    part_index = lax.axis_index("tensor")
    bias_up = lax.dynamic_slice_in_dim(
        vector_rows[15:].reshape(-1), part_index * quarter, quarter, 0
    )
    row_count = latents.shape[0]
    slot_row = jnp.arange(row_count, dtype=jnp.int32) // LAT
    cross_seen = slot_row[:, None] == segment[None, :]
    self_seen = slot_row[:, None] == slot_row[None, :]
    input_float = inputs.astype(jnp.float32)
    normed = layer_norm(latents, vector_rows[0], vector_rows[1]).astype(jnp.bfloat16)
    context = layer_norm(input_float, vector_rows[2], vector_rows[3]).astype(jnp.bfloat16)
    queries = (product(normed, cross_full[:D]) + vector_rows[4]).astype(jnp.bfloat16)
    keys_in = product(context, cross_full[D : 2 * D]).astype(jnp.bfloat16)
    values_in = (product(context, cross_full[2 * D : 3 * D]) + vector_rows[5]).astype(jnp.bfloat16)
    cross_read, cross_peaks, cross_denoms = attend_forward(queries, keys_in, values_in, cross_seen)
    after_cross = latents + (product(cross_read, cross_full[3 * D :]) + vector_rows[6])
    normed_two = layer_norm(after_cross, vector_rows[7], vector_rows[8]).astype(jnp.bfloat16)
    queries_two = (product(normed_two, self_full[:D]) + vector_rows[9]).astype(jnp.bfloat16)
    keys_two = product(normed_two, self_full[D : 2 * D]).astype(jnp.bfloat16)
    values_two = (product(normed_two, self_full[2 * D : 3 * D]) + vector_rows[10]).astype(
        jnp.bfloat16
    )
    self_read, self_peaks, self_denoms = attend_forward(
        queries_two, keys_two, values_two, self_seen
    )
    after_self = after_cross + (product(self_read, self_full[3 * D :]) + vector_rows[11])
    normed_three = layer_norm(after_self, vector_rows[12], vector_rows[13]).astype(jnp.bfloat16)
    gathered = lax.all_gather(normed_three, "tensor", axis=0, tiled=True)
    pre_act = product(gathered, up_full) + bias_up
    hidden = jax.nn.gelu(pre_act, approximate=False).astype(jnp.bfloat16)
    reduced = lax.psum_scatter(
        product(hidden, down_full).astype(jnp.bfloat16), "tensor", scatter_dimension=0, tiled=True
    ).astype(jnp.float32)
    latents_out = after_self + (reduced + vector_rows[14])
    cross_full, self_full, vector_half = (
        lax.all_gather(cross_weights, ("dp", "tensor"), axis=0, tiled=True),
        lax.all_gather(self_weights, ("dp", "tensor"), axis=0, tiled=True),
        lax.all_gather(vectors, ("dp", "tensor"), axis=1, tiled=True),
    )
    up_full, down_full = (
        lax.all_gather(up_weight, "dp", axis=0, tiled=True),
        lax.all_gather(down_weight, "dp", axis=1, tiled=True),
    )
    vector_rows = vector_half.astype(jnp.float32)
    grad_y = cotangent.astype(jnp.bfloat16)
    grad_b2 = column_sum(grad_y)
    grad_rows = lax.all_gather(grad_y, "tensor", axis=0, tiled=True)
    grad_down = product_tn(hidden, grad_rows)
    grad_hidden = product_nt(grad_rows, down_full)
    unused, gelu_pull = jax.vjp(partial(jax.nn.gelu, approximate=False), pre_act)
    grad_pre = gelu_pull(grad_hidden)[0].astype(jnp.bfloat16)
    grad_b1 = column_sum(grad_pre)
    grad_up = product_tn(gathered, grad_pre)
    mlp_sums = (
        sent_and_summed(grad_up.astype(jnp.bfloat16), "dp", 0),
        sent_and_summed(grad_down.astype(jnp.bfloat16), "dp", 1),
    )
    grad_normed_three = lax.psum_scatter(
        product_nt(grad_pre, up_full).astype(jnp.bfloat16),
        "tensor",
        scatter_dimension=0,
        tiled=True,
    ).astype(jnp.float32)
    back_self, grad_gain_three, grad_shift_three = norm_backward(
        after_self, vector_rows[12], vector_rows[13], grad_normed_three
    )
    grad_after_self = cotangent + back_self
    grad_out_two = grad_after_self.astype(jnp.bfloat16)
    grad_bias_out_two = column_sum(grad_out_two)
    grad_wo_two = product_tn(self_read, grad_out_two)
    grad_read_two = product_nt(grad_out_two, self_full[3 * D :]).astype(jnp.bfloat16)
    grad_q_two, grad_k_two, grad_v_two = attend_backward(
        queries_two, keys_two, values_two, self_seen, self_peaks, self_denoms, grad_read_two
    )
    grad_self = jnp.concatenate(
        [
            product_tn(normed_two, grad_q_two),
            product_tn(normed_two, grad_k_two),
            product_tn(normed_two, grad_v_two),
            grad_wo_two,
        ],
        axis=0,
    )
    grad_normed_two = (
        product_nt(grad_q_two, self_full[:D])
        + product_nt(grad_k_two, self_full[D : 2 * D])
        + product_nt(grad_v_two, self_full[2 * D : 3 * D])
    )
    back_cross, grad_gain_two, grad_shift_two = norm_backward(
        after_cross, vector_rows[7], vector_rows[8], grad_normed_two
    )
    grad_after_cross = grad_after_self + back_cross
    grad_out_one = grad_after_cross.astype(jnp.bfloat16)
    grad_bias_out_one = column_sum(grad_out_one)
    grad_wo_one = product_tn(cross_read, grad_out_one)
    grad_read_one = product_nt(grad_out_one, cross_full[3 * D :]).astype(jnp.bfloat16)
    grad_q_one, grad_k_one, grad_v_one = attend_backward(
        queries, keys_in, values_in, cross_seen, cross_peaks, cross_denoms, grad_read_one
    )
    grad_cross = jnp.concatenate(
        [
            product_tn(normed, grad_q_one),
            product_tn(context, grad_k_one),
            product_tn(context, grad_v_one),
            grad_wo_one,
        ],
        axis=0,
    )
    grad_normed = product_nt(grad_q_one, cross_full[:D])
    back_latent, grad_gain_one, grad_shift_one = norm_backward(
        latents, vector_rows[0], vector_rows[1], grad_normed
    )
    grad_latents = grad_after_cross + back_latent
    grad_context = product_nt(grad_k_one, cross_full[D : 2 * D]) + product_nt(
        grad_v_one, cross_full[2 * D : 3 * D]
    )
    back_input, grad_gain_input, grad_shift_input = norm_backward(
        input_float, vector_rows[2], vector_rows[3], grad_context
    )
    grad_inputs = back_input.astype(jnp.bfloat16)
    full_bias = lax.dynamic_update_slice_in_dim(
        jnp.zeros((FF,), jnp.float32), grad_b1, part_index * quarter, 0
    )
    grad_vectors = jnp.concatenate(
        [
            jnp.stack(
                [
                    grad_gain_one,
                    grad_shift_one,
                    grad_gain_input,
                    grad_shift_input,
                    column_sum(grad_q_one),
                    column_sum(grad_v_one),
                    grad_bias_out_one,
                    grad_gain_two,
                    grad_shift_two,
                    column_sum(grad_q_two),
                    column_sum(grad_v_two),
                    grad_bias_out_two,
                    grad_gain_three,
                    grad_shift_three,
                    grad_b2,
                ],
                axis=0,
            ),
            full_bias.reshape(-1, D),
        ],
        axis=0,
    )
    cross_sums, self_sums, vector_sums = (
        lax.psum_scatter(grad_cross, ("dp", "tensor"), scatter_dimension=0, tiled=True),
        lax.psum_scatter(grad_self, ("dp", "tensor"), scatter_dimension=0, tiled=True),
        lax.psum_scatter(grad_vectors, ("dp", "tensor"), scatter_dimension=1, tiled=True),
    )
    return (
        latents_out,
        grad_latents,
        grad_inputs,
        cross_sums,
        self_sums,
        vector_sums,
        mlp_sums[0],
        mlp_sums[1],
    )


BF = jnp.bfloat16
F32 = jnp.float32
MESH = pl.DeviceIdType.MESH
TILE = 256
PAD = 128
GROUP = 256
GROUPS = D // GROUP
GHEADS = GROUP // HEAD_DIM
LANES = 128
HIDE = -1e30
VEC_PAD = 32
NROWS = 4 * D
SLOT1_FIRST = 2
SLOT1_TILES = 2
VMEM_LIMIT = 63 * 1024 * 1024


GATHER_PLAN = {
    "start": ((0, 0), (0, 4), (0, 8)),
    "vecb": ((1, 0),),
    "vecc": ((0, 1),),
    "ln0": ((0, 2),),
    "ln2": ((2, 0),),
    "ln3": ((0, 3), (1, 1)),
    "ln7": ((1, 2),),
    "ln9": ((0, 5),),
    "post": ((1, 3), (1, 4)),
    "q": ((3, 0), (0, 6), (2, 1), (2, 2), (3, 1), (1, 5), (3, 2), (0, 7), (2, 3), (2, 4), (3, 3)),
    "kv0": ((1, 6), (0, 9)),
    "kv3": ((2, 5), (0, 10)),
    "kv5": ((1, 7), (1, 8)),
    "kv9": ((2, 6), (0, 11)),
    "kv11": ((1, 9),),
    "p0_1": ((1, 10),),
    "t0": ((0, 12),),
    "p1_0": ((2, 7),),
    "p1_1": ((2, 8), (0, 13)),
    "p1_3": ((1, 11),),
    "p2_1": ((2, 9),),
    "p2_2": ((0, 14),),
    "p2_3": ((2, 10),),
    "self0": ((1, 12), (3, 4), (3, 5), (3, 6), (3, 7)),
    "self1": ((1, 13), (0, 15)),
    "up0": ((2, 11), (3, 8)),
    "up1": ((3, 9),),
    "up2": ((1, 14), (3, 10)),
    "up3": ((3, 11),),
    "down0": ((2, 12), (2, 13), (3, 12)),
    "down1": ((1, 15), (3, 13)),
    "down2": ((2, 14), (2, 15), (3, 14)),
    "down3": ((3, 15),),
}
SCATTER_PLAN = {
    "b": ((0, 0), (0, 1)),
    "d": ((0, 2),),
    "CS2": ((0, 3),),
    "e": ((1, 0), (1, 1)),
    "f": ((0, 4),),
    "t0": ((1, 2), (2, 0)),
    "t1": ((0, 5),),
    "t2": ((1, 3), (2, 1)),
    "t3": ((2, 2), (0, 6)),
    "t4": ((1, 4), (2, 3), (0, 7)),
    "t5": ((1, 5), (3, 0)),
    "t6": ((0, 8),),
    "t7": ((1, 6), (2, 4)),
    "t8": ((2, 5), (0, 9)),
    "t9": ((1, 7),),
    "t10": ((2, 6), (0, 10)),
    "t11": ((1, 8),),
    "t12": ((2, 7), (0, 11)),
    "g": ((1, 9), (3, 1)),
    "u0": ((1, 10), (2, 8)),
    "u1": ((2, 9),),
    "u2": ((0, 12),),
    "u3": ((1, 11), (0, 13)),
    "u4": ((2, 10),),
    "u6": ((0, 14),),
    "u8": ((1, 12), (2, 11)),
    "u9": ((0, 15), (3, 2)),
    "u11": ((1, 13),),
    "h": ((2, 12),),
    "v1": ((1, 14), (2, 13)),
    "v3": ((1, 15), (2, 14)),
    "end": ((2, 15), (3, 3)),
}


def nn(left, right):
    return jnp.dot(left, right, preferred_element_type=F32)


def nt(left, right):
    return lax.dot_general(
        left, right, (((1,), (1,)), ((), ())), preferred_element_type=F32
    )


def ln_parts(values):
    average = jnp.mean(values, axis=-1, keepdims=True)
    centred = values - average
    variance = jnp.mean(centred * centred, axis=-1, keepdims=True)
    scale = lax.rsqrt(variance + 1e-05)
    return centred * scale, scale


def ln_rows(values, gain_row, shift_row):
    return ln_parts(values)[0] * gain_row + shift_row


def neighbours(tensor_count):
    dp = lax.axis_index("dp")
    z = lax.axis_index("tensor")
    core = lax.rem(dp, 2)
    flip_x = dp + 2 * (1 - 2 * lax.rem(dp // 2, 2))
    flip_y = dp + 4 * (1 - 2 * (dp // 4))
    other = dp + 1 - 2 * core
    first = (1 - core) * flip_x + core * flip_y
    second = (1 - core) * flip_y + core * flip_x
    both = flip_x + flip_y - dp
    peers = [lax.rem(z + step, tensor_count) for step in range(1, tensor_count)]
    return dp, z, core, other, first, second, both, peers


def meet(dp, z, other, first, second, peers):
    barrier = pltpu.get_barrier_semaphore()
    devices = [(other, z), (first, z), (second, z)] + [(dp, peer) for peer in peers]
    for device in devices:
        pl.semaphore_signal(barrier, inc=1, device_id=device, device_id_type=MESH)
    pl.semaphore_wait(barrier, len(devices))


def head_mask(rows):
    row_head = lax.broadcasted_iota(jnp.int32, (rows, GROUP), 0) // LAT
    col_head = lax.broadcasted_iota(jnp.int32, (rows, GROUP), 1) // HEAD_DIM
    return row_head == col_head


def spread_heads(block, mask):
    wide = jnp.concatenate([block.astype(F32)] * GHEADS, axis=0)
    return jnp.where(mask, wide, 0.0).astype(BF)


def pick_heads(stacked):
    col_head = lax.broadcasted_iota(jnp.int32, (LAT, GROUP), 1) // HEAD_DIM
    total = jnp.zeros((LAT, GROUP), F32)
    for head in range(GHEADS):
        part = stacked[head * LAT : (head + 1) * LAT]
        total = total + jnp.where(col_head == head, part, 0.0)
    return total


def forward_kernel(
    tensor_count,
    lat,
    inp,
    seg_in,
    cross_shard,
    self_shard,
    up_shard,
    down_shard,
    vectors,
    cot,
    out_o,
    wc_o,
    ws_o,
    ctx_o,
    key_o,
    val_o,
    prob_o,
    gup_o,
    gdn_o,
    vec_o,
    query_h,
    read_h,
    mid_h,
    query2_h,
    key2_h,
    val2_h,
    prob2_h,
    read2_h,
    late_h,
    gn3_o,
    gb1_o,
    inv_o,
    query_o,
    read,
    mid_o,
    query2_o,
    key2_o,
    val2_o,
    prob2_o,
    read2_o,
    late_o,
    seg,
    vec_own,
    w_cross,
    w_self,
    w_up,
    w_down,
    ctx,
    keys,
    vals,
    scores,
    probs,
    inbuf,
    qbd,
    peak,
    denom,
    oacc,
    norm_t,
    gy_t,
    vec_in,
    vec_sum,
    send_sem,
    recv_sem,
    vec_ssem,
    vec_rsem,
    in_sem,
    out_sem,
):
    dp, z, core, other, first, second, both, peers = neighbours(tensor_count)
    meet(dp, z, other, first, second, peers)
    weights = (w_cross, w_self, w_up, w_down)
    shards = (cross_shard, self_shard, up_shard, down_shard)
    shard_rows = cross_shard.shape[0]
    tiles = ctx.shape[0] // TILE
    chunk_count = 4 * tensor_count
    kinds = 7

    def place(unit, owner, part):
        if unit < 2:
            start = (owner * tensor_count + part) * shard_rows
        else:
            start = part * D + owner * shard_rows
        return pl.ds(pl.multiple_of(start, shard_rows), shard_rows)

    def remote(source, target, number, device):
        return pltpu.make_async_remote_copy(
            src_ref=source,
            dst_ref=target,
            send_sem=send_sem.at[number],
            recv_sem=recv_sem.at[number],
            device_id=device,
            device_id_type=MESH,
        )

    def z_copy(unit, step):
        rows = place(unit, dp, z)
        number = chunk_count * kinds + unit * (tensor_count - 1) + step - 1
        return remote(shards[unit], weights[unit].at[rows], number, (dp, peers[step - 1]))

    def plane_copy(chunk, kind):
        unit, step = divmod(chunk, tensor_count)
        part = lax.rem(z - step + tensor_count, tensor_count)
        owner = (dp, dp, first, dp, first, second, both)[kind]
        target = (first, second, second, other, other, other, other)[kind]
        rows = place(unit, owner, part)
        return remote(
            weights[unit].at[rows], weights[unit].at[rows], chunk * kinds + kind, (target, z)
        )

    def z_start(unit):
        for step in range(1, tensor_count):
            z_copy(unit, step).start()

    def stage0(chunk):
        unit, step = divmod(chunk, tensor_count)
        if step:
            z_copy(unit, step).wait_recv()
        for kind in (0, 1, 3):
            plane_copy(chunk, kind).start()

    def stage1(chunk):
        plane_copy(chunk, 0).wait_recv()
        for kind in (2, 4):
            plane_copy(chunk, kind).start()

    def stage2(chunk):
        plane_copy(chunk, 1).wait_recv()
        plane_copy(chunk, 5).start()
        plane_copy(chunk, 2).wait_recv()
        plane_copy(chunk, 6).start()

    def stage3(chunk):
        for kind in (3, 4, 5, 6):
            plane_copy(chunk, kind).wait_recv()

    def send_first(chunk):
        stage0(chunk)
        unit, step = divmod(chunk, tensor_count)
        if step == tensor_count - 2 and unit < 3:
            z_start(unit + 1)

    stages = (send_first, stage1, stage2, stage3)

    def run_at(name):
        for stage, chunk in GATHER_PLAN.get(name, ()):
            stages[stage](chunk)

    def run_each(name, index, count):
        for number in range(count):
            if GATHER_PLAN.get(name + str(number)):
                pl.when(index == number)(partial(run_at, name + str(number)))

    def vec_copy(hop):
        if hop < tensor_count - 1:
            source, device = vec_own, (dp, peers[hop])
        else:
            level = hop - (tensor_count - 1)
            source, device = vec_sum.at[level], ((first, second, other)[level], z)
        return pltpu.make_async_remote_copy(
            src_ref=source,
            dst_ref=vec_in.at[hop],
            send_sem=vec_ssem.at[hop],
            recv_sem=vec_rsem.at[hop],
            device_id=device,
            device_id_type=MESH,
        )

    def read_in(index):
        rows = inbuf.shape[1]
        start = pl.multiple_of(index * rows, rows)
        slot = lax.rem(index, 2)
        return pltpu.make_async_copy(
            inp.at[pl.ds(start, rows)], inbuf.at[slot], in_sem.at[slot]
        )

    def keep(source, target, number):
        return pltpu.make_async_copy(source, target, out_sem.at[number])

    width = vectors.shape[1]
    first_col = (dp * tensor_count + z) * width
    row = lax.broadcasted_iota(jnp.int32, (width, D), 0)
    col = lax.broadcasted_iota(jnp.int32, (width, D), 1)
    spot = jnp.where(col == row + first_col, 1.0, 0.0).astype(BF)
    vec_own[...] = jnp.zeros(vec_own.shape, BF)
    vec_own[0 : vectors.shape[0], :] = nn(vectors[...], spot).astype(BF)
    for hop in range(tensor_count - 1):
        vec_copy(hop).start()
    w_cross[place(0, dp, z), :] = cross_shard[...]
    z_start(0)
    read_in(0).start()
    keep(cot, gn3_o, 16).start()
    for unit in range(1, 4):
        weights[unit][place(unit, dp, z), :] = shards[unit][...]
    seg[...] = jnp.full(seg.shape, 2, jnp.int32)
    for row in range(seg_in.shape[0]):
        seg[:, PAD + row * LANES : PAD + (row + 1) * LANES] = seg_in[row : row + 1, :]
    run_at("start")
    run_at("vecz")
    for hop in range(tensor_count - 1):
        vec_copy(hop).wait_recv()
    total = vec_own[...].astype(F32)
    for hop in range(tensor_count - 1):
        total = total + vec_in[hop].astype(F32)
    for level in range(3):
        vec_sum[level] = total.astype(BF)
        hop = tensor_count - 1 + level
        vec_copy(hop).start()
        run_at(("veca", "vecb", "vecc")[level])
        vec_copy(hop).wait_recv()
        total = total + vec_in[hop].astype(F32)
    vec_o[...] = total

    def vec(row):
        return vec_o[row : row + 1, :]

    ctx[0:PAD, :] = jnp.zeros((PAD, D), BF)
    in_rows = inbuf.shape[1]
    reads = inp.shape[0] // in_rows

    def norm_inputs(index, carry):
        @pl.when(index + 1 < reads)
        def _():
            read_in(index + 1).start()

        read_in(index).wait()
        slot = lax.rem(index, 2)

        def rows_of(part, carry2):
            start = pl.multiple_of(part * 64, 64)
            values = inbuf[slot, pl.ds(start, 64), :].astype(F32)
            ctx[pl.ds(pl.multiple_of(PAD + index * in_rows + start, 64), 64), :] = ln_rows(
                values, vec(2), vec(3)
            ).astype(BF)
            return carry2

        lax.fori_loop(0, in_rows // 64, rows_of, 0)

        run_each("ln", index, reads)
        return carry

    lax.fori_loop(0, reads, norm_inputs, 0)
    run_at("post")
    normed = ln_rows(lat[...], vec(0), vec(1)).astype(BF)
    keep(cot, gn3_o, 16).wait()
    gy = gn3_o[...].astype(BF)
    gy_t[...] = gn3_o[...].T.astype(BF)
    run_at("q")
    keep(w_cross, wc_o, 0).start()
    mask = head_mask(GHEADS * LAT)

    query = (nn(normed, w_cross[0:D, :]) + vec(4)).astype(BF)
    scaled = (query.astype(F32) * HEAD_DIM ** (-0.5)).astype(BF)
    query_o[...] = scaled
    for slot in range(2):
        for group in range(GROUPS):
            block = scaled[slot * LAT : (slot + 1) * LAT, group * GROUP : (group + 1) * GROUP]
            qbd[slot * GROUPS + group] = spread_heads(block, mask)

    def project(index, carry):
        rows = pl.ds(pl.multiple_of(index * TILE, TILE), TILE)
        block = ctx[rows, :]
        keys[rows, :] = nn(block, w_cross[D : 2 * D, :]).astype(BF)
        vals[rows, :] = (nn(block, w_cross[2 * D : 3 * D, :]) + vec(5)).astype(BF)

        run_each("kv", index, tiles)
        return carry

    lax.fori_loop(0, tiles, project, 0)
    keep(ctx, ctx_o, 1).start()
    keep(keys, key_o, 2).start()
    keep(vals, val_o, 3).start()

    wide = 3 * TILE
    whole = tiles // 3
    rest = [
        (0, slice(whole * wide, tiles * TILE), slice(whole * wide, tiles * TILE)),
        (
            1,
            slice(SLOT1_FIRST * TILE, (SLOT1_FIRST + SLOT1_TILES) * TILE),
            slice(tiles * TILE, (tiles + SLOT1_TILES) * TILE),
        ),
    ]

    def wide_cols(index):
        return pl.ds(pl.multiple_of(index * wide, wide), wide)

    def fold(values, op):
        parts = [values[:, at : at + LANES] for at in range(0, values.shape[1], LANES)]
        while len(parts) > 1:
            parts = [
                op(parts[at], parts[at + 1]) if at + 1 < len(parts) else parts[at]
                for at in range(0, len(parts), 2)
            ]
        return parts[0]

    seen = []
    for slot in range(2):
        hit = jnp.where(seg[...] == slot, 1.0, 0.0)
        seen.append(jnp.max(hit, axis=1, keepdims=True))

    for group in range(GROUPS):
        gcols = slice(group * GROUP, (group + 1) * GROUP)
        peak[...] = jnp.full(peak.shape, HIDE, F32)
        denom[...] = jnp.zeros(denom.shape, F32)
        oacc[...] = jnp.zeros(oacc.shape, F32)

        def score_part(slot, rows, cols):
            values = nt(qbd[slot * GROUPS + group], keys[rows, gcols])
            values = jnp.where(seg[:, rows] == slot, values, HIDE)
            scores[:, cols] = values
            peak[slot] = jnp.maximum(peak[slot], fold(values, jnp.maximum))

        def score(index, carry):
            score_part(0, wide_cols(index), wide_cols(index))
            return carry

        run_at("s%d" % group)
        lax.fori_loop(0, whole, score, 0)
        for slot, rows, cols in rest:
            score_part(slot, rows, cols)
        for slot in range(2):
            top = jnp.max(peak[slot], axis=1, keepdims=True)
            top = jnp.where(seen[slot] > 0.0, top, 0.0)
            peak[slot] = jnp.broadcast_to(top, (GHEADS * LAT, LANES))
        if group:
            keep(probs, prob_o.at[group - 1], 4).wait()

        def spread_part(slot, rows, cols):
            for head in range(GHEADS):
                part = slice(head * LAT, (head + 1) * LAT)
                values = scores[part, cols]
                count = values.shape[1] // LANES
                top = jnp.concatenate([peak[slot, part, :]] * count, axis=1)
                values = jnp.exp(values - top)
                probs[part, cols] = values.astype(BF)
                denom[slot, part, :] += fold(values, jnp.add)
            oacc[slot] += nn(probs[:, cols], vals[rows, gcols])

        def spread(index, carry):
            run_each("p%d_" % group, index, whole)
            spread_part(0, wide_cols(index), wide_cols(index))
            return carry

        lax.fori_loop(0, whole, spread, 0)
        for slot, rows, cols in rest:
            spread_part(slot, rows, cols)
        keep(probs, prob_o.at[group], 4).start()
        run_at("t%d" % group)
        for slot in range(2):
            total = jnp.sum(denom[slot], axis=1, keepdims=True) + 1.0 - seen[slot]
            scale = 1.0 / total
            across = jnp.broadcast_to(scale, (GHEADS * LAT, LANES)).T
            at = slot * GROUPS + group
            inv_o[at : at + 1, :] = across[0:1, :]
            read[slot * LAT : (slot + 1) * LAT, gcols] = pick_heads(oacc[slot] * scale)

    run_at("mid")
    mid = lat[...] + (nn(read[...].astype(BF), w_cross[3 * D :, :]) + vec(6))
    mid_o[...] = mid
    normed_two = ln_rows(mid, vec(7), vec(8)).astype(BF)
    run_at("self0")
    keep(w_self, ws_o, 5).start()
    query_two = (nn(normed_two, w_self[0:D, :]) + vec(9)).astype(BF)
    query2_o[...] = (query_two.astype(F32) * HEAD_DIM ** (-0.5)).astype(BF)
    key2_o[...] = nn(normed_two, w_self[D : 2 * D, :]).astype(BF)
    val2_o[...] = (nn(normed_two, w_self[2 * D : 3 * D, :]) + vec(10)).astype(BF)
    run_at("self1")
    for slot in range(2):
        srows = slice(slot * LAT, (slot + 1) * LAT)
        for group in range(GROUPS):
            gcols = slice(group * GROUP, (group + 1) * GROUP)
            wide = spread_heads(query2_o[srows, gcols], mask)
            values = nt(wide, key2_o[srows, gcols])
            values = jnp.exp(values - jnp.max(values, axis=1, keepdims=True))
            values = values / jnp.sum(values, axis=1, keepdims=True)
            values = values.astype(BF)
            prob2_o[slot, group] = values
            read2_o[srows, gcols] = pick_heads(nn(values, val2_o[srows, gcols]))
    late = mid_o[...] + (nn(read2_o[...].astype(BF), w_self[3 * D :, :]) + vec(11))
    late_o[...] = late
    normed_three = ln_rows(late, vec(12), vec(13))
    norm_t[...] = normed_three.T.astype(BF)
    normed_three = normed_three.astype(BF)
    keep(probs, prob_o.at[GROUPS - 1], 4).wait()
    keep(keys, key_o, 2).wait()
    keep(vals, val_o, 3).wait()

    small = [
        (query_o, query_h),
        (read, read_h),
        (mid_o, mid_h),
        (query2_o, query2_h),
        (key2_o, key2_h),
        (val2_o, val2_h),
        (prob2_o, prob2_h),
        (read2_o, read2_h),
        (late_o, late_h),
    ]
    for number, (source, target) in enumerate(small):
        keep(source, target, 17 + number).start()

    rows_all = slice(0, 2 * LAT)

    def quarter(step):
        part = lax.rem(z - step + tensor_count, tensor_count)
        return part, pl.ds(pl.multiple_of(part * D, D), D)

    def up_part(step):
        part, rows = quarter(step)
        cols = slice(step * D, (step + 1) * D)
        pre = nn(normed_three, w_up[rows, :]) + vec_o[pl.ds(15 + part, 1), :]
        half = 0.5 * (1.0 + lax.erf(pre * 0.5**0.5))
        slope = half + pre * jnp.exp(-0.5 * pre * pre) * 0.3989422804014327
        hidden = (pre * half).astype(BF)
        probs[rows_all, cols] = hidden
        scores[rows_all, cols] = slope
        vals[rows, :] = nn(gy_t[...], hidden).astype(BF)
        keep(vals.at[rows], gdn_o.at[rows], 6 + step).start()

    def down_part(step):
        part, rows = quarter(step)
        cols = slice(step * D, (step + 1) * D)
        down = w_down[rows, :]
        y_part = nt(probs[rows_all, cols], down)
        grad_pre = (scores[rows_all, cols] * nn(gy, down)).astype(BF)
        keys[rows, :] = nn(norm_t[...], grad_pre).astype(BF)
        keep(keys.at[rows], gup_o.at[rows], 6 + tensor_count + step).start()
        x_part = nt(grad_pre, w_up[rows, :])
        if step == 0:
            out_o[...] = late_o[...] + vec(14) + y_part
            gn3_o[...] = x_part
        else:
            out_o[...] += y_part
            gn3_o[...] += x_part
        gb1_o[pl.ds(part, 1), :] = jnp.sum(grad_pre.astype(F32), axis=0, keepdims=True)

    gb1_o[...] = jnp.zeros(gb1_o.shape, F32)
    for step in range(tensor_count):
        run_at("up%d" % step)
        up_part(step)
    for step in range(tensor_count):
        run_at("down%d" % step)
        down_part(step)
    for number, (source, target) in enumerate(small):
        keep(source, target, 17 + number).wait()
    keep(w_cross, wc_o, 0).wait()
    keep(ctx, ctx_o, 1).wait()
    keep(w_self, ws_o, 5).wait()
    for step in range(tensor_count):
        part, rows = quarter(step)
        keep(vals.at[rows], gdn_o.at[rows], 6 + step).wait()
        keep(keys.at[rows], gup_o.at[rows], 6 + tensor_count + step).wait()
    for hop in range(tensor_count + 2):
        vec_copy(hop).wait_send()
    for unit in range(4):
        for step in range(1, tensor_count):
            z_copy(unit, step).wait_send()
    for chunk in range(chunk_count):
        for kind in range(kinds):
            plane_copy(chunk, kind).wait_send()


def forward_call(tensor_count, lat, inp, seg, cross_w, self_w, up_w, down_w, vectors, cot):
    rows = lat.shape[0]
    tokens = inp.shape[0] + PAD
    virtual = (tokens // TILE + SLOT1_TILES) * TILE
    sds = jax.ShapeDtypeStruct
    hbm = pl.BlockSpec(memory_space=pl.ANY)
    vmem = pl.BlockSpec(memory_space=pltpu.VMEM)
    stacked = GHEADS * LAT
    copies = 4 * tensor_count * 7 + 4 * (tensor_count - 1)
    outs = [
        (sds((rows, D), F32), vmem),
        (sds((NROWS, D), BF), hbm),
        (sds((NROWS, D), BF), hbm),
        (sds((tokens, D), BF), hbm),
        (sds((tokens, D), BF), hbm),
        (sds((tokens, D), BF), hbm),
        (sds((GROUPS, stacked, virtual), BF), hbm),
        (sds((NROWS, D), BF), hbm),
        (sds((NROWS, D), BF), hbm),
        (sds((VEC_PAD, D), F32), vmem),
        (sds((rows, D), BF), hbm),
        (sds((rows, D), F32), hbm),
        (sds((rows, D), F32), hbm),
        (sds((rows, D), BF), hbm),
        (sds((rows, D), BF), hbm),
        (sds((rows, D), BF), hbm),
        (sds((2, GROUPS, stacked, LAT), BF), hbm),
        (sds((rows, D), F32), hbm),
        (sds((rows, D), F32), hbm),
        (sds((rows, D), F32), vmem),
        (sds((8, D), F32), vmem),
        (sds((8, stacked), F32), vmem),
    ]
    return pl.pallas_call(
        partial(forward_kernel, tensor_count),
        out_shape=[shape for shape, spec in outs],
        out_specs=[spec for shape, spec in outs],
        in_specs=[vmem, hbm] + [vmem] * 6 + [hbm],
        scratch_shapes=[
            pltpu.VMEM((rows, D), BF),
            pltpu.VMEM((rows, D), F32),
            pltpu.VMEM((rows, D), F32),
            pltpu.VMEM((rows, D), BF),
            pltpu.VMEM((rows, D), BF),
            pltpu.VMEM((rows, D), BF),
            pltpu.VMEM((2, GROUPS, stacked, LAT), BF),
            pltpu.VMEM((rows, D), F32),
            pltpu.VMEM((rows, D), F32),
            pltpu.VMEM((1, tokens), jnp.int32),
            pltpu.VMEM((VEC_PAD, D), BF),
            pltpu.VMEM((NROWS, D), BF),
            pltpu.VMEM((NROWS, D), BF),
            pltpu.VMEM((NROWS, D), BF),
            pltpu.VMEM((NROWS, D), BF),
            pltpu.VMEM((tokens, D), BF),
            pltpu.VMEM((tokens, D), BF),
            pltpu.VMEM((tokens, D), BF),
            pltpu.VMEM((stacked, virtual), F32),
            pltpu.VMEM((stacked, virtual), BF),
            pltpu.VMEM((2, 320, D), BF),
            pltpu.VMEM((2 * GROUPS, stacked, GROUP), BF),
            pltpu.VMEM((2, stacked, LANES), F32),
            pltpu.VMEM((2, stacked, LANES), F32),
            pltpu.VMEM((2, stacked, GROUP), F32),
            pltpu.VMEM((D, rows), BF),
            pltpu.VMEM((D, rows), BF),
            pltpu.VMEM((tensor_count + 2, VEC_PAD, D), BF),
            pltpu.VMEM((3, VEC_PAD, D), BF),
            pltpu.SemaphoreType.DMA((copies,)),
            pltpu.SemaphoreType.DMA((copies,)),
            pltpu.SemaphoreType.DMA((tensor_count + 2,)),
            pltpu.SemaphoreType.DMA((tensor_count + 2,)),
            pltpu.SemaphoreType.DMA((2,)),
            pltpu.SemaphoreType.DMA((26,)),
        ],
        compiler_params=pltpu.CompilerParams(
            collective_id=0, has_side_effects=True, vmem_limit_bytes=VMEM_LIMIT
        ),
        name="gather_forward",
    )(lat, inp, seg, cross_w, self_w, up_w, down_w, vectors, cot)


def tn(left, right):
    return lax.dot_general(
        left, right, (((0,), (0,)), ((), ())), preferred_element_type=F32
    )


def ln_back(values, gain_row, incoming):
    unit, scale = ln_parts(values)
    scaled = incoming * gain_row
    inner = jnp.mean(scaled * unit, axis=-1, keepdims=True)
    outgoing = scale * (scaled - jnp.mean(scaled, axis=-1, keepdims=True) - unit * inner)
    gain = jnp.sum(incoming * unit, axis=0, keepdims=True)
    return outgoing, gain, jnp.sum(incoming, axis=0, keepdims=True)


def backward_kernel(
    tensor_count,
    lat_h,
    cot_h,
    mid_h,
    late_h,
    gn3_h,
    read_h,
    read2_h,
    query_h,
    query2_h,
    key2_h,
    val2_h,
    prob2_h,
    vecs,
    gb1,
    inv,
    wc_h,
    ws_h,
    ctx_h,
    key_h,
    val_h,
    prob_h,
    gup_h,
    gdn_h,
    inp,
    glat_o,
    ginp_o,
    gcross_o,
    gself_o,
    gvec_o,
    gup_o,
    gdn_o,
    dkv_h,
    w_cross,
    g_mlp,
    g_sc,
    rc,
    rb,
    ra,
    rz,
    dwk,
    dwv,
    kt,
    vt,
    ct,
    it,
    pt,
    p1,
    ot,
    dkv,
    gbd,
    gbd_t,
    qbd_t,
    row_r,
    dqacc,
    gread,
    dq2,
    dk2,
    dv2,
    gbias,
    gvec,
    vec_in,
    vec_sum,
    c_ssem,
    c_rsem,
    b_ssem,
    b_rsem,
    a_ssem,
    a_rsem,
    z_ssem,
    z_rsem,
    v_ssem,
    v_rsem,
    tile_sem,
    load_sem,
    credit,
):
    dp, z, core, other, first, second, both, peers = neighbours(tensor_count)
    meet(dp, z, other, first, second, peers)
    shard = gcross_o.shape[0]
    quad = 4 * shard
    yy = dp // 4
    xx = lax.rem(dp // 2, 2)
    tiles = ctx_h.shape[0] // TILE
    chunk_count = 4 * tensor_count
    w_self_at = NROWS

    def mult(value, by):
        return pl.multiple_of(value, by)

    def chunk_part(chunk):
        return lax.rem(z + 1 + chunk % tensor_count, tensor_count)

    def own_ref(chunk):
        unit, part = chunk // tensor_count, chunk_part(chunk)
        if unit < 2:
            return g_mlp, (unit * tensor_count + part) * quad
        return g_sc, (((unit - 2) * 2 + core) * tensor_count + part) * quad

    def rows_at(start, count):
        return pl.ds(mult(start, shard), count)

    def remote(source, target, send, recv, device):
        return pltpu.make_async_remote_copy(
            src_ref=source,
            dst_ref=target,
            send_sem=send,
            recv_sem=recv,
            device_id=device,
            device_id_type=MESH,
        )

    def c_slot(chunk):
        return rc.at[chunk % 8]

    def c_whole(chunk):
        return remote(
            c_slot(chunk), c_slot(chunk), c_ssem.at[chunk], c_rsem.at[chunk], (other, z)
        )

    def c_start(chunk):
        unit, part = chunk // tensor_count, chunk_part(chunk)
        if unit < 2:
            source = (gdn_h, gup_h)[unit]
            for q in range(4):
                start = part * D + (2 * q + 1 - core) * shard
                remote(
                    source.at[rows_at(start, shard)],
                    c_slot(chunk).at[pl.ds(q * shard, shard)],
                    c_ssem.at[chunk],
                    c_rsem.at[chunk],
                    (other, z),
                ).start()
        else:
            start = (((unit - 2) * 2 + 1 - core) * tensor_count + part) * quad
            remote(
                g_sc.at[rows_at(start, quad)],
                c_slot(chunk),
                c_ssem.at[chunk],
                c_rsem.at[chunk],
                (other, z),
            ).start()

    def b_copy(chunk, half):
        ref, base = own_ref(chunk)
        q = (1 - core) * ((1 - yy) * 2 + half) + core * (half * 2 + 1 - xx)
        number = chunk * 2 + half
        return remote(
            ref.at[rows_at(base + q * shard, shard)],
            rb.at[chunk, half],
            b_ssem.at[number],
            b_rsem.at[number],
            (second, z),
        )

    def a_copy(chunk):
        ref, base = own_ref(chunk)
        q = (1 - core) * (yy * 2 + 1 - xx) + core * ((1 - yy) * 2 + xx)
        return remote(
            ref.at[rows_at(base + q * shard, shard)],
            ra.at[chunk],
            a_ssem.at[chunk],
            a_rsem.at[chunk],
            (first, z),
        )

    def z_copy(chunk):
        unit, step = divmod(chunk, tensor_count)
        ref, base = own_ref(chunk)
        number = unit * (tensor_count - 1) + step
        return remote(
            ref.at[rows_at(base + (yy * 2 + xx) * shard, shard)],
            rz.at[number],
            z_ssem.at[number],
            z_rsem.at[number],
            (dp, peers[step]),
        )

    piece = 32

    def add_rows(ref, start, source, count):
        def body(index, carry):
            rows = pl.ds(mult(start + index * piece, piece), piece)
            part = source[pl.ds(mult(index * piece, piece), piece), :]
            ref[rows, :] = (ref[rows, :].astype(F32) + part.astype(F32)).astype(BF)
            return carry

        lax.fori_loop(0, count // piece, body, 0)

    def stage1(chunk):
        c_whole(chunk).wait_recv()
        ref, base = own_ref(chunk)
        add_rows(ref, base, c_slot(chunk), quad)
        if chunk in (3, 7):
            pl.semaphore_signal(
                credit, inc=1, device_id=(other, z), device_id_type=MESH
            )
        for half in range(2):
            b_copy(chunk, half).start()

    def stage2(chunk):
        ref, base = own_ref(chunk)
        for half in range(2):
            b_copy(chunk, half).wait_recv()
            q = (1 - core) * (yy * 2 + half) + core * (half * 2 + xx)
            add_rows(ref, base + q * shard, rb.at[chunk, half], shard)
        a_copy(chunk).start()

    def stage3(chunk):
        a_copy(chunk).wait_recv()
        ref, base = own_ref(chunk)
        add_rows(ref, base + (yy * 2 + xx) * shard, ra.at[chunk], shard)
        if chunk % tensor_count < tensor_count - 1:
            z_copy(chunk).start()

    def finish(unit):
        chunk = unit * tensor_count + tensor_count - 1
        ref, base = own_ref(chunk)
        target = (gdn_o, gup_o, gself_o, gcross_o)[unit]
        for step in range(tensor_count - 1):
            z_copy(unit * tensor_count + step).wait_recv()

        def body(index, carry):
            rows = pl.ds(mult(index * piece, piece), piece)
            start = base + (yy * 2 + xx) * shard + index * piece
            total = ref[pl.ds(mult(start, piece), piece), :].astype(F32)
            for step in range(tensor_count - 1):
                total = total + rz[unit * (tensor_count - 1) + step, rows, :].astype(F32)
            target[rows, :] = total
            return carry

        lax.fori_loop(0, shard // piece, body, 0)

    stages = (stage1, stage2, stage3, finish)

    def run_at(name):
        for stage, chunk in SCATTER_PLAN.get(name, ()):
            stages[stage](chunk)

    def run_each(name, index, count):
        for number in range(count):
            if SCATTER_PLAN.get(name + str(number)):
                pl.when(index == number)(partial(run_at, name + str(number)))

    def send_unit(unit):
        pl.semaphore_wait(credit, 1)
        for chunk in range(unit * tensor_count, (unit + 1) * tensor_count):
            c_start(chunk)

    def store_grad(unit, block, values):
        for part in range(8):
            parity, zpart = divmod(part, tensor_count)
            start = (((unit * 2 + parity) * tensor_count + zpart) * 4 + block) * shard
            g_sc[start : start + shard, :] = values[part * shard : (part + 1) * shard].astype(BF)

    def load(source, target, number):
        return pltpu.make_async_copy(source, target, load_sem.at[number])

    w_self = g_sc.at[pl.ds(w_self_at, NROWS)]
    for chunk in range(2 * tensor_count):
        c_start(chunk)
    for unit in range(2):
        source = (gdn_h, gup_h)[unit]
        for part in range(tensor_count):
            for q in range(4):
                pltpu.make_async_copy(
                    source.at[rows_at(part * D + (2 * q + core) * shard, shard)],
                    g_mlp.at[pl.ds(((unit * tensor_count + part) * 4 + q) * shard, shard)],
                    load_sem.at[1 + unit],
                ).start()
    lat_rows = 2 * LAT
    late, gn3, read2 = (dwk.at[pl.ds(third * lat_rows, lat_rows)] for third in range(3))
    read, mid, lat = (dwv.at[pl.ds(third * lat_rows, lat_rows)] for third in range(3))
    prob2 = pt.at[:, :, :, pl.ds(0, LAT)]
    early = [
        (cot_h, glat_o),
        (late_h, late),
        (gn3_h, gn3),
        (read2_h, read2),
        (read_h, read),
        (mid_h, mid),
        (prob2_h, prob2),
        (query2_h, kt.at[0]),
        (key2_h, kt.at[1]),
        (val2_h, vt.at[0]),
        (query_h, vt.at[1]),
    ]
    query2, key2, val2, query = kt.at[0], kt.at[1], vt.at[0], vt.at[1]
    for number, (source, target) in enumerate(early):
        load(source, target, 5 + number).start()
    load(ws_h, w_self, 0).start()
    load(wc_h, w_cross, 3).start()

    def load_p1(extra):
        return load(prob_h.at[:, :, pl.ds((tiles + extra) * TILE, TILE)], p1, 4)

    load_p1(0).start()
    half_mlp = tensor_count * quad
    for unit in range(2):
        whole = g_mlp.at[pl.ds(unit * half_mlp, half_mlp)]
        load(whole, whole, 1 + unit).wait()

    def vec(row):
        return vecs[row : row + 1, :]

    mask = head_mask(GHEADS * LAT)
    gvec[...] = jnp.zeros(gvec.shape, F32)

    def note(row, values):
        gvec[row : row + 1, :] = values

    def col_sum(values):
        return jnp.sum(values.astype(F32), axis=0, keepdims=True)

    def row_terms(grad_block, read_block):
        wide = jnp.concatenate([grad_block.astype(F32) * read_block] * GHEADS, axis=0)
        return jnp.sum(jnp.where(mask, wide, 0.0), axis=1, keepdims=True)

    run_at("a")
    for number, (source, target) in enumerate(early):
        load(source, target, 5 + number).wait()
    note(14, col_sum(glat_o[...].astype(BF)))
    gvec[15 : 15 + tensor_count, :] = gb1[0:tensor_count, :]
    back, gain, shift = ln_back(late[...], vec(12), gn3[...])
    note(12, gain)
    note(13, shift)
    gas = glat_o[...] + back
    glat_o[...] = gas
    grad_out = gas.astype(BF)
    note(11, col_sum(grad_out))
    load(ws_h, w_self, 0).wait()

    def self_block(block):
        return g_sc[w_self_at + block * D : w_self_at + (block + 1) * D, :]

    run_at("b")
    store_grad(0, 3, nn(read2[...].T.astype(BF), grad_out))
    gread[...] = nt(grad_out, self_block(3)).astype(BF)
    run_at("c")
    for slot in range(2):
        srows = slice(slot * LAT, (slot + 1) * LAT)
        for group in range(GROUPS):
            gcols = slice(group * GROUP, (group + 1) * GROUP)
            grads = spread_heads(gread[srows, gcols], mask)
            inner = row_terms(gread[srows, gcols], read2[srows, gcols])
            chance = prob2[slot, group]
            dprob = nt(grads, val2[srows, gcols])
            dscore = (chance.astype(F32) * (dprob - inner)).astype(BF)
            dq2[srows, gcols] = (
                pick_heads(nn(dscore, key2[srows, gcols])) * HEAD_DIM ** (-0.5)
            ).astype(BF)
            wide = spread_heads(query2[srows, gcols], mask)
            dk2[srows, gcols] = tn(dscore, wide).astype(BF)
            dv2[srows, gcols] = tn(chance, grads).astype(BF)
    run_at("d")
    note(9, col_sum(dq2[...]))
    note(10, col_sum(dv2[...]))
    unit_two, scale_two = ln_parts(mid[...])
    norm_t = (unit_two * vec(7) + vec(8)).T.astype(BF)
    store_grad(0, 0, nn(norm_t, dq2[...]))
    store_grad(0, 1, nn(norm_t, dk2[...]))
    store_grad(0, 2, nn(norm_t, dv2[...]))
    incoming = nt(dq2[...], self_block(0)) + nt(dk2[...], self_block(1))
    incoming = incoming + nt(dv2[...], self_block(2))
    back, gain, shift = ln_back(mid[...], vec(7), incoming)
    note(7, gain)
    note(8, shift)
    total = glat_o[...] + back
    glat_o[...] = total
    run_at("CS2")
    send_unit(2)
    run_at("e")
    grad_out = total.astype(BF)
    note(6, col_sum(grad_out))
    load(wc_h, w_cross, 3).wait()
    store_grad(1, 3, nn(read[...].T.astype(BF), grad_out))
    gread[...] = nt(grad_out, w_cross[3 * D :, :]).astype(BF)
    run_at("f")
    for slot in range(2):
        srows = slice(slot * LAT, (slot + 1) * LAT)
        for group in range(GROUPS):
            gcols = slice(group * GROUP, (group + 1) * GROUP)
            at = slot * GROUPS + group
            grads = jnp.concatenate([gread[srows, gcols].astype(F32)] * GHEADS, axis=0)
            grads = jnp.where(mask, grads, 0.0).T * inv[at : at + 1, :]
            gbd_t[at] = grads.astype(BF)
            grads = grads.T
            gbd[at] = grads.astype(BF)
            wide = jnp.concatenate([query[srows, gcols].astype(F32)] * GHEADS, axis=0)
            qbd_t[at] = jnp.where(mask, wide, 0.0).T.astype(BF)
            wide = jnp.concatenate([read[srows, gcols]] * GHEADS, axis=0)
            inner = jnp.sum(grads * wide, axis=1, keepdims=True)
            row_r[at] = jnp.broadcast_to(inner, (GHEADS * LAT, LANES))
    dqacc[...] = jnp.zeros(dqacc.shape, F32)
    dwk[...] = jnp.zeros(dwk.shape, F32)
    dwv[...] = jnp.zeros(dwv.shape, F32)
    gbias[...] = jnp.zeros(gbias.shape, F32)
    it[0] = jnp.zeros(it.shape[1:], BF)

    def fetches(index):
        slot = lax.rem(index, 2)
        rows = pl.ds(mult(index * TILE, TILE), TILE)
        copies = [
            (key_h.at[rows], kt.at[slot]),
            (val_h.at[rows], vt.at[slot]),
            (ctx_h.at[rows], ct.at[slot]),
            (prob_h.at[:, :, rows], pt.at[slot]),
        ]
        return [
            pltpu.make_async_copy(source, target, tile_sem.at[slot, number])
            for number, (source, target) in enumerate(copies)
        ]

    def spill(index):
        slot = lax.rem(index, 2)
        return pltpu.make_async_copy(dkv.at[slot], dkv_h.at[index], tile_sem.at[slot, 4])

    for copy in fetches(jnp.int32(0)):
        copy.start()

    def attend_back(slot, chance_of, buffer, first_time):
        for group in range(GROUPS):
            gcols = slice(group * GROUP, (group + 1) * GROUP)
            at = slot * GROUPS + group
            chance = chance_of(group)
            dprob = nt(gbd[at], vt[buffer, :, gcols])
            inner = row_r[at]
            dscore = chance.astype(F32) * (dprob - jnp.concatenate([inner, inner], axis=1))
            dscore = dscore.astype(BF)
            dk_part = nn(qbd_t[at], dscore)
            dv_part = nn(gbd_t[at], chance)
            if not first_time:
                dk_part = dk_part + dkv[buffer, 0, gcols, :].astype(F32)
                dv_part = dv_part + dkv[buffer, 1, gcols, :].astype(F32)
            dkv[buffer, 0, gcols, :] = dk_part.astype(BF)
            dkv[buffer, 1, gcols, :] = dv_part.astype(BF)
            dqacc[at] += nn(dscore, kt[buffer, :, gcols])

    def tile_body(index, carry):
        buffer = lax.rem(index, 2)

        @pl.when(index + 1 < tiles)
        def _():
            for copy in fetches(index + 1):
                copy.start()

        run_each("t", index, tiles)

        @pl.when(index > 1)
        def _():
            spill(index - 2).wait()

        for copy in fetches(index):
            copy.wait()
        attend_back(0, lambda group: pt[buffer, group], buffer, True)
        for extra in range(SLOT1_TILES):

            @pl.when(index == SLOT1_FIRST + extra)
            def _():
                load_p1(extra).wait()
                attend_back(1, lambda group: p1[group], buffer, False)
                if extra + 1 < SLOT1_TILES:
                    load_p1(extra + 1).start()

        spill(index).start()
        dk = dkv[buffer, 0]
        dv = dkv[buffer, 1]
        gbias[...] += dv[:, :LANES].astype(F32) + dv[:, LANES:].astype(F32)
        block = ct[buffer]
        dwk[...] += nn(dk, block)
        dwv[...] += nn(dv, block)

        return carry

    lax.fori_loop(0, tiles, tile_body, 0)
    run_at("g")
    store_grad(1, 2, dwv[...].T)
    load(lat_h, lat, 16).start()
    store_grad(1, 1, dwk[...].T)
    for slot in range(2):
        srows = slice(slot * LAT, (slot + 1) * LAT)
        for group in range(GROUPS):
            gcols = slice(group * GROUP, (group + 1) * GROUP)
            dq2[srows, gcols] = (
                pick_heads(dqacc[slot * GROUPS + group]) * HEAD_DIM ** (-0.5)
            ).astype(BF)
    load(lat_h, lat, 16).wait()
    unit_one, scale_one = ln_parts(lat[...])
    norm_t = (unit_one * vec(0) + vec(1)).T.astype(BF)
    store_grad(1, 0, nn(norm_t, dq2[...]))
    run_at("CS3")
    send_unit(3)
    spill(tiles - 2).wait()
    spill(tiles - 1).wait()

    def fetch_back(index, at_start):
        slot = 0 if at_start else lax.rem(index, 2)
        back_rows = inp.at[pl.ds(0, TILE - PAD)]
        target = it.at[0, pl.ds(PAD, TILE - PAD)]
        if not at_start:
            back_rows = inp.at[pl.ds(mult(index * TILE - PAD, PAD), TILE)]
            target = it.at[slot]
        tile = 0 if at_start else index
        return [
            pltpu.make_async_copy(back_rows, target, tile_sem.at[slot, 0]),
            pltpu.make_async_copy(dkv_h.at[tile], dkv.at[slot], tile_sem.at[slot, 1]),
        ]

    def put(index, at_start):
        slot = 0 if at_start else lax.rem(index, 2)
        if at_start:
            source, rows = ot.at[0, pl.ds(PAD, TILE - PAD)], pl.ds(0, TILE - PAD)
        else:
            source, rows = ot.at[slot], pl.ds(mult(index * TILE - PAD, PAD), TILE)
        return pltpu.make_async_copy(source, ginp_o.at[rows], tile_sem.at[slot, 5])

    for copy in fetch_back(0, True):
        copy.start()

    def token_body(index, carry):
        buffer = lax.rem(index, 2)

        @pl.when(index + 1 < tiles)
        def _():
            for copy in fetch_back(index + 1, False):
                copy.start()

        @pl.when(index == 0)
        def _():
            for copy in fetch_back(0, True):
                copy.wait()

        @pl.when(index > 0)
        def _():
            for copy in fetch_back(index, False):
                copy.wait()

        run_each("u", index, tiles)
        incoming = nn(w_cross[D : 2 * D, :], dkv[buffer, 0])
        incoming = incoming + nn(w_cross[2 * D : 3 * D, :], dkv[buffer, 1])
        back, gain, shift = ln_back(it[buffer].astype(F32), vec(2), incoming.T)
        gvec[2:3, :] += gain
        gvec[3:4, :] += shift

        @pl.when(index == 2)
        def _():
            put(0, True).wait()

        @pl.when(index > 2)
        def _():
            put(index - 2, False).wait()

        ot[buffer] = back.astype(BF)

        @pl.when(index == 0)
        def _():
            put(0, True).start()

        @pl.when(index > 0)
        def _():
            put(index, False).start()

        return carry

    lax.fori_loop(0, tiles, token_body, 0)
    run_at("h")
    note(4, col_sum(dq2[...]))
    note(5, jnp.sum(gbias[...].T, axis=0, keepdims=True))
    incoming = nt(dq2[...], w_cross[0:D, :])
    back, gain, shift = ln_back(lat[...], vec(0), incoming)
    note(0, gain)
    note(1, shift)
    glat_o[...] = glat_o[...] + back

    def vec_copy(hop):
        if hop < 3:
            source, device = vec_sum.at[hop], ((other, second, first)[hop], z)
        else:
            source, device = vec_sum.at[3], (dp, peers[hop - 3])
        return remote(source, vec_in.at[hop], v_ssem.at[hop], v_rsem.at[hop], device)

    total = gvec[...]
    for hop in range(3):
        vec_sum[hop] = total
        vec_copy(hop).start()
        run_at("v%d" % hop)
        vec_copy(hop).wait_recv()
        total = total + vec_in[hop]
    vec_sum[3] = total
    for hop in range(3, 2 + tensor_count):
        vec_copy(hop).start()
    run_at("v3")
    run_at("end")
    for hop in range(3, 2 + tensor_count):
        vec_copy(hop).wait_recv()
        total = total + vec_in[hop]
    width = gvec_o.shape[1]
    turn = lax.rem(D - (dp * tensor_count + z) * width, D)
    gvec_o[...] = pltpu.roll(total, turn, 1)[0 : gvec_o.shape[0], 0:width]
    put(tiles - 2, False).wait()
    put(tiles - 1, False).wait()
    for hop in range(2 + tensor_count):
        vec_copy(hop).wait_send()
    for chunk in range(chunk_count):
        c_whole(chunk).wait_send()
        b_copy(chunk, 0).wait_send()
        b_copy(chunk, 1).wait_send()
        a_copy(chunk).wait_send()
        if chunk % tensor_count < tensor_count - 1:
            z_copy(chunk).wait_send()


def backward_call(tensor_count, shard, vec_shape, operands):
    sds = jax.ShapeDtypeStruct
    hbm = pl.BlockSpec(memory_space=pl.ANY)
    vmem = pl.BlockSpec(memory_space=pltpu.VMEM)
    rows = operands[0].shape[0]
    inp = operands[-1]
    stacked = GHEADS * LAT
    chunks = 4 * tensor_count
    zs = 4 * (tensor_count - 1)
    at = 2 * GROUPS
    sem = pltpu.SemaphoreType.DMA
    outs = [
        (sds((rows, D), F32), vmem),
        (sds(inp.shape, BF), hbm),
        (sds((shard, D), F32), vmem),
        (sds((shard, D), F32), vmem),
        (sds(vec_shape, F32), vmem),
        (sds((shard, D), F32), vmem),
        (sds((shard, D), F32), vmem),
        (sds(((inp.shape[0] + PAD) // TILE, 2, D, TILE), BF), hbm),
    ]
    return pl.pallas_call(
        partial(backward_kernel, tensor_count),
        out_shape=[shape for shape, spec in outs],
        out_specs=[spec for shape, spec in outs],
        in_specs=[hbm] * 12 + [vmem] * 3 + [hbm] * 9,
        scratch_shapes=[
            pltpu.VMEM((NROWS, D), BF),
            pltpu.VMEM((NROWS, D), BF),
            pltpu.VMEM((2 * NROWS, D), BF),
            pltpu.VMEM((8, 4 * shard, D), BF),
            pltpu.VMEM((chunks, 2, shard, D), BF),
            pltpu.VMEM((chunks, shard, D), BF),
            pltpu.VMEM((zs, shard, D), BF),
            pltpu.VMEM((D, D), F32),
            pltpu.VMEM((D, D), F32),
            pltpu.VMEM((2, TILE, D), BF),
            pltpu.VMEM((2, TILE, D), BF),
            pltpu.VMEM((2, TILE, D), BF),
            pltpu.VMEM((2, TILE, D), BF),
            pltpu.VMEM((2, GROUPS, stacked, TILE), BF),
            pltpu.VMEM((GROUPS, stacked, TILE), BF),
            pltpu.VMEM((2, TILE, D), BF),
            pltpu.VMEM((2, 2, D, TILE), BF),
            pltpu.VMEM((at, stacked, GROUP), BF),
            pltpu.VMEM((at, GROUP, stacked), BF),
            pltpu.VMEM((at, GROUP, stacked), BF),
            pltpu.VMEM((at, stacked, LANES), F32),
            pltpu.VMEM((at, stacked, GROUP), F32),
            pltpu.VMEM((rows, D), BF),
            pltpu.VMEM((rows, D), BF),
            pltpu.VMEM((rows, D), BF),
            pltpu.VMEM((rows, D), BF),
            pltpu.VMEM((D, LANES), F32),
            pltpu.VMEM((VEC_PAD, D), F32),
            pltpu.VMEM((2 + tensor_count, VEC_PAD, D), F32),
            pltpu.VMEM((4, VEC_PAD, D), F32),
            sem((chunks,)),
            sem((chunks,)),
            sem((2 * chunks,)),
            sem((2 * chunks,)),
            sem((chunks,)),
            sem((chunks,)),
            sem((zs,)),
            sem((zs,)),
            sem((2 + tensor_count,)),
            sem((2 + tensor_count,)),
            sem((2, 6)),
            sem((17,)),
            pltpu.SemaphoreType.REGULAR,
        ],
        compiler_params=pltpu.CompilerParams(
            collective_id=1, has_side_effects=True, vmem_limit_bytes=VMEM_LIMIT
        ),
        name="backward_scatter",
    )(*operands)


def copy_kernel(count, *refs):
    sources, targets = refs[:count], refs[count : 2 * count]
    buffers, (load_sem, store_sem) = refs[2 * count : 3 * count], refs[3 * count :]
    loads, stores = [], []
    for source, target, buffer in zip(sources, targets, buffers):
        rows = source.shape[0]
        pieces = 10 if rows >= 1024 else 1
        for piece in range(pieces):
            part = pl.ds(piece * (rows // pieces), rows // pieces)
            number = len(loads)
            loads.append(
                pltpu.make_async_copy(source.at[part], buffer.at[part], load_sem.at[number])
            )
            stores.append(
                pltpu.make_async_copy(buffer.at[part], target.at[part], store_sem.at[number])
            )
    for copy in loads:
        copy.start()
    for load, store in zip(loads, stores):
        load.wait()
        store.start()
    for copy in stores:
        copy.wait()


def hand_out(arrays):
    count = len(arrays)
    hbm = pl.BlockSpec(memory_space=pl.ANY)
    return pl.pallas_call(
        partial(copy_kernel, count),
        out_shape=[jax.ShapeDtypeStruct(array.shape, array.dtype) for array in arrays],
        in_specs=[hbm] * count,
        out_specs=[hbm] * count,
        scratch_shapes=[pltpu.VMEM(array.shape, array.dtype) for array in arrays]
        + [pltpu.SemaphoreType.DMA((10 + count,))] * 2,
        name="hand_out",
    )(*arrays)


def local_fused(
    latents,
    inputs,
    segment,
    cross_weights,
    self_weights,
    vectors,
    up_weight,
    down_weight,
    cotangent,
):
    tensor_count = lax.axis_size("tensor")
    shard = cross_weights.shape[0]
    seg = segment.reshape(-1, LANES)
    (
        latents_out,
        wc,
        ws,
        ctx,
        keys,
        vals,
        prob,
        gup,
        gdn,
        vecs,
        query,
        read,
        mid,
        query2,
        key2,
        val2,
        prob2,
        read2,
        late,
        gn3,
        gb1,
        inv,
    ) = forward_call(
        tensor_count,
        latents,
        inputs,
        seg,
        cross_weights,
        self_weights,
        up_weight,
        down_weight.T,
        vectors,
        cotangent,
    )
    operands = [latents, cotangent, mid, late, gn3, read, read2, query, query2, key2, val2]
    operands += [prob2, vecs, gb1, inv, wc, ws, ctx, keys, vals, prob, gup, gdn, inputs]
    glat, ginp, gcross, gself, gvec, gup_sum, gdn_sum, unused = backward_call(
        tensor_count, shard, vectors.shape, operands
    )
    results = hand_out([latents_out, glat, ginp, gcross, gself, gvec, gup_sum, gdn_sum])
    return (*results[:7], results[7].T)


def solution(mesh):
    placed = (
        P(("dp", "tensor"), None),
        P(("dp", "tensor"), None),
        P(("dp", "tensor")),
        P(("dp", "tensor"), None),
        P(("dp", "tensor"), None),
        P(None, ("dp", "tensor")),
        P("dp", "tensor"),
        P("tensor", "dp"),
        P(("dp", "tensor"), None),
    )
    shards = mesh.shape["dp"] * mesh.shape["tensor"]
    fused = mesh.shape["dp"] == 8 and mesh.shape["tensor"] == 4 and 4 * D % (32 * shards) == 0
    return jax.shard_map(
        local_fused if fused else local,
        mesh=mesh,
        in_specs=placed,
        out_specs=(
            P(("dp", "tensor"), None),
            P(("dp", "tensor"), None),
            P(("dp", "tensor"), None),
            P(("dp", "tensor"), None),
            P(("dp", "tensor"), None),
            P(None, ("dp", "tensor")),
            P("dp", "tensor"),
            P("tensor", "dp"),
        ),
        check_vma=False,
    )
```

```python
from functools import partial

import jax
import jax.numpy as jnp
from jax import lax
from jax.experimental import pallas as pl
from jax.experimental.pallas import tpu as pltpu
from jax.sharding import PartitionSpec as P

D = 768
HEAD_DIM = 64
FF = 3072
LAT = 128


def cut_along(x, dim, size):
    before, after = (x.shape[:dim], x.shape[dim + 1 :])
    return jnp.moveaxis(x.reshape(*before, size, -1, *after), dim, 0)


def sent_and_summed(x, axis, dim):
    parts = cut_along(x, dim, lax.axis_size(axis))
    arrived = lax.all_to_all(parts, axis, split_axis=0, concat_axis=0, tiled=True)
    return arrived.astype(jnp.float32).sum(axis=0)


def product(left, right):
    return jnp.dot(left, right, preferred_element_type=jnp.float32)


def product_tn(left, right):
    return lax.dot_general(
        left, right, (((0,), (0,)), ((), ())), preferred_element_type=jnp.float32
    )


def product_nt(left, right):
    return lax.dot_general(
        left, right, (((1,), (1,)), ((), ())), preferred_element_type=jnp.float32
    )


def layer_norm(values, gain_row, shift_row):
    average = jnp.mean(values, axis=-1, keepdims=True)
    centred = values - average
    variance = jnp.mean(centred * centred, axis=-1, keepdims=True)
    return centred * lax.rsqrt(variance + 1e-05) * gain_row + shift_row


def norm_backward(values, gain_row, shift_row, incoming):
    unused, pullback = jax.vjp(layer_norm, values, gain_row, shift_row)
    return pullback(incoming)


def split_heads(values):
    return values.reshape(values.shape[0], -1, HEAD_DIM).transpose(1, 0, 2)


def merge_heads(values):
    return values.transpose(1, 0, 2).reshape(values.shape[1], -1)


def head_probs(head_query, head_key, visible, peak_score, denominator):
    scores = product_nt(head_query, head_key) * HEAD_DIM ** (-0.5)
    exponent = jnp.exp(jnp.where(visible, scores - peak_score, -200.0)) * visible.astype(
        jnp.float32
    )
    return exponent / denominator


def attend_forward(queries, keys_in, values_in, visible):
    has_keys = jnp.any(visible, axis=-1, keepdims=True)
    seen_float = visible.astype(jnp.float32)

    def one_head(operands):
        head_query, head_key, head_value = operands
        scores = product_nt(head_query, head_key) * HEAD_DIM ** (-0.5)
        peak_score = jnp.max(jnp.where(visible, scores, -1000000000.0), axis=-1, keepdims=True)
        peak_score = jnp.where(has_keys, peak_score, 0.0)
        exponent = jnp.exp(jnp.where(visible, scores - peak_score, -200.0)) * seen_float
        denominator = jnp.sum(exponent, axis=-1, keepdims=True) + 1.0 - has_keys.astype(jnp.float32)
        attn_probs = (exponent / denominator).astype(jnp.bfloat16)
        return (product(attn_probs, head_value), peak_score, denominator)

    outputs, peaks, denominators = lax.map(
        one_head, (split_heads(queries), split_heads(keys_in), split_heads(values_in))
    )
    return (merge_heads(outputs).astype(jnp.bfloat16), peaks, denominators)


def attend_backward(queries, keys_in, values_in, visible, peaks, denominators, grad_read):
    score_scale = HEAD_DIM ** (-0.5)

    def one_head(operands):
        head_query, head_key, head_value, peak_score, denominator, head_grad = operands
        attn_probs = head_probs(head_query, head_key, visible, peak_score, denominator)
        grad_probs = product_nt(head_grad, head_value)
        grad_value = product_tn(attn_probs.astype(jnp.bfloat16), head_grad)
        inner_sum = jnp.sum(grad_probs * attn_probs, axis=-1, keepdims=True)
        grad_scores = (attn_probs * (grad_probs - inner_sum)).astype(jnp.bfloat16)
        grad_query = product(grad_scores, head_key) * score_scale
        grad_key = product_tn(grad_scores, head_query) * score_scale
        return (grad_query, grad_key, grad_value)

    grad_q, grad_k, grad_v = lax.map(
        one_head,
        (
            split_heads(queries),
            split_heads(keys_in),
            split_heads(values_in),
            peaks,
            denominators,
            split_heads(grad_read),
        ),
    )
    return (
        merge_heads(grad_q).astype(jnp.bfloat16),
        merge_heads(grad_k).astype(jnp.bfloat16),
        merge_heads(grad_v).astype(jnp.bfloat16),
    )


def column_sum(values):
    return jnp.sum(values.astype(jnp.float32), axis=0)


def local(
    latents,
    inputs,
    segment,
    cross_weights,
    self_weights,
    vectors,
    up_weight,
    down_weight,
    cotangent,
):
    cross_full, self_full, vector_half = (
        lax.all_gather(cross_weights, ("dp", "tensor"), axis=0, tiled=True),
        lax.all_gather(self_weights, ("dp", "tensor"), axis=0, tiled=True),
        lax.all_gather(vectors, ("dp", "tensor"), axis=1, tiled=True),
    )
    up_full, down_full = (
        lax.all_gather(up_weight, "dp", axis=0, tiled=True),
        lax.all_gather(down_weight, "dp", axis=1, tiled=True),
    )
    vector_rows = vector_half.astype(jnp.float32)
    quarter = up_full.shape[1]
    part_index = lax.axis_index("tensor")
    bias_up = lax.dynamic_slice_in_dim(
        vector_rows[15:].reshape(-1), part_index * quarter, quarter, 0
    )
    row_count = latents.shape[0]
    slot_row = jnp.arange(row_count, dtype=jnp.int32) // LAT
    cross_seen = slot_row[:, None] == segment[None, :]
    self_seen = slot_row[:, None] == slot_row[None, :]
    input_float = inputs.astype(jnp.float32)
    normed = layer_norm(latents, vector_rows[0], vector_rows[1]).astype(jnp.bfloat16)
    context = layer_norm(input_float, vector_rows[2], vector_rows[3]).astype(jnp.bfloat16)
    queries = (product(normed, cross_full[:D]) + vector_rows[4]).astype(jnp.bfloat16)
    keys_in = product(context, cross_full[D : 2 * D]).astype(jnp.bfloat16)
    values_in = (product(context, cross_full[2 * D : 3 * D]) + vector_rows[5]).astype(jnp.bfloat16)
    cross_read, cross_peaks, cross_denoms = attend_forward(queries, keys_in, values_in, cross_seen)
    after_cross = latents + (product(cross_read, cross_full[3 * D :]) + vector_rows[6])
    normed_two = layer_norm(after_cross, vector_rows[7], vector_rows[8]).astype(jnp.bfloat16)
    queries_two = (product(normed_two, self_full[:D]) + vector_rows[9]).astype(jnp.bfloat16)
    keys_two = product(normed_two, self_full[D : 2 * D]).astype(jnp.bfloat16)
    values_two = (product(normed_two, self_full[2 * D : 3 * D]) + vector_rows[10]).astype(
        jnp.bfloat16
    )
    self_read, self_peaks, self_denoms = attend_forward(
        queries_two, keys_two, values_two, self_seen
    )
    after_self = after_cross + (product(self_read, self_full[3 * D :]) + vector_rows[11])
    normed_three = layer_norm(after_self, vector_rows[12], vector_rows[13]).astype(jnp.bfloat16)
    gathered = lax.all_gather(normed_three, "tensor", axis=0, tiled=True)
    pre_act = product(gathered, up_full) + bias_up
    hidden = jax.nn.gelu(pre_act, approximate=False).astype(jnp.bfloat16)
    reduced = lax.psum_scatter(
        product(hidden, down_full).astype(jnp.bfloat16), "tensor", scatter_dimension=0, tiled=True
    ).astype(jnp.float32)
    latents_out = after_self + (reduced + vector_rows[14])
    cross_full, self_full, vector_half = (
        lax.all_gather(cross_weights, ("dp", "tensor"), axis=0, tiled=True),
        lax.all_gather(self_weights, ("dp", "tensor"), axis=0, tiled=True),
        lax.all_gather(vectors, ("dp", "tensor"), axis=1, tiled=True),
    )
    up_full, down_full = (
        lax.all_gather(up_weight, "dp", axis=0, tiled=True),
        lax.all_gather(down_weight, "dp", axis=1, tiled=True),
    )
    vector_rows = vector_half.astype(jnp.float32)
    grad_y = cotangent.astype(jnp.bfloat16)
    grad_b2 = column_sum(grad_y)
    grad_rows = lax.all_gather(grad_y, "tensor", axis=0, tiled=True)
    grad_down = product_tn(hidden, grad_rows)
    grad_hidden = product_nt(grad_rows, down_full)
    unused, gelu_pull = jax.vjp(partial(jax.nn.gelu, approximate=False), pre_act)
    grad_pre = gelu_pull(grad_hidden)[0].astype(jnp.bfloat16)
    grad_b1 = column_sum(grad_pre)
    grad_up = product_tn(gathered, grad_pre)
    mlp_sums = (
        sent_and_summed(grad_up.astype(jnp.bfloat16), "dp", 0),
        sent_and_summed(grad_down.astype(jnp.bfloat16), "dp", 1),
    )
    grad_normed_three = lax.psum_scatter(
        product_nt(grad_pre, up_full).astype(jnp.bfloat16),
        "tensor",
        scatter_dimension=0,
        tiled=True,
    ).astype(jnp.float32)
    back_self, grad_gain_three, grad_shift_three = norm_backward(
        after_self, vector_rows[12], vector_rows[13], grad_normed_three
    )
    grad_after_self = cotangent + back_self
    grad_out_two = grad_after_self.astype(jnp.bfloat16)
    grad_bias_out_two = column_sum(grad_out_two)
    grad_wo_two = product_tn(self_read, grad_out_two)
    grad_read_two = product_nt(grad_out_two, self_full[3 * D :]).astype(jnp.bfloat16)
    grad_q_two, grad_k_two, grad_v_two = attend_backward(
        queries_two, keys_two, values_two, self_seen, self_peaks, self_denoms, grad_read_two
    )
    grad_self = jnp.concatenate(
        [
            product_tn(normed_two, grad_q_two),
            product_tn(normed_two, grad_k_two),
            product_tn(normed_two, grad_v_two),
            grad_wo_two,
        ],
        axis=0,
    )
    grad_normed_two = (
        product_nt(grad_q_two, self_full[:D])
        + product_nt(grad_k_two, self_full[D : 2 * D])
        + product_nt(grad_v_two, self_full[2 * D : 3 * D])
    )
    back_cross, grad_gain_two, grad_shift_two = norm_backward(
        after_cross, vector_rows[7], vector_rows[8], grad_normed_two
    )
    grad_after_cross = grad_after_self + back_cross
    grad_out_one = grad_after_cross.astype(jnp.bfloat16)
    grad_bias_out_one = column_sum(grad_out_one)
    grad_wo_one = product_tn(cross_read, grad_out_one)
    grad_read_one = product_nt(grad_out_one, cross_full[3 * D :]).astype(jnp.bfloat16)
    grad_q_one, grad_k_one, grad_v_one = attend_backward(
        queries, keys_in, values_in, cross_seen, cross_peaks, cross_denoms, grad_read_one
    )
    grad_cross = jnp.concatenate(
        [
            product_tn(normed, grad_q_one),
            product_tn(context, grad_k_one),
            product_tn(context, grad_v_one),
            grad_wo_one,
        ],
        axis=0,
    )
    grad_normed = product_nt(grad_q_one, cross_full[:D])
    back_latent, grad_gain_one, grad_shift_one = norm_backward(
        latents, vector_rows[0], vector_rows[1], grad_normed
    )
    grad_latents = grad_after_cross + back_latent
    grad_context = product_nt(grad_k_one, cross_full[D : 2 * D]) + product_nt(
        grad_v_one, cross_full[2 * D : 3 * D]
    )
    back_input, grad_gain_input, grad_shift_input = norm_backward(
        input_float, vector_rows[2], vector_rows[3], grad_context
    )
    grad_inputs = back_input.astype(jnp.bfloat16)
    full_bias = lax.dynamic_update_slice_in_dim(
        jnp.zeros((FF,), jnp.float32), grad_b1, part_index * quarter, 0
    )
    grad_vectors = jnp.concatenate(
        [
            jnp.stack(
                [
                    grad_gain_one,
                    grad_shift_one,
                    grad_gain_input,
                    grad_shift_input,
                    column_sum(grad_q_one),
                    column_sum(grad_v_one),
                    grad_bias_out_one,
                    grad_gain_two,
                    grad_shift_two,
                    column_sum(grad_q_two),
                    column_sum(grad_v_two),
                    grad_bias_out_two,
                    grad_gain_three,
                    grad_shift_three,
                    grad_b2,
                ],
                axis=0,
            ),
            full_bias.reshape(-1, D),
        ],
        axis=0,
    )
    cross_sums, self_sums, vector_sums = (
        lax.psum_scatter(grad_cross, ("dp", "tensor"), scatter_dimension=0, tiled=True),
        lax.psum_scatter(grad_self, ("dp", "tensor"), scatter_dimension=0, tiled=True),
        lax.psum_scatter(grad_vectors, ("dp", "tensor"), scatter_dimension=1, tiled=True),
    )
    return (
        latents_out,
        grad_latents,
        grad_inputs,
        cross_sums,
        self_sums,
        vector_sums,
        mlp_sums[0],
        mlp_sums[1],
    )


BF = jnp.bfloat16
F32 = jnp.float32
MESH = pl.DeviceIdType.MESH
TILE = 256
PAD = 128
GROUP = 256
GROUPS = D // GROUP
GHEADS = GROUP // HEAD_DIM
LANES = 128
HIDE = -1e30
VEC_PAD = 32
VEC_TOP = 24
NROWS = 4 * D
SLOT1_FIRST = 2
SLOT1_TILES = 2
VMEM_LIMIT = 63 * 1024 * 1024


GATHER_PLAN = {
    "start": ((0, 0), (0, 4)),
    "vecb": ((1, 0), (0, 1)),
    "ln0": ((0, 2),),
    "ln1": ((1, 1), (2, 0)),
    "ln4": ((0, 3),),
    "ln6": ((1, 2),),
    "ln8": ((2, 1), (0, 5)),
    "post": ((1, 3), (1, 4)),
    "q": ((3, 0), (3, 1), (0, 6), (2, 2), (3, 2), (2, 3), (1, 5), (0, 7), (3, 3), (0, 8)),
    "kv0": ((1, 6), (2, 4)),
    "kv1": ((0, 9),),
    "kv4": ((1, 7),),
    "kv7": ((0, 10),),
    "kv8": ((1, 8),),
    "p0_0": ((0, 11), (0, 12)),
    "p0_3": ((2, 5), (2, 6), (2, 7), (0, 13)),
    "p1_1": ((2, 8),),
    "t1": ((0, 14),),
    "t2": ((0, 15),),
    "self0": ((3, 4), (3, 5), (3, 6), (3, 7), (1, 9), (1, 10), (1, 11), (1, 12), (1, 13)),
    "self1": ((1, 14),),
    "up0": ((1, 15), (3, 8)),
    "up1": ((2, 9), (2, 10), (3, 9)),
    "up2": ((2, 11), (3, 10)),
    "up3": ((2, 12), (3, 11)),
    "down0": ((2, 13), (3, 12)),
    "down1": ((2, 14), (3, 13)),
    "down2": ((2, 15), (3, 14)),
    "down3": ((3, 15),),
}
SCATTER_PLAN = {
    "b": ((0, 0), (0, 1)),
    "d": ((0, 2),),
    "CS2": ((0, 3),),
    "e": ((1, 0), (1, 1)),
    "f": ((0, 4), (0, 5)),
    "t0": ((1, 2), (2, 0)),
    "t1": ((0, 6),),
    "t2": ((1, 3), (2, 1)),
    "t3": ((2, 2),),
    "t4": ((1, 5), (2, 3), (0, 7), (0, 8)),
    "t5": ((1, 6),),
    "t6": ((2, 5),),
    "t7": ((0, 9),),
    "t8": ((1, 7), (2, 6), (0, 10), (3, 0)),
    "t9": ((1, 8),),
    "t11": ((2, 7), (0, 11)),
    "t12": ((1, 9), (2, 8)),
    "g": ((1, 10), (3, 1)),
    "u0": ((2, 9),),
    "u1": ((1, 11), (2, 10)),
    "u2": ((0, 12),),
    "u3": ((0, 13),),
    "u4": ((2, 11), (0, 14)),
    "u8": ((1, 13),),
    "u11": ((1, 14),),
    "u12": ((2, 13), (3, 2)),
    "end": ((4, 0), (2, 14), (4, 1), (0, 15), (4, 2), (4, 3), (1, 15), (4, 4), (2, 15), (3, 3)),
}
Z_UNITS = (1, 2)
Z_UNITS_BACK = (1, 3)


def nn(left, right):
    return jnp.dot(left, right, preferred_element_type=F32)


def nt(left, right):
    return lax.dot_general(
        left, right, (((1,), (1,)), ((), ())), preferred_element_type=F32
    )


def ln_parts(values):
    average = jnp.mean(values, axis=-1, keepdims=True)
    centred = values - average
    variance = jnp.mean(centred * centred, axis=-1, keepdims=True)
    scale = lax.rsqrt(variance + 1e-05)
    return centred * scale, scale


def ln_rows(values, gain_row, shift_row):
    return ln_parts(values)[0] * gain_row + shift_row


def flipped(z, step):
    value = z
    if step % 2:
        value = value + 1 - 2 * lax.rem(z, 2)
    if step // 2:
        value = value + 2 - 4 * (z // 2)
    return value


def neighbours(tensor_count):
    dp = lax.axis_index("dp")
    z = lax.axis_index("tensor")
    core = lax.rem(dp, 2)
    flip_x = dp + 2 * (1 - 2 * lax.rem(dp // 2, 2))
    flip_y = dp + 4 * (1 - 2 * (dp // 4))
    other = dp + 1 - 2 * core
    first = (1 - core) * flip_x + core * flip_y
    second = (1 - core) * flip_y + core * flip_x
    both = flip_x + flip_y - dp
    peers = [flipped(z, step) for step in range(1, tensor_count)]
    return dp, z, core, other, first, second, both, peers


def meet(dp, z, other, first, second, peers):
    barrier = pltpu.get_barrier_semaphore()
    devices = [(other, z), (first, z), (second, z)] + [(dp, peer) for peer in peers]
    for device in devices:
        pl.semaphore_signal(barrier, inc=1, device_id=device, device_id_type=MESH)
    pl.semaphore_wait(barrier, len(devices))


def head_mask(rows):
    row_head = lax.broadcasted_iota(jnp.int32, (rows, GROUP), 0) // LAT
    col_head = lax.broadcasted_iota(jnp.int32, (rows, GROUP), 1) // HEAD_DIM
    return row_head == col_head


def spread_heads(block, mask):
    wide = jnp.concatenate([block.astype(F32)] * GHEADS, axis=0)
    return jnp.where(mask, wide, 0.0).astype(BF)


def pick_heads(stacked):
    col_head = lax.broadcasted_iota(jnp.int32, (LAT, GROUP), 1) // HEAD_DIM
    total = jnp.zeros((LAT, GROUP), F32)
    for head in range(GHEADS):
        part = stacked[head * LAT : (head + 1) * LAT]
        total = total + jnp.where(col_head == head, part, 0.0)
    return total


def forward_kernel(
    tensor_count,
    lat,
    inp,
    seg_in,
    cross_shard,
    self_shard,
    up_shard,
    down_shard,
    vectors,
    cot,
    out_o,
    wc_o,
    ws_o,
    ctx_o,
    key_o,
    val_o,
    prob_o,
    gup_o,
    gdn_o,
    vec_o,
    query_h,
    read_h,
    mid_h,
    query2_h,
    key2_h,
    val2_h,
    prob2_h,
    read2_h,
    late_h,
    gn3_o,
    gb1_o,
    inv_o,
    query_o,
    read,
    mid_o,
    query2_o,
    key2_o,
    val2_o,
    prob2_o,
    read2_o,
    late_o,
    seg,
    vec_own,
    w_cross,
    w_self,
    w_up,
    w_down,
    ctx,
    keys,
    vals,
    scores,
    probs,
    inbuf,
    qbd,
    peak,
    denom,
    oacc,
    norm_t,
    gy_t,
    vec_in,
    vec_sum,
    send_sem,
    recv_sem,
    vec_ssem,
    vec_rsem,
    in_sem,
    out_sem,
):
    dp, z, core, other, first, second, both, peers = neighbours(tensor_count)
    meet(dp, z, other, first, second, peers)
    weights = (w_cross, w_self, w_up, w_down)
    shards = (cross_shard, self_shard, up_shard, down_shard)
    shard_rows = cross_shard.shape[0]
    tiles = ctx.shape[0] // TILE
    chunk_count = 4 * tensor_count
    kinds = 7

    def place(unit, owner, part):
        if unit < 2:
            start = (owner * tensor_count + part) * shard_rows
        else:
            start = part * D + owner * shard_rows
        return pl.ds(pl.multiple_of(start, shard_rows), shard_rows)

    def remote(source, target, number, device):
        return pltpu.make_async_remote_copy(
            src_ref=source,
            dst_ref=target,
            send_sem=send_sem.at[number],
            recv_sem=recv_sem.at[number],
            device_id=device,
            device_id_type=MESH,
        )

    def z_copy(unit, step):
        rows = place(unit, dp, z)
        number = chunk_count * kinds + unit * (tensor_count - 1) + step - 1
        return remote(shards[unit], weights[unit].at[rows], number, (dp, peers[step - 1]))

    by_z = [unit * tensor_count + 1 for unit in Z_UNITS]

    def plane_copy(chunk, kind):
        unit, step = divmod(chunk, tensor_count)
        part = flipped(z, step)
        owner = (dp, dp, first, dp, first, second, both)[kind]
        device = ((first, second, second, other, other, other, other)[kind], z)
        if chunk in by_z and kind < 3:
            part, owner, device = z, (first, second, both)[kind], (dp, peers[0])
        rows = place(unit, owner, part)
        return remote(
            weights[unit].at[rows], weights[unit].at[rows], chunk * kinds + kind, device
        )

    def z_start(unit):
        for step in range(1, tensor_count):
            z_copy(unit, step).start()

    def stage0(chunk):
        unit, step = divmod(chunk, tensor_count)
        if step:
            z_copy(unit, step).wait_recv()
        for kind in (3,) if chunk in by_z else (0, 1, 3):
            plane_copy(chunk, kind).start()

    def pass_on(chunk, kind):
        if chunk + 1 in by_z:
            plane_copy(chunk + 1, kind).start()

    def stage1(chunk):
        plane_copy(chunk, 0).wait_recv()
        for kind in (4,) if chunk in by_z else (2, 4):
            plane_copy(chunk, kind).start()
        pass_on(chunk, 0)

    def stage2(chunk):
        plane_copy(chunk, 1).wait_recv()
        plane_copy(chunk, 5).start()
        pass_on(chunk, 1)
        plane_copy(chunk, 2).wait_recv()
        plane_copy(chunk, 6).start()
        pass_on(chunk, 2)

    def stage3(chunk):
        for kind in (3, 4, 5, 6):
            plane_copy(chunk, kind).wait_recv()

    def send_first(chunk):
        stage0(chunk)
        unit, step = divmod(chunk, tensor_count)
        if step == tensor_count - 2 and unit < 3:
            z_start(unit + 1)

    stages = (send_first, stage1, stage2, stage3)

    def run_at(name):
        for stage, chunk in GATHER_PLAN.get(name, ()):
            stages[stage](chunk)

    def run_each(name, index, count):
        for number in range(count):
            if GATHER_PLAN.get(name + str(number)):
                pl.when(index == number)(partial(run_at, name + str(number)))

    def vec_copy(hop):
        if hop < tensor_count - 1:
            source, device = vec_own, (dp, peers[hop])
        else:
            level = hop - (tensor_count - 1)
            source, device = vec_sum.at[level], ((first, second, other)[level], z)
        return pltpu.make_async_remote_copy(
            src_ref=source,
            dst_ref=vec_in.at[hop],
            send_sem=vec_ssem.at[hop],
            recv_sem=vec_rsem.at[hop],
            device_id=device,
            device_id_type=MESH,
        )

    def read_in(index):
        rows = inbuf.shape[1]
        start = pl.multiple_of(index * rows, rows)
        slot = lax.rem(index, 2)
        return pltpu.make_async_copy(
            inp.at[pl.ds(start, rows)], inbuf.at[slot], in_sem.at[slot]
        )

    def keep(source, target, number):
        return pltpu.make_async_copy(source, target, out_sem.at[number])

    width = vectors.shape[1]
    first_col = (dp * tensor_count + z) * width
    row = lax.broadcasted_iota(jnp.int32, (width, D), 0)
    col = lax.broadcasted_iota(jnp.int32, (width, D), 1)
    spot = jnp.where(col == row + first_col, 1.0, 0.0).astype(BF)
    vec_own[...] = jnp.zeros(vec_own.shape, BF)
    vec_own[0 : vectors.shape[0], :] = nn(vectors[...], spot).astype(BF)
    for hop in range(tensor_count - 1):
        vec_copy(hop).start()
    w_cross[place(0, dp, z), :] = cross_shard[...]
    z_start(0)
    read_in(0).start()
    keep(cot, gn3_o, 16).start()
    for unit in range(1, 4):
        weights[unit][place(unit, dp, z), :] = shards[unit][...]
    seg[...] = jnp.full(seg.shape, 2, jnp.int32)
    for row in range(seg_in.shape[0]):
        seg[:, PAD + row * LANES : PAD + (row + 1) * LANES] = seg_in[row : row + 1, :]
    run_at("start")
    run_at("vecz")
    for hop in range(tensor_count - 1):
        vec_copy(hop).wait_recv()
    total = vec_own[...].astype(F32)
    for hop in range(tensor_count - 1):
        total = total + vec_in[hop].astype(F32)
    for level in range(3):
        vec_sum[level] = total.astype(BF)
        hop = tensor_count - 1 + level
        vec_copy(hop).start()
        run_at(("veca", "vecb", "vecc")[level])
        vec_copy(hop).wait_recv()
        total = total + vec_in[hop].astype(F32)
    vec_o[...] = total

    def vec(row):
        return vec_o[row : row + 1, :]

    ctx[0:PAD, :] = jnp.zeros((PAD, D), BF)
    in_rows = inbuf.shape[1]
    reads = inp.shape[0] // in_rows

    def norm_inputs(index, carry):
        @pl.when(index + 1 < reads)
        def _():
            read_in(index + 1).start()

        read_in(index).wait()
        slot = lax.rem(index, 2)

        def rows_of(part, carry2):
            start = pl.multiple_of(part * 64, 64)
            values = inbuf[slot, pl.ds(start, 64), :].astype(F32)
            ctx[pl.ds(pl.multiple_of(PAD + index * in_rows + start, 64), 64), :] = ln_rows(
                values, vec(2), vec(3)
            ).astype(BF)
            return carry2

        lax.fori_loop(0, in_rows // 64, rows_of, 0)

        run_each("ln", index, reads)
        return carry

    lax.fori_loop(0, reads, norm_inputs, 0)
    run_at("post")
    normed = ln_rows(lat[...], vec(0), vec(1)).astype(BF)
    keep(cot, gn3_o, 16).wait()
    gy = gn3_o[...].astype(BF)
    gy_t[...] = gn3_o[...].T.astype(BF)
    run_at("q")
    keep(w_cross, wc_o, 0).start()
    mask = head_mask(GHEADS * LAT)

    query = (nn(normed, w_cross[0:D, :]) + vec(4)).astype(BF)
    scaled = (query.astype(F32) * HEAD_DIM ** (-0.5)).astype(BF)
    query_o[...] = scaled
    for slot in range(2):
        for group in range(GROUPS):
            block = scaled[slot * LAT : (slot + 1) * LAT, group * GROUP : (group + 1) * GROUP]
            qbd[slot * GROUPS + group] = spread_heads(block, mask)

    def project(index, carry):
        rows = pl.ds(pl.multiple_of(index * TILE, TILE), TILE)
        block = ctx[rows, :]
        keys[rows, :] = nn(block, w_cross[D : 2 * D, :]).astype(BF)
        vals[rows, :] = (nn(block, w_cross[2 * D : 3 * D, :]) + vec(5)).astype(BF)

        run_each("kv", index, tiles)
        return carry

    lax.fori_loop(0, tiles, project, 0)
    keep(ctx, ctx_o, 1).start()
    keep(keys, key_o, 2).start()
    keep(vals, val_o, 3).start()

    wide = 3 * TILE
    whole = tiles // 3
    rest = [
        (0, slice(whole * wide, tiles * TILE), slice(whole * wide, tiles * TILE)),
        (
            1,
            slice(SLOT1_FIRST * TILE, (SLOT1_FIRST + SLOT1_TILES) * TILE),
            slice(tiles * TILE, (tiles + SLOT1_TILES) * TILE),
        ),
    ]

    def wide_cols(index):
        return pl.ds(pl.multiple_of(index * wide, wide), wide)

    def fold(values, op):
        parts = [values[:, at : at + LANES] for at in range(0, values.shape[1], LANES)]
        while len(parts) > 1:
            parts = [
                op(parts[at], parts[at + 1]) if at + 1 < len(parts) else parts[at]
                for at in range(0, len(parts), 2)
            ]
        return parts[0]

    seen = []
    for slot in range(2):
        hit = jnp.where(seg[...] == slot, 1.0, 0.0)
        seen.append(jnp.max(hit, axis=1, keepdims=True))

    for group in range(GROUPS):
        gcols = slice(group * GROUP, (group + 1) * GROUP)
        peak[...] = jnp.full(peak.shape, HIDE, F32)
        denom[...] = jnp.zeros(denom.shape, F32)
        oacc[...] = jnp.zeros(oacc.shape, F32)

        def score_part(slot, rows, cols):
            values = nt(qbd[slot * GROUPS + group], keys[rows, gcols])
            values = jnp.where(seg[:, rows] == slot, values, HIDE)
            scores[:, cols] = values
            peak[slot] = jnp.maximum(peak[slot], fold(values, jnp.maximum))

        def score(index, carry):
            score_part(0, wide_cols(index), wide_cols(index))
            return carry

        run_at("s%d" % group)
        lax.fori_loop(0, whole, score, 0)
        for slot, rows, cols in rest:
            score_part(slot, rows, cols)
        for slot in range(2):
            top = jnp.max(peak[slot], axis=1, keepdims=True)
            top = jnp.where(seen[slot] > 0.0, top, 0.0)
            peak[slot] = jnp.broadcast_to(top, (GHEADS * LAT, LANES))
        if group:
            keep(probs, prob_o.at[group - 1], 4).wait()

        def spread_part(slot, rows, cols):
            for head in range(GHEADS):
                part = slice(head * LAT, (head + 1) * LAT)
                values = scores[part, cols]
                count = values.shape[1] // LANES
                top = jnp.concatenate([peak[slot, part, :]] * count, axis=1)
                values = jnp.exp(values - top)
                probs[part, cols] = values.astype(BF)
                denom[slot, part, :] += fold(values, jnp.add)
            oacc[slot] += nn(probs[:, cols], vals[rows, gcols])

        def spread(index, carry):
            run_each("p%d_" % group, index, whole)
            spread_part(0, wide_cols(index), wide_cols(index))
            return carry

        lax.fori_loop(0, whole, spread, 0)
        for slot, rows, cols in rest:
            spread_part(slot, rows, cols)
        keep(probs, prob_o.at[group], 4).start()
        run_at("t%d" % group)
        for slot in range(2):
            total = jnp.sum(denom[slot], axis=1, keepdims=True) + 1.0 - seen[slot]
            scale = 1.0 / total
            full = jnp.broadcast_to(scale, (GHEADS * LAT, GROUP))
            inv_o[slot * LAT : (slot + 1) * LAT, gcols] = pick_heads(full)
            read[slot * LAT : (slot + 1) * LAT, gcols] = pick_heads(oacc[slot] * scale)

    run_at("mid")
    mid = lat[...] + (nn(read[...].astype(BF), w_cross[3 * D :, :]) + vec(6))
    mid_o[...] = mid
    normed_two = ln_rows(mid, vec(7), vec(8)).astype(BF)
    run_at("self0")
    keep(w_self, ws_o, 5).start()
    query_two = (nn(normed_two, w_self[0:D, :]) + vec(9)).astype(BF)
    query2_o[...] = (query_two.astype(F32) * HEAD_DIM ** (-0.5)).astype(BF)
    key2_o[...] = nn(normed_two, w_self[D : 2 * D, :]).astype(BF)
    val2_o[...] = (nn(normed_two, w_self[2 * D : 3 * D, :]) + vec(10)).astype(BF)
    run_at("self1")
    for slot in range(2):
        srows = slice(slot * LAT, (slot + 1) * LAT)
        for group in range(GROUPS):
            gcols = slice(group * GROUP, (group + 1) * GROUP)
            wide = spread_heads(query2_o[srows, gcols], mask)
            values = nt(wide, key2_o[srows, gcols])
            values = jnp.exp(values - jnp.max(values, axis=1, keepdims=True))
            values = values / jnp.sum(values, axis=1, keepdims=True)
            values = values.astype(BF)
            prob2_o[slot, group] = values
            read2_o[srows, gcols] = pick_heads(nn(values, val2_o[srows, gcols]))
    late = mid_o[...] + (nn(read2_o[...].astype(BF), w_self[3 * D :, :]) + vec(11))
    late_o[...] = late
    normed_three = ln_rows(late, vec(12), vec(13))
    norm_t[...] = normed_three.T.astype(BF)
    normed_three = normed_three.astype(BF)
    keep(probs, prob_o.at[GROUPS - 1], 4).wait()
    keep(keys, key_o, 2).wait()
    keep(vals, val_o, 3).wait()

    small = [
        (query_o, query_h),
        (read, read_h),
        (mid_o, mid_h),
        (query2_o, query2_h),
        (key2_o, key2_h),
        (val2_o, val2_h),
        (prob2_o, prob2_h),
        (read2_o, read2_h),
        (late_o, late_h),
    ]
    for number, (source, target) in enumerate(small):
        keep(source, target, 17 + number).start()

    rows_all = slice(0, 2 * LAT)

    def quarter(step):
        part = flipped(z, step)
        return part, pl.ds(pl.multiple_of(part * D, D), D)

    def up_part(step):
        part, rows = quarter(step)
        cols = slice(step * D, (step + 1) * D)
        pre = nn(normed_three, w_up[rows, :]) + vec_o[pl.ds(15 + part, 1), :]
        half = 0.5 * (1.0 + lax.erf(pre * 0.5**0.5))
        slope = half + pre * jnp.exp(-0.5 * pre * pre) * 0.3989422804014327
        hidden = (pre * half).astype(BF)
        probs[rows_all, cols] = hidden
        scores[rows_all, cols] = slope
        vals[rows, :] = nn(gy_t[...], hidden).astype(BF)
        keep(vals.at[rows], gdn_o.at[rows], 6 + step).start()

    def down_part(step):
        part, rows = quarter(step)
        cols = slice(step * D, (step + 1) * D)
        down = w_down[rows, :]
        y_part = nt(probs[rows_all, cols], down)
        grad_pre = (scores[rows_all, cols] * nn(gy, down)).astype(BF)
        keys[rows, :] = nn(norm_t[...], grad_pre).astype(BF)
        keep(keys.at[rows], gup_o.at[rows], 6 + tensor_count + step).start()
        x_part = nt(grad_pre, w_up[rows, :])
        if step == 0:
            out_o[...] = late_o[...] + vec(14) + y_part
            gn3_o[...] = x_part
        else:
            out_o[...] += y_part
            gn3_o[...] += x_part
        gb1_o[pl.ds(part, 1), :] = jnp.sum(grad_pre.astype(F32), axis=0, keepdims=True)

    gb1_o[...] = jnp.zeros(gb1_o.shape, F32)
    for step in range(tensor_count):
        run_at("up%d" % step)
        up_part(step)
    for step in range(tensor_count):
        run_at("down%d" % step)
        down_part(step)
    for number, (source, target) in enumerate(small):
        keep(source, target, 17 + number).wait()
    keep(w_cross, wc_o, 0).wait()
    keep(ctx, ctx_o, 1).wait()
    keep(w_self, ws_o, 5).wait()
    for step in range(tensor_count):
        part, rows = quarter(step)
        keep(vals.at[rows], gdn_o.at[rows], 6 + step).wait()
        keep(keys.at[rows], gup_o.at[rows], 6 + tensor_count + step).wait()
    for hop in range(tensor_count + 2):
        vec_copy(hop).wait_send()
    for unit in range(4):
        for step in range(1, tensor_count):
            z_copy(unit, step).wait_send()
    for chunk in range(chunk_count):
        for kind in range(kinds):
            plane_copy(chunk, kind).wait_send()


def forward_call(tensor_count, lat, inp, seg, cross_w, self_w, up_w, down_w, vectors, cot):
    rows = lat.shape[0]
    tokens = inp.shape[0] + PAD
    virtual = (tokens // TILE + SLOT1_TILES) * TILE
    sds = jax.ShapeDtypeStruct
    hbm = pl.BlockSpec(memory_space=pl.ANY)
    vmem = pl.BlockSpec(memory_space=pltpu.VMEM)
    stacked = GHEADS * LAT
    copies = 4 * tensor_count * 7 + 4 * (tensor_count - 1)
    outs = [
        (sds((rows, D), F32), vmem),
        (sds((NROWS, D), BF), hbm),
        (sds((NROWS, D), BF), hbm),
        (sds((tokens, D), BF), hbm),
        (sds((tokens, D), BF), hbm),
        (sds((tokens, D), BF), hbm),
        (sds((GROUPS, stacked, virtual), BF), hbm),
        (sds((NROWS, D), BF), hbm),
        (sds((NROWS, D), BF), hbm),
        (sds((VEC_PAD, D), F32), vmem),
        (sds((rows, D), BF), hbm),
        (sds((rows, D), F32), hbm),
        (sds((rows, D), F32), hbm),
        (sds((rows, D), BF), hbm),
        (sds((rows, D), BF), hbm),
        (sds((rows, D), BF), hbm),
        (sds((2, GROUPS, stacked, LAT), BF), hbm),
        (sds((rows, D), F32), hbm),
        (sds((rows, D), F32), hbm),
        (sds((rows, D), F32), vmem),
        (sds((8, D), F32), vmem),
        (sds((rows, D), F32), vmem),
    ]
    return pl.pallas_call(
        partial(forward_kernel, tensor_count),
        out_shape=[shape for shape, spec in outs],
        out_specs=[spec for shape, spec in outs],
        in_specs=[vmem, hbm] + [vmem] * 6 + [hbm],
        scratch_shapes=[
            pltpu.VMEM((rows, D), BF),
            pltpu.VMEM((rows, D), F32),
            pltpu.VMEM((rows, D), F32),
            pltpu.VMEM((rows, D), BF),
            pltpu.VMEM((rows, D), BF),
            pltpu.VMEM((rows, D), BF),
            pltpu.VMEM((2, GROUPS, stacked, LAT), BF),
            pltpu.VMEM((rows, D), F32),
            pltpu.VMEM((rows, D), F32),
            pltpu.VMEM((1, tokens), jnp.int32),
            pltpu.VMEM((VEC_PAD, D), BF),
            pltpu.VMEM((NROWS, D), BF),
            pltpu.VMEM((NROWS, D), BF),
            pltpu.VMEM((NROWS, D), BF),
            pltpu.VMEM((NROWS, D), BF),
            pltpu.VMEM((tokens, D), BF),
            pltpu.VMEM((tokens, D), BF),
            pltpu.VMEM((tokens, D), BF),
            pltpu.VMEM((stacked, virtual), F32),
            pltpu.VMEM((stacked, virtual), BF),
            pltpu.VMEM((2, 320, D), BF),
            pltpu.VMEM((2 * GROUPS, stacked, GROUP), BF),
            pltpu.VMEM((2, stacked, LANES), F32),
            pltpu.VMEM((2, stacked, LANES), F32),
            pltpu.VMEM((2, stacked, GROUP), F32),
            pltpu.VMEM((D, rows), BF),
            pltpu.VMEM((D, rows), BF),
            pltpu.VMEM((tensor_count + 2, VEC_PAD, D), BF),
            pltpu.VMEM((3, VEC_PAD, D), BF),
            pltpu.SemaphoreType.DMA((copies,)),
            pltpu.SemaphoreType.DMA((copies,)),
            pltpu.SemaphoreType.DMA((tensor_count + 2,)),
            pltpu.SemaphoreType.DMA((tensor_count + 2,)),
            pltpu.SemaphoreType.DMA((2,)),
            pltpu.SemaphoreType.DMA((26,)),
        ],
        compiler_params=pltpu.CompilerParams(
            collective_id=0, has_side_effects=True, vmem_limit_bytes=VMEM_LIMIT
        ),
        name="gather_forward",
    )(lat, inp, seg, cross_w, self_w, up_w, down_w, vectors, cot)


def tn(left, right):
    return lax.dot_general(
        left, right, (((0,), (0,)), ((), ())), preferred_element_type=F32
    )


def ln_back(values, gain_row, incoming):
    unit, scale = ln_parts(values)
    scaled = incoming * gain_row
    inner = jnp.mean(scaled * unit, axis=-1, keepdims=True)
    outgoing = scale * (scaled - jnp.mean(scaled, axis=-1, keepdims=True) - unit * inner)
    gain = jnp.sum(incoming * unit, axis=0, keepdims=True)
    return outgoing, gain, jnp.sum(incoming, axis=0, keepdims=True)


def head_mask_t(rows):
    row_head = lax.broadcasted_iota(jnp.int32, (GROUP, rows), 0) // HEAD_DIM
    col_head = lax.broadcasted_iota(jnp.int32, (GROUP, rows), 1) // LAT
    return row_head == col_head


def spread_columns(block, mask):
    wide = jnp.concatenate([block.T] * GHEADS, axis=1)
    return jnp.where(mask, wide, 0.0).astype(BF)


def backward_kernel(
    tensor_count,
    lat_h,
    cot_h,
    mid_h,
    late_h,
    gn3_h,
    read_h,
    read2_h,
    query_h,
    query2_h,
    key2_h,
    val2_h,
    prob2_h,
    vecs,
    gb1,
    inv,
    wc_h,
    ws_h,
    ctx_h,
    key_h,
    val_h,
    prob_h,
    gup_h,
    gdn_h,
    inp,
    glat_o,
    ginp_o,
    gcross_o,
    gself_o,
    gvec_o,
    gup_o,
    gdn_o,
    dkv_h,
    w_cross,
    g_mlp,
    g_sc,
    rc,
    rb,
    ra,
    rz,
    rq,
    dwk,
    dwv,
    kt,
    vt,
    ct,
    it,
    pt,
    p1,
    ot,
    dkv,
    gbd,
    gbd_t,
    qbd_t,
    row_r,
    dqacc,
    gread,
    dq2,
    dk2,
    dv2,
    gbias,
    gvec,
    vec_in,
    vec_sum,
    c_ssem,
    c_rsem,
    b_ssem,
    b_rsem,
    a_ssem,
    a_rsem,
    z_ssem,
    z_rsem,
    v_ssem,
    v_rsem,
    tile_sem,
    load_sem,
    credit,
):
    dp, z, core, other, first, second, both, peers = neighbours(tensor_count)
    meet(dp, z, other, first, second, peers)
    shard = gcross_o.shape[0]
    quad = 4 * shard
    yy = dp // 4
    xx = lax.rem(dp // 2, 2)
    tiles = ctx_h.shape[0] // TILE
    chunk_count = 4 * tensor_count
    w_self_at = NROWS

    def mult(value, by):
        return pl.multiple_of(value, by)

    def chunk_part(chunk):
        step = chunk % tensor_count + 1
        return flipped(z, step) if step < tensor_count else z

    def own_ref(chunk):
        unit, part = chunk // tensor_count, chunk_part(chunk)
        if unit < 2:
            return g_mlp, (unit * tensor_count + part) * quad
        return g_sc, (((unit - 2) * 2 + core) * tensor_count + part) * quad

    def rows_at(start, count):
        return pl.ds(mult(start, shard), count)

    def remote(source, target, send, recv, device):
        return pltpu.make_async_remote_copy(
            src_ref=source,
            dst_ref=target,
            send_sem=send,
            recv_sem=recv,
            device_id=device,
            device_id_type=MESH,
        )

    def c_slot(chunk):
        return rc.at[chunk % 8]

    def c_whole(chunk):
        return remote(
            c_slot(chunk), c_slot(chunk), c_ssem.at[chunk], c_rsem.at[chunk], (other, z)
        )

    def c_start(chunk):
        unit, part = chunk // tensor_count, chunk_part(chunk)
        if unit < 2:
            source = (gdn_h, gup_h)[unit]
            for q in range(4):
                start = part * D + (2 * q + 1 - core) * shard
                remote(
                    source.at[rows_at(start, shard)],
                    c_slot(chunk).at[pl.ds(q * shard, shard)],
                    c_ssem.at[chunk],
                    c_rsem.at[chunk],
                    (other, z),
                ).start()
        else:
            start = (((unit - 2) * 2 + 1 - core) * tensor_count + part) * quad
            remote(
                g_sc.at[rows_at(start, quad)],
                c_slot(chunk),
                c_ssem.at[chunk],
                c_rsem.at[chunk],
                (other, z),
            ).start()

    by_z = [unit * tensor_count for unit in Z_UNITS_BACK]

    in_plane = [chunk for chunk in range(chunk_count) if chunk not in by_z]

    def b_copy(chunk, half):
        ref, base = own_ref(chunk)
        q = (1 - core) * ((1 - yy) * 2 + half) + core * (half * 2 + 1 - xx)
        number = chunk * 2 + half
        return remote(
            ref.at[rows_at(base + q * shard, shard)],
            rb.at[in_plane.index(chunk), half],
            b_ssem.at[number],
            b_rsem.at[number],
            (second, z),
        )

    def a_copy(chunk):
        ref, base = own_ref(chunk)
        q = (1 - core) * (yy * 2 + 1 - xx) + core * ((1 - yy) * 2 + xx)
        return remote(
            ref.at[rows_at(base + q * shard, shard)],
            ra.at[in_plane.index(chunk)],
            a_ssem.at[chunk],
            a_rsem.at[chunk],
            (first, z),
        )

    def z_copy(chunk):
        unit, step = divmod(chunk, tensor_count)
        ref, base = own_ref(chunk)
        number = unit * (tensor_count - 1) + step
        if chunk in by_z:
            return remote(
                ref.at[rows_at(base, quad)],
                rq.at[by_z.index(chunk)],
                z_ssem.at[number],
                z_rsem.at[number],
                (dp, peers[0]),
            )
        return remote(
            ref.at[rows_at(base + (yy * 2 + xx) * shard, shard)],
            rz.at[number],
            z_ssem.at[number],
            z_rsem.at[number],
            (dp, peers[step]),
        )

    piece = 32

    def add_rows(ref, start, source, count):
        def body(index, carry):
            rows = pl.ds(mult(start + index * piece, piece), piece)
            part = source[pl.ds(mult(index * piece, piece), piece), :]
            ref[rows, :] = (ref[rows, :].astype(F32) + part.astype(F32)).astype(BF)
            return carry

        lax.fori_loop(0, count // piece, body, 0)

    def stage1(chunk):
        c_whole(chunk).wait_recv()
        ref, base = own_ref(chunk)
        add_rows(ref, base, c_slot(chunk), quad)
        if chunk in (3, 7):
            pl.semaphore_signal(
                credit, inc=1, device_id=(other, z), device_id_type=MESH
            )
        if chunk in by_z:
            z_copy(chunk).start()
            return
        whole = chunk - (tensor_count - 1)
        if whole in by_z:
            z_copy(whole).wait_recv()
            add_rows(ref, base, rq.at[by_z.index(whole)], quad)
        for half in range(2):
            b_copy(chunk, half).start()

    def stage2(chunk):
        ref, base = own_ref(chunk)
        for half in range(2):
            b_copy(chunk, half).wait_recv()
            q = (1 - core) * (yy * 2 + half) + core * (half * 2 + xx)
            add_rows(ref, base + q * shard, rb.at[in_plane.index(chunk), half], shard)
        a_copy(chunk).start()

    def stage3(chunk):
        a_copy(chunk).wait_recv()
        ref, base = own_ref(chunk)
        add_rows(ref, base + (yy * 2 + xx) * shard, ra.at[in_plane.index(chunk)], shard)
        if chunk % tensor_count < tensor_count - 1:
            z_copy(chunk).start()

    def finish(unit):
        chunk = unit * tensor_count + tensor_count - 1
        ref, base = own_ref(chunk)
        target = (gdn_o, gup_o, gself_o, gcross_o)[unit]
        steps = range(1 if unit in Z_UNITS_BACK else 0, tensor_count - 1)
        for step in steps:
            z_copy(unit * tensor_count + step).wait_recv()

        def body(index, carry):
            rows = pl.ds(mult(index * piece, piece), piece)
            start = base + (yy * 2 + xx) * shard + index * piece
            total = ref[pl.ds(mult(start, piece), piece), :].astype(F32)
            for step in steps:
                total = total + rz[unit * (tensor_count - 1) + step, rows, :].astype(F32)
            target[rows, :] = total
            return carry

        lax.fori_loop(0, shard // piece, body, 0)

    def vec_copy(hop):
        if hop < 3:
            source, device = vec_sum.at[hop], ((other, second, first)[hop], z)
        else:
            source, device = vec_sum.at[3], (dp, peers[hop - 3])
        return remote(source, vec_in.at[hop], v_ssem.at[hop], v_rsem.at[hop], device)

    def vec_step(step):
        if step == 0:
            vec_sum[0] = gvec[...]
        elif step <= 3:
            vec_copy(step - 1).wait_recv()
            vec_sum[step] = vec_sum[step - 1] + vec_in[step - 1]
        if step < 3:
            vec_copy(step).start()
        elif step == 3:
            for hop in range(3, 2 + tensor_count):
                vec_copy(hop).start()
        else:
            total = vec_sum[3]
            for hop in range(3, 2 + tensor_count):
                vec_copy(hop).wait_recv()
                total = total + vec_in[hop]
            width = gvec_o.shape[1]
            turn = lax.rem(D - (dp * tensor_count + z) * width, D)
            gvec_o[...] = pltpu.roll(total, turn, 1)[0 : gvec_o.shape[0], 0:width]

    stages = (stage1, stage2, stage3, finish, vec_step)

    def run_at(name):
        for stage, chunk in SCATTER_PLAN.get(name, ()):
            stages[stage](chunk)

    def run_each(name, index, count):
        for number in range(count):
            if SCATTER_PLAN.get(name + str(number)):
                pl.when(index == number)(partial(run_at, name + str(number)))

    def send_unit(unit):
        pl.semaphore_wait(credit, 1)
        for chunk in range(unit * tensor_count, (unit + 1) * tensor_count):
            c_start(chunk)

    def store_grad(unit, block, values):
        for part in range(8):
            parity, zpart = divmod(part, tensor_count)
            start = (((unit * 2 + parity) * tensor_count + zpart) * 4 + block) * shard
            g_sc[start : start + shard, :] = values[part * shard : (part + 1) * shard].astype(BF)

    def load(source, target, number):
        return pltpu.make_async_copy(source, target, load_sem.at[number])

    w_self = g_sc.at[pl.ds(w_self_at, NROWS)]
    for chunk in range(2 * tensor_count):
        c_start(chunk)
    for unit in range(2):
        source = (gdn_h, gup_h)[unit]
        for part in range(tensor_count):
            for q in range(4):
                pltpu.make_async_copy(
                    source.at[rows_at(part * D + (2 * q + core) * shard, shard)],
                    g_mlp.at[pl.ds(((unit * tensor_count + part) * 4 + q) * shard, shard)],
                    load_sem.at[1 + unit],
                ).start()
    lat_rows = 2 * LAT
    late, gn3, read2 = (dwk.at[pl.ds(third * lat_rows, lat_rows)] for third in range(3))
    read, mid, lat = (dwv.at[pl.ds(third * lat_rows, lat_rows)] for third in range(3))
    prob2 = pt.at[:, :, :, pl.ds(0, LAT)]
    early = [
        (cot_h, glat_o),
        (late_h, late),
        (gn3_h, gn3),
        (read2_h, read2),
        (read_h, read),
        (mid_h, mid),
        (prob2_h, prob2),
        (query2_h, kt.at[0]),
        (key2_h, kt.at[1]),
        (val2_h, vt.at[0]),
        (query_h, vt.at[1]),
    ]
    query2, key2, val2, query = kt.at[0], kt.at[1], vt.at[0], vt.at[1]
    for number, (source, target) in enumerate(early):
        load(source, target, 5 + number).start()
    load(ws_h, w_self, 0).start()
    load(wc_h, w_cross, 3).start()

    def load_p1(extra):
        return load(prob_h.at[:, :, pl.ds((tiles + extra) * TILE, TILE)], p1, 4)

    load_p1(0).start()
    half_mlp = tensor_count * quad
    for unit in range(2):
        whole = g_mlp.at[pl.ds(unit * half_mlp, half_mlp)]
        load(whole, whole, 1 + unit).wait()

    def vec(row):
        return vecs[row : row + 1, :]

    mask = head_mask(GHEADS * LAT)
    mask_t = head_mask_t(GHEADS * LAT)
    gvec[...] = jnp.zeros(gvec.shape, F32)

    def note(row, values):
        gvec[row : row + 1, :] = values

    def col_sum(values):
        return jnp.sum(values.astype(F32), axis=0, keepdims=True)

    def row_terms(grad_block, read_block):
        wide = jnp.concatenate([grad_block.astype(F32) * read_block] * GHEADS, axis=0)
        return jnp.sum(jnp.where(mask, wide, 0.0), axis=1, keepdims=True)

    run_at("a")
    for number, (source, target) in enumerate(early):
        load(source, target, 5 + number).wait()
    note(14, col_sum(glat_o[...].astype(BF)))
    gvec[15 : 15 + tensor_count, :] = gb1[0:tensor_count, :]
    back, gain, shift = ln_back(late[...], vec(12), gn3[...])
    note(12, gain)
    note(13, shift)
    gas = glat_o[...] + back
    glat_o[...] = gas
    grad_out = gas.astype(BF)
    note(11, col_sum(grad_out))
    load(ws_h, w_self, 0).wait()

    def self_block(block):
        return g_sc[w_self_at + block * D : w_self_at + (block + 1) * D, :]

    run_at("b")
    store_grad(0, 3, nn(read2[...].T.astype(BF), grad_out))
    gread[...] = nt(grad_out, self_block(3)).astype(BF)
    run_at("c")
    for slot in range(2):
        srows = slice(slot * LAT, (slot + 1) * LAT)
        for group in range(GROUPS):
            gcols = slice(group * GROUP, (group + 1) * GROUP)
            grads = spread_heads(gread[srows, gcols], mask)
            inner = row_terms(gread[srows, gcols], read2[srows, gcols])
            chance = prob2[slot, group]
            dprob = nt(grads, val2[srows, gcols])
            dscore = (chance.astype(F32) * (dprob - inner)).astype(BF)
            dq2[srows, gcols] = (
                pick_heads(nn(dscore, key2[srows, gcols])) * HEAD_DIM ** (-0.5)
            ).astype(BF)
            wide = spread_heads(query2[srows, gcols], mask)
            dk2[srows, gcols] = tn(dscore, wide).astype(BF)
            dv2[srows, gcols] = tn(chance, grads).astype(BF)
    run_at("d")
    note(9, col_sum(dq2[...]))
    note(10, col_sum(dv2[...]))
    unit_two, scale_two = ln_parts(mid[...])
    norm_t = (unit_two * vec(7) + vec(8)).T.astype(BF)
    store_grad(0, 0, nn(norm_t, dq2[...]))
    store_grad(0, 1, nn(norm_t, dk2[...]))
    store_grad(0, 2, nn(norm_t, dv2[...]))
    incoming = nt(dq2[...], self_block(0)) + nt(dk2[...], self_block(1))
    incoming = incoming + nt(dv2[...], self_block(2))
    back, gain, shift = ln_back(mid[...], vec(7), incoming)
    note(7, gain)
    note(8, shift)
    total = glat_o[...] + back
    glat_o[...] = total
    run_at("CS2")
    send_unit(2)
    run_at("e")
    grad_out = total.astype(BF)
    note(6, col_sum(grad_out))
    load(wc_h, w_cross, 3).wait()
    store_grad(1, 3, nn(read[...].T.astype(BF), grad_out))
    gread[...] = nt(grad_out, w_cross[3 * D :, :]).astype(BF)
    run_at("f")
    for slot in range(2):
        srows = slice(slot * LAT, (slot + 1) * LAT)
        for group in range(GROUPS):
            gcols = slice(group * GROUP, (group + 1) * GROUP)
            at = slot * GROUPS + group
            grads = gread[srows, gcols].astype(F32) * inv[srows, gcols]
            gbd[at] = spread_heads(grads, mask)
            gbd_t[at] = spread_columns(grads, mask_t)
            qbd_t[at] = spread_columns(query[srows, gcols].astype(F32), mask_t)
            inner = row_terms(grads, read[srows, gcols])
            row_r[at] = jnp.broadcast_to(inner, (GHEADS * LAT, LANES))
    dqacc[...] = jnp.zeros(dqacc.shape, F32)
    dwk[...] = jnp.zeros(dwk.shape, F32)
    dwv[...] = jnp.zeros(dwv.shape, F32)
    gbias[...] = jnp.zeros(gbias.shape, F32)
    it[0] = jnp.zeros(it.shape[1:], BF)

    def fetches(index):
        slot = lax.rem(index, 2)
        rows = pl.ds(mult(index * TILE, TILE), TILE)
        copies = [
            (key_h.at[rows], kt.at[slot]),
            (val_h.at[rows], vt.at[slot]),
            (ctx_h.at[rows], ct.at[slot]),
            (prob_h.at[:, :, rows], pt.at[slot]),
        ]
        return [
            pltpu.make_async_copy(source, target, tile_sem.at[slot, number])
            for number, (source, target) in enumerate(copies)
        ]

    def spill(index):
        slot = lax.rem(index, 2)
        return pltpu.make_async_copy(dkv.at[slot], dkv_h.at[index], tile_sem.at[slot, 4])

    for copy in fetches(jnp.int32(0)):
        copy.start()

    def attend_back(slot, chance_of, buffer, first_time):
        for group in range(GROUPS):
            gcols = slice(group * GROUP, (group + 1) * GROUP)
            at = slot * GROUPS + group
            chance = chance_of(group)
            dprob = nt(gbd[at], vt[buffer, :, gcols])
            inner = row_r[at]
            dscore = chance.astype(F32) * (dprob - jnp.concatenate([inner, inner], axis=1))
            dscore = dscore.astype(BF)
            dk_part = nn(qbd_t[at], dscore)
            dv_part = nn(gbd_t[at], chance)
            if not first_time:
                dk_part = dk_part + dkv[buffer, 0, gcols, :].astype(F32)
                dv_part = dv_part + dkv[buffer, 1, gcols, :].astype(F32)
            dkv[buffer, 0, gcols, :] = dk_part.astype(BF)
            dkv[buffer, 1, gcols, :] = dv_part.astype(BF)
            dqacc[at] += nn(dscore, kt[buffer, :, gcols])

    def tile_body(index, carry):
        buffer = lax.rem(index, 2)

        @pl.when(index + 1 < tiles)
        def _():
            for copy in fetches(index + 1):
                copy.start()

        run_each("t", index, tiles)

        @pl.when(index > 1)
        def _():
            spill(index - 2).wait()

        for copy in fetches(index):
            copy.wait()
        attend_back(0, lambda group: pt[buffer, group], buffer, True)
        for extra in range(SLOT1_TILES):

            @pl.when(index == SLOT1_FIRST + extra)
            def _():
                load_p1(extra).wait()
                attend_back(1, lambda group: p1[group], buffer, False)
                if extra + 1 < SLOT1_TILES:
                    load_p1(extra + 1).start()

        spill(index).start()
        dk = dkv[buffer, 0]
        dv = dkv[buffer, 1]
        gbias[...] += dv[:, :LANES].astype(F32) + dv[:, LANES:].astype(F32)
        block = ct[buffer]
        dwk[...] += nn(dk, block)
        dwv[...] += nn(dv, block)

        return carry

    lax.fori_loop(0, tiles, tile_body, 0)
    run_at("g")
    row = lax.broadcasted_iota(jnp.int32, (D, D), 0)
    col = lax.broadcasted_iota(jnp.int32, (D, D), 1)
    unity = jnp.where(row == col, 1.0, 0.0).astype(BF)
    store_grad(1, 2, nt(unity, dwv[...].astype(BF)))
    load(lat_h, lat, 16).start()
    store_grad(1, 1, nt(unity, dwk[...].astype(BF)))
    for slot in range(2):
        srows = slice(slot * LAT, (slot + 1) * LAT)
        for group in range(GROUPS):
            gcols = slice(group * GROUP, (group + 1) * GROUP)
            dq2[srows, gcols] = (
                pick_heads(dqacc[slot * GROUPS + group]) * HEAD_DIM ** (-0.5)
            ).astype(BF)
    load(lat_h, lat, 16).wait()
    unit_one, scale_one = ln_parts(lat[...])
    norm_t = (unit_one * vec(0) + vec(1)).T.astype(BF)
    store_grad(1, 0, nn(norm_t, dq2[...]))
    run_at("CS3")
    send_unit(3)
    spill(tiles - 2).wait()
    spill(tiles - 1).wait()

    def fetch_back(index, at_start):
        slot = 0 if at_start else lax.rem(index, 2)
        back_rows = inp.at[pl.ds(0, TILE - PAD)]
        target = it.at[0, pl.ds(PAD, TILE - PAD)]
        if not at_start:
            back_rows = inp.at[pl.ds(mult(index * TILE - PAD, PAD), TILE)]
            target = it.at[slot]
        tile = 0 if at_start else index
        return [
            pltpu.make_async_copy(back_rows, target, tile_sem.at[slot, 0]),
            pltpu.make_async_copy(dkv_h.at[tile], dkv.at[slot], tile_sem.at[slot, 1]),
        ]

    def put(index, at_start):
        slot = 0 if at_start else lax.rem(index, 2)
        if at_start:
            source, rows = ot.at[0, pl.ds(PAD, TILE - PAD)], pl.ds(0, TILE - PAD)
        else:
            source, rows = ot.at[slot], pl.ds(mult(index * TILE - PAD, PAD), TILE)
        return pltpu.make_async_copy(source, ginp_o.at[rows], tile_sem.at[slot, 5])

    for copy in fetch_back(0, True):
        copy.start()

    def token_body(index, carry):
        buffer = lax.rem(index, 2)

        @pl.when(index + 1 < tiles)
        def _():
            for copy in fetch_back(index + 1, False):
                copy.start()

        @pl.when(index == 0)
        def _():
            for copy in fetch_back(0, True):
                copy.wait()

        @pl.when(index > 0)
        def _():
            for copy in fetch_back(index, False):
                copy.wait()

        run_each("u", index, tiles)
        incoming = nn(w_cross[D : 2 * D, :], dkv[buffer, 0])
        incoming = incoming + nn(w_cross[2 * D : 3 * D, :], dkv[buffer, 1])
        back, gain, shift = ln_back(it[buffer].astype(F32), vec(2), incoming.T)
        gvec[2:3, :] += gain
        gvec[3:4, :] += shift

        @pl.when(index == 2)
        def _():
            put(0, True).wait()

        @pl.when(index > 2)
        def _():
            put(index - 2, False).wait()

        ot[buffer] = back.astype(BF)

        @pl.when(index == 0)
        def _():
            put(0, True).start()

        @pl.when(index > 0)
        def _():
            put(index, False).start()

        return carry

    lax.fori_loop(0, tiles, token_body, 0)
    run_at("h")
    note(4, col_sum(dq2[...]))
    note(5, jnp.sum(gbias[...].T, axis=0, keepdims=True))
    incoming = nt(dq2[...], w_cross[0:D, :])
    back, gain, shift = ln_back(lat[...], vec(0), incoming)
    note(0, gain)
    note(1, shift)
    glat_o[...] = glat_o[...] + back

    run_at("end")
    put(tiles - 2, False).wait()
    put(tiles - 1, False).wait()
    for hop in range(2 + tensor_count):
        vec_copy(hop).wait_send()
    for chunk in range(chunk_count):
        c_whole(chunk).wait_send()
        if chunk not in by_z:
            b_copy(chunk, 0).wait_send()
            b_copy(chunk, 1).wait_send()
            a_copy(chunk).wait_send()
        if chunk % tensor_count < tensor_count - 1:
            z_copy(chunk).wait_send()


def backward_call(tensor_count, shard, vec_shape, operands):
    sds = jax.ShapeDtypeStruct
    hbm = pl.BlockSpec(memory_space=pl.ANY)
    vmem = pl.BlockSpec(memory_space=pltpu.VMEM)
    rows = operands[0].shape[0]
    inp = operands[-1]
    stacked = GHEADS * LAT
    chunks = 4 * tensor_count
    zs = 4 * (tensor_count - 1)
    at = 2 * GROUPS
    sem = pltpu.SemaphoreType.DMA
    outs = [
        (sds((rows, D), F32), vmem),
        (sds(inp.shape, BF), hbm),
        (sds((shard, D), F32), vmem),
        (sds((shard, D), F32), vmem),
        (sds(vec_shape, F32), vmem),
        (sds((shard, D), F32), vmem),
        (sds((shard, D), F32), vmem),
        (sds(((inp.shape[0] + PAD) // TILE, 2, D, TILE), BF), hbm),
    ]
    return pl.pallas_call(
        partial(backward_kernel, tensor_count),
        out_shape=[shape for shape, spec in outs],
        out_specs=[spec for shape, spec in outs],
        in_specs=[hbm] * 12 + [vmem] * 3 + [hbm] * 9,
        scratch_shapes=[
            pltpu.VMEM((NROWS, D), BF),
            pltpu.VMEM((NROWS, D), BF),
            pltpu.VMEM((2 * NROWS, D), BF),
            pltpu.VMEM((8, 4 * shard, D), BF),
            pltpu.VMEM((chunks - len(Z_UNITS_BACK), 2, shard, D), BF),
            pltpu.VMEM((chunks - len(Z_UNITS_BACK), shard, D), BF),
            pltpu.VMEM((zs, shard, D), BF),
            pltpu.VMEM((len(Z_UNITS_BACK), 4 * shard, D), BF),
            pltpu.VMEM((D, D), F32),
            pltpu.VMEM((D, D), F32),
            pltpu.VMEM((2, TILE, D), BF),
            pltpu.VMEM((2, TILE, D), BF),
            pltpu.VMEM((2, TILE, D), BF),
            pltpu.VMEM((2, TILE, D), BF),
            pltpu.VMEM((2, GROUPS, stacked, TILE), BF),
            pltpu.VMEM((GROUPS, stacked, TILE), BF),
            pltpu.VMEM((2, TILE, D), BF),
            pltpu.VMEM((2, 2, D, TILE), BF),
            pltpu.VMEM((at, stacked, GROUP), BF),
            pltpu.VMEM((at, GROUP, stacked), BF),
            pltpu.VMEM((at, GROUP, stacked), BF),
            pltpu.VMEM((at, stacked, LANES), F32),
            pltpu.VMEM((at, stacked, GROUP), F32),
            pltpu.VMEM((rows, D), BF),
            pltpu.VMEM((rows, D), BF),
            pltpu.VMEM((rows, D), BF),
            pltpu.VMEM((rows, D), BF),
            pltpu.VMEM((D, LANES), F32),
            pltpu.VMEM((VEC_TOP, D), F32),
            pltpu.VMEM((2 + tensor_count, VEC_TOP, D), F32),
            pltpu.VMEM((4, VEC_TOP, D), F32),
            sem((chunks,)),
            sem((chunks,)),
            sem((2 * chunks,)),
            sem((2 * chunks,)),
            sem((chunks,)),
            sem((chunks,)),
            sem((zs,)),
            sem((zs,)),
            sem((2 + tensor_count,)),
            sem((2 + tensor_count,)),
            sem((2, 6)),
            sem((17,)),
            pltpu.SemaphoreType.REGULAR,
        ],
        compiler_params=pltpu.CompilerParams(
            collective_id=1, has_side_effects=True, vmem_limit_bytes=VMEM_LIMIT
        ),
        name="backward_scatter",
    )(*operands)


def copy_kernel(count, *refs):
    sources, targets = refs[:count], refs[count : 2 * count]
    buffers, (load_sem, store_sem) = refs[2 * count : 3 * count], refs[3 * count :]
    loads, stores = [], []
    for source, target, buffer in zip(sources, targets, buffers):
        rows = source.shape[0]
        pieces = 10 if rows >= 1024 else 1
        for piece in range(pieces):
            part = pl.ds(piece * (rows // pieces), rows // pieces)
            number = len(loads)
            loads.append(
                pltpu.make_async_copy(source.at[part], buffer.at[part], load_sem.at[number])
            )
            stores.append(
                pltpu.make_async_copy(buffer.at[part], target.at[part], store_sem.at[number])
            )
    for copy in loads:
        copy.start()
    for load, store in zip(loads, stores):
        load.wait()
        store.start()
    for copy in stores:
        copy.wait()


def hand_out(arrays):
    count = len(arrays)
    hbm = pl.BlockSpec(memory_space=pl.ANY)
    return pl.pallas_call(
        partial(copy_kernel, count),
        out_shape=[jax.ShapeDtypeStruct(array.shape, array.dtype) for array in arrays],
        in_specs=[hbm] * count,
        out_specs=[hbm] * count,
        scratch_shapes=[pltpu.VMEM(array.shape, array.dtype) for array in arrays]
        + [pltpu.SemaphoreType.DMA((10 + count,))] * 2,
        name="hand_out",
    )(*arrays)


def local_fused(
    latents,
    inputs,
    segment,
    cross_weights,
    self_weights,
    vectors,
    up_weight,
    down_weight,
    cotangent,
):
    tensor_count = lax.axis_size("tensor")
    shard = cross_weights.shape[0]
    seg = segment.reshape(-1, LANES)
    (
        latents_out,
        wc,
        ws,
        ctx,
        keys,
        vals,
        prob,
        gup,
        gdn,
        vecs,
        query,
        read,
        mid,
        query2,
        key2,
        val2,
        prob2,
        read2,
        late,
        gn3,
        gb1,
        inv,
    ) = forward_call(
        tensor_count,
        latents,
        inputs,
        seg,
        cross_weights,
        self_weights,
        up_weight,
        down_weight.T,
        vectors,
        cotangent,
    )
    operands = [latents, cotangent, mid, late, gn3, read, read2, query, query2, key2, val2]
    operands += [prob2, vecs, gb1, inv, wc, ws, ctx, keys, vals, prob, gup, gdn, inputs]
    glat, ginp, gcross, gself, gvec, gup_sum, gdn_sum, unused = backward_call(
        tensor_count, shard, vectors.shape, operands
    )
    results = hand_out([latents_out, glat, ginp, gcross, gself, gvec, gup_sum, gdn_sum])
    return (*results[:7], results[7].T)


def solution(mesh):
    placed = (
        P(("dp", "tensor"), None),
        P(("dp", "tensor"), None),
        P(("dp", "tensor")),
        P(("dp", "tensor"), None),
        P(("dp", "tensor"), None),
        P(None, ("dp", "tensor")),
        P("dp", "tensor"),
        P("tensor", "dp"),
        P(("dp", "tensor"), None),
    )
    shards = mesh.shape["dp"] * mesh.shape["tensor"]
    fused = mesh.shape["dp"] == 8 and mesh.shape["tensor"] == 4 and 4 * D % (32 * shards) == 0
    return jax.shard_map(
        local_fused if fused else local,
        mesh=mesh,
        in_specs=placed,
        out_specs=(
            P(("dp", "tensor"), None),
            P(("dp", "tensor"), None),
            P(("dp", "tensor"), None),
            P(("dp", "tensor"), None),
            P(("dp", "tensor"), None),
            P(None, ("dp", "tensor")),
            P("dp", "tensor"),
            P("tensor", "dp"),
        ),
        check_vma=False,
    )
```

```python
from functools import partial

import jax
import jax.numpy as jnp
from jax import lax
from jax.experimental import pallas as pl
from jax.experimental.pallas import tpu as pltpu
from jax.sharding import PartitionSpec as P

D = 768
HEAD_DIM = 64
FF = 3072
LAT = 128


def cut_along(x, dim, size):
    before, after = (x.shape[:dim], x.shape[dim + 1 :])
    return jnp.moveaxis(x.reshape(*before, size, -1, *after), dim, 0)


def sent_and_summed(x, axis, dim):
    parts = cut_along(x, dim, lax.axis_size(axis))
    arrived = lax.all_to_all(parts, axis, split_axis=0, concat_axis=0, tiled=True)
    return arrived.astype(jnp.float32).sum(axis=0)


def product(left, right):
    return jnp.dot(left, right, preferred_element_type=jnp.float32)


def product_tn(left, right):
    return lax.dot_general(
        left, right, (((0,), (0,)), ((), ())), preferred_element_type=jnp.float32
    )


def product_nt(left, right):
    return lax.dot_general(
        left, right, (((1,), (1,)), ((), ())), preferred_element_type=jnp.float32
    )


def layer_norm(values, gain_row, shift_row):
    average = jnp.mean(values, axis=-1, keepdims=True)
    centred = values - average
    variance = jnp.mean(centred * centred, axis=-1, keepdims=True)
    return centred * lax.rsqrt(variance + 1e-05) * gain_row + shift_row


def norm_backward(values, gain_row, shift_row, incoming):
    unused, pullback = jax.vjp(layer_norm, values, gain_row, shift_row)
    return pullback(incoming)


def split_heads(values):
    return values.reshape(values.shape[0], -1, HEAD_DIM).transpose(1, 0, 2)


def merge_heads(values):
    return values.transpose(1, 0, 2).reshape(values.shape[1], -1)


def head_probs(head_query, head_key, visible, peak_score, denominator):
    scores = product_nt(head_query, head_key) * HEAD_DIM ** (-0.5)
    exponent = jnp.exp(jnp.where(visible, scores - peak_score, -200.0)) * visible.astype(
        jnp.float32
    )
    return exponent / denominator


def attend_forward(queries, keys_in, values_in, visible):
    has_keys = jnp.any(visible, axis=-1, keepdims=True)
    seen_float = visible.astype(jnp.float32)

    def one_head(operands):
        head_query, head_key, head_value = operands
        scores = product_nt(head_query, head_key) * HEAD_DIM ** (-0.5)
        peak_score = jnp.max(jnp.where(visible, scores, -1000000000.0), axis=-1, keepdims=True)
        peak_score = jnp.where(has_keys, peak_score, 0.0)
        exponent = jnp.exp(jnp.where(visible, scores - peak_score, -200.0)) * seen_float
        denominator = jnp.sum(exponent, axis=-1, keepdims=True) + 1.0 - has_keys.astype(jnp.float32)
        attn_probs = (exponent / denominator).astype(jnp.bfloat16)
        return (product(attn_probs, head_value), peak_score, denominator)

    outputs, peaks, denominators = lax.map(
        one_head, (split_heads(queries), split_heads(keys_in), split_heads(values_in))
    )
    return (merge_heads(outputs).astype(jnp.bfloat16), peaks, denominators)


def attend_backward(queries, keys_in, values_in, visible, peaks, denominators, grad_read):
    score_scale = HEAD_DIM ** (-0.5)

    def one_head(operands):
        head_query, head_key, head_value, peak_score, denominator, head_grad = operands
        attn_probs = head_probs(head_query, head_key, visible, peak_score, denominator)
        grad_probs = product_nt(head_grad, head_value)
        grad_value = product_tn(attn_probs.astype(jnp.bfloat16), head_grad)
        inner_sum = jnp.sum(grad_probs * attn_probs, axis=-1, keepdims=True)
        grad_scores = (attn_probs * (grad_probs - inner_sum)).astype(jnp.bfloat16)
        grad_query = product(grad_scores, head_key) * score_scale
        grad_key = product_tn(grad_scores, head_query) * score_scale
        return (grad_query, grad_key, grad_value)

    grad_q, grad_k, grad_v = lax.map(
        one_head,
        (
            split_heads(queries),
            split_heads(keys_in),
            split_heads(values_in),
            peaks,
            denominators,
            split_heads(grad_read),
        ),
    )
    return (
        merge_heads(grad_q).astype(jnp.bfloat16),
        merge_heads(grad_k).astype(jnp.bfloat16),
        merge_heads(grad_v).astype(jnp.bfloat16),
    )


def column_sum(values):
    return jnp.sum(values.astype(jnp.float32), axis=0)


def local(
    latents,
    inputs,
    segment,
    cross_weights,
    self_weights,
    vectors,
    up_weight,
    down_weight,
    cotangent,
):
    cross_full, self_full, vector_half = (
        lax.all_gather(cross_weights, ("dp", "tensor"), axis=0, tiled=True),
        lax.all_gather(self_weights, ("dp", "tensor"), axis=0, tiled=True),
        lax.all_gather(vectors, ("dp", "tensor"), axis=1, tiled=True),
    )
    up_full, down_full = (
        lax.all_gather(up_weight, "dp", axis=0, tiled=True),
        lax.all_gather(down_weight, "dp", axis=1, tiled=True),
    )
    vector_rows = vector_half.astype(jnp.float32)
    quarter = up_full.shape[1]
    part_index = lax.axis_index("tensor")
    bias_up = lax.dynamic_slice_in_dim(
        vector_rows[15:].reshape(-1), part_index * quarter, quarter, 0
    )
    row_count = latents.shape[0]
    slot_row = jnp.arange(row_count, dtype=jnp.int32) // LAT
    cross_seen = slot_row[:, None] == segment[None, :]
    self_seen = slot_row[:, None] == slot_row[None, :]
    input_float = inputs.astype(jnp.float32)
    normed = layer_norm(latents, vector_rows[0], vector_rows[1]).astype(jnp.bfloat16)
    context = layer_norm(input_float, vector_rows[2], vector_rows[3]).astype(jnp.bfloat16)
    queries = (product(normed, cross_full[:D]) + vector_rows[4]).astype(jnp.bfloat16)
    keys_in = product(context, cross_full[D : 2 * D]).astype(jnp.bfloat16)
    values_in = (product(context, cross_full[2 * D : 3 * D]) + vector_rows[5]).astype(jnp.bfloat16)
    cross_read, cross_peaks, cross_denoms = attend_forward(queries, keys_in, values_in, cross_seen)
    after_cross = latents + (product(cross_read, cross_full[3 * D :]) + vector_rows[6])
    normed_two = layer_norm(after_cross, vector_rows[7], vector_rows[8]).astype(jnp.bfloat16)
    queries_two = (product(normed_two, self_full[:D]) + vector_rows[9]).astype(jnp.bfloat16)
    keys_two = product(normed_two, self_full[D : 2 * D]).astype(jnp.bfloat16)
    values_two = (product(normed_two, self_full[2 * D : 3 * D]) + vector_rows[10]).astype(
        jnp.bfloat16
    )
    self_read, self_peaks, self_denoms = attend_forward(
        queries_two, keys_two, values_two, self_seen
    )
    after_self = after_cross + (product(self_read, self_full[3 * D :]) + vector_rows[11])
    normed_three = layer_norm(after_self, vector_rows[12], vector_rows[13]).astype(jnp.bfloat16)
    gathered = lax.all_gather(normed_three, "tensor", axis=0, tiled=True)
    pre_act = product(gathered, up_full) + bias_up
    hidden = jax.nn.gelu(pre_act, approximate=False).astype(jnp.bfloat16)
    reduced = lax.psum_scatter(
        product(hidden, down_full).astype(jnp.bfloat16), "tensor", scatter_dimension=0, tiled=True
    ).astype(jnp.float32)
    latents_out = after_self + (reduced + vector_rows[14])
    cross_full, self_full, vector_half = (
        lax.all_gather(cross_weights, ("dp", "tensor"), axis=0, tiled=True),
        lax.all_gather(self_weights, ("dp", "tensor"), axis=0, tiled=True),
        lax.all_gather(vectors, ("dp", "tensor"), axis=1, tiled=True),
    )
    up_full, down_full = (
        lax.all_gather(up_weight, "dp", axis=0, tiled=True),
        lax.all_gather(down_weight, "dp", axis=1, tiled=True),
    )
    vector_rows = vector_half.astype(jnp.float32)
    grad_y = cotangent.astype(jnp.bfloat16)
    grad_b2 = column_sum(grad_y)
    grad_rows = lax.all_gather(grad_y, "tensor", axis=0, tiled=True)
    grad_down = product_tn(hidden, grad_rows)
    grad_hidden = product_nt(grad_rows, down_full)
    unused, gelu_pull = jax.vjp(partial(jax.nn.gelu, approximate=False), pre_act)
    grad_pre = gelu_pull(grad_hidden)[0].astype(jnp.bfloat16)
    grad_b1 = column_sum(grad_pre)
    grad_up = product_tn(gathered, grad_pre)
    mlp_sums = (
        sent_and_summed(grad_up.astype(jnp.bfloat16), "dp", 0),
        sent_and_summed(grad_down.astype(jnp.bfloat16), "dp", 1),
    )
    grad_normed_three = lax.psum_scatter(
        product_nt(grad_pre, up_full).astype(jnp.bfloat16),
        "tensor",
        scatter_dimension=0,
        tiled=True,
    ).astype(jnp.float32)
    back_self, grad_gain_three, grad_shift_three = norm_backward(
        after_self, vector_rows[12], vector_rows[13], grad_normed_three
    )
    grad_after_self = cotangent + back_self
    grad_out_two = grad_after_self.astype(jnp.bfloat16)
    grad_bias_out_two = column_sum(grad_out_two)
    grad_wo_two = product_tn(self_read, grad_out_two)
    grad_read_two = product_nt(grad_out_two, self_full[3 * D :]).astype(jnp.bfloat16)
    grad_q_two, grad_k_two, grad_v_two = attend_backward(
        queries_two, keys_two, values_two, self_seen, self_peaks, self_denoms, grad_read_two
    )
    grad_self = jnp.concatenate(
        [
            product_tn(normed_two, grad_q_two),
            product_tn(normed_two, grad_k_two),
            product_tn(normed_two, grad_v_two),
            grad_wo_two,
        ],
        axis=0,
    )
    grad_normed_two = (
        product_nt(grad_q_two, self_full[:D])
        + product_nt(grad_k_two, self_full[D : 2 * D])
        + product_nt(grad_v_two, self_full[2 * D : 3 * D])
    )
    back_cross, grad_gain_two, grad_shift_two = norm_backward(
        after_cross, vector_rows[7], vector_rows[8], grad_normed_two
    )
    grad_after_cross = grad_after_self + back_cross
    grad_out_one = grad_after_cross.astype(jnp.bfloat16)
    grad_bias_out_one = column_sum(grad_out_one)
    grad_wo_one = product_tn(cross_read, grad_out_one)
    grad_read_one = product_nt(grad_out_one, cross_full[3 * D :]).astype(jnp.bfloat16)
    grad_q_one, grad_k_one, grad_v_one = attend_backward(
        queries, keys_in, values_in, cross_seen, cross_peaks, cross_denoms, grad_read_one
    )
    grad_cross = jnp.concatenate(
        [
            product_tn(normed, grad_q_one),
            product_tn(context, grad_k_one),
            product_tn(context, grad_v_one),
            grad_wo_one,
        ],
        axis=0,
    )
    grad_normed = product_nt(grad_q_one, cross_full[:D])
    back_latent, grad_gain_one, grad_shift_one = norm_backward(
        latents, vector_rows[0], vector_rows[1], grad_normed
    )
    grad_latents = grad_after_cross + back_latent
    grad_context = product_nt(grad_k_one, cross_full[D : 2 * D]) + product_nt(
        grad_v_one, cross_full[2 * D : 3 * D]
    )
    back_input, grad_gain_input, grad_shift_input = norm_backward(
        input_float, vector_rows[2], vector_rows[3], grad_context
    )
    grad_inputs = back_input.astype(jnp.bfloat16)
    full_bias = lax.dynamic_update_slice_in_dim(
        jnp.zeros((FF,), jnp.float32), grad_b1, part_index * quarter, 0
    )
    grad_vectors = jnp.concatenate(
        [
            jnp.stack(
                [
                    grad_gain_one,
                    grad_shift_one,
                    grad_gain_input,
                    grad_shift_input,
                    column_sum(grad_q_one),
                    column_sum(grad_v_one),
                    grad_bias_out_one,
                    grad_gain_two,
                    grad_shift_two,
                    column_sum(grad_q_two),
                    column_sum(grad_v_two),
                    grad_bias_out_two,
                    grad_gain_three,
                    grad_shift_three,
                    grad_b2,
                ],
                axis=0,
            ),
            full_bias.reshape(-1, D),
        ],
        axis=0,
    )
    cross_sums, self_sums, vector_sums = (
        lax.psum_scatter(grad_cross, ("dp", "tensor"), scatter_dimension=0, tiled=True),
        lax.psum_scatter(grad_self, ("dp", "tensor"), scatter_dimension=0, tiled=True),
        lax.psum_scatter(grad_vectors, ("dp", "tensor"), scatter_dimension=1, tiled=True),
    )
    return (
        latents_out,
        grad_latents,
        grad_inputs,
        cross_sums,
        self_sums,
        vector_sums,
        mlp_sums[0],
        mlp_sums[1],
    )


BF = jnp.bfloat16
F32 = jnp.float32
MESH = pl.DeviceIdType.MESH
TILE = 256
PAD = 128
GROUP = 256
GROUPS = D // GROUP
GHEADS = GROUP // HEAD_DIM
LANES = 128
HIDE = -1e30
VEC_PAD = 32
VEC_TOP = 24
NROWS = 4 * D
SLOT1_FIRST = 2
SLOT1_TILES = 2
VMEM_LIMIT = 63 * 1024 * 1024


GATHER_PLAN = {
    "start": ((0, 0), (0, 4)),
    "vecb": ((1, 0), (0, 1)),
    "ln0": ((0, 2),),
    "ln1": ((1, 1), (2, 0)),
    "ln4": ((0, 3),),
    "ln6": ((1, 2),),
    "ln8": ((2, 1), (0, 5)),
    "post": ((1, 3), (1, 4)),
    "q": ((3, 0), (3, 1), (0, 6), (2, 2), (3, 2), (2, 3), (1, 5), (0, 7), (3, 3), (0, 8)),
    "kv0": ((1, 6), (2, 4)),
    "kv1": ((0, 9),),
    "kv4": ((1, 7),),
    "kv7": ((0, 10),),
    "kv8": ((1, 8),),
    "p0_0": ((0, 11), (0, 12)),
    "p0_3": ((2, 5), (2, 6), (2, 7), (0, 13)),
    "p1_1": ((2, 8),),
    "t1": ((0, 14),),
    "t2": ((0, 15),),
    "self0": ((3, 4), (3, 5), (3, 6), (3, 7), (1, 9), (1, 10), (1, 11), (1, 12), (1, 13)),
    "self1": ((1, 14),),
    "up0": ((1, 15), (3, 8)),
    "up1": ((2, 9), (2, 10), (3, 9)),
    "up2": ((2, 11), (3, 10)),
    "up3": ((2, 12), (3, 11)),
    "down0": ((2, 13), (3, 12)),
    "down1": ((2, 14), (3, 13)),
    "down2": ((2, 15), (3, 14)),
    "down3": ((3, 15),),
}
SCATTER_PLAN = {
    "b": ((0, 0), (0, 1)),
    "d": ((0, 2),),
    "CS2": ((0, 3),),
    "e": ((1, 0), (1, 1)),
    "f": ((0, 4), (0, 5)),
    "t0": ((1, 2), (2, 0)),
    "t1": ((0, 6),),
    "t2": ((1, 3), (2, 1)),
    "t3": ((2, 2),),
    "t4": ((1, 5), (2, 3), (0, 7), (0, 8)),
    "t5": ((1, 6),),
    "t6": ((2, 5),),
    "t7": ((0, 9),),
    "t8": ((1, 7), (2, 6), (0, 10), (3, 0)),
    "t9": ((1, 8),),
    "t11": ((2, 7), (0, 11)),
    "t12": ((1, 9), (2, 8)),
    "g": ((1, 10), (3, 1)),
    "u0": ((2, 9),),
    "u1": ((1, 11), (2, 10)),
    "u2": ((0, 12),),
    "u3": ((0, 13),),
    "u4": ((2, 11), (0, 14)),
    "u8": ((1, 13),),
    "u11": ((1, 14),),
    "u12": ((2, 13), (3, 2)),
    "end": ((4, 0), (2, 14), (4, 1), (0, 15), (4, 2), (4, 3), (1, 15), (4, 4), (2, 15), (3, 3)),
}
Z_UNITS = (1, 2)
Z_UNITS_BACK = (1, 3)


def nn(left, right):
    return jnp.dot(left, right, preferred_element_type=F32)


def nt(left, right):
    return lax.dot_general(
        left, right, (((1,), (1,)), ((), ())), preferred_element_type=F32
    )


def ln_parts(values):
    average = jnp.mean(values, axis=-1, keepdims=True)
    centred = values - average
    variance = jnp.mean(centred * centred, axis=-1, keepdims=True)
    scale = lax.rsqrt(variance + 1e-05)
    return centred * scale, scale


def ln_rows(values, gain_row, shift_row):
    return ln_parts(values)[0] * gain_row + shift_row


def flipped(z, step):
    value = z
    if step % 2:
        value = value + 1 - 2 * lax.rem(z, 2)
    if step // 2:
        value = value + 2 - 4 * (z // 2)
    return value


def neighbours(tensor_count):
    dp = lax.axis_index("dp")
    z = lax.axis_index("tensor")
    core = lax.rem(dp, 2)
    flip_x = dp + 2 * (1 - 2 * lax.rem(dp // 2, 2))
    flip_y = dp + 4 * (1 - 2 * (dp // 4))
    other = dp + 1 - 2 * core
    first = (1 - core) * flip_x + core * flip_y
    second = (1 - core) * flip_y + core * flip_x
    both = flip_x + flip_y - dp
    peers = [flipped(z, step) for step in range(1, tensor_count)]
    return dp, z, core, other, first, second, both, peers


def meet(dp, z, other, first, second, peers):
    barrier = pltpu.get_barrier_semaphore()
    devices = [(other, z), (first, z), (second, z)] + [(dp, peer) for peer in peers]
    for device in devices:
        pl.semaphore_signal(barrier, inc=1, device_id=device, device_id_type=MESH)
    pl.semaphore_wait(barrier, len(devices))


def head_mask(rows):
    row_head = lax.broadcasted_iota(jnp.int32, (rows, GROUP), 0) // LAT
    col_head = lax.broadcasted_iota(jnp.int32, (rows, GROUP), 1) // HEAD_DIM
    return row_head == col_head


def spread_heads(block, mask):
    wide = jnp.concatenate([block.astype(F32)] * GHEADS, axis=0)
    return jnp.where(mask, wide, 0.0).astype(BF)


def pick_heads(stacked):
    col_head = lax.broadcasted_iota(jnp.int32, (LAT, GROUP), 1) // HEAD_DIM
    total = jnp.zeros((LAT, GROUP), F32)
    for head in range(GHEADS):
        part = stacked[head * LAT : (head + 1) * LAT]
        total = total + jnp.where(col_head == head, part, 0.0)
    return total


def forward_kernel(
    tensor_count,
    lat,
    inp,
    seg_in,
    cross_shard,
    self_shard,
    up_shard,
    down_shard,
    vectors,
    cot,
    out_o,
    wc_o,
    ws_o,
    ctx_o,
    key_o,
    val_o,
    prob_o,
    gup_o,
    gdn_o,
    vec_o,
    query_h,
    read_h,
    mid_h,
    query2_h,
    key2_h,
    val2_h,
    prob2_h,
    read2_h,
    late_h,
    gn3_o,
    gb1_o,
    inv_o,
    query_o,
    read,
    mid_o,
    query2_o,
    key2_o,
    val2_o,
    prob2_o,
    read2_o,
    late_o,
    seg,
    vec_own,
    w_cross,
    w_self,
    w_up,
    w_down,
    ctx,
    keys,
    vals,
    scores,
    probs,
    inbuf,
    qbd,
    peak,
    denom,
    oacc,
    norm_t,
    gy_t,
    vec_in,
    vec_sum,
    send_sem,
    recv_sem,
    vec_ssem,
    vec_rsem,
    in_sem,
    out_sem,
):
    dp, z, core, other, first, second, both, peers = neighbours(tensor_count)
    meet(dp, z, other, first, second, peers)
    weights = (w_cross, w_self, w_up, w_down)
    shards = (cross_shard, self_shard, up_shard, down_shard)
    shard_rows = cross_shard.shape[0]
    tiles = ctx.shape[0] // TILE
    chunk_count = 4 * tensor_count
    kinds = 7

    def place(unit, owner, part):
        if unit < 2:
            start = (owner * tensor_count + part) * shard_rows
        else:
            start = part * D + owner * shard_rows
        return pl.ds(pl.multiple_of(start, shard_rows), shard_rows)

    def remote(source, target, number, device):
        return pltpu.make_async_remote_copy(
            src_ref=source,
            dst_ref=target,
            send_sem=send_sem.at[number],
            recv_sem=recv_sem.at[number],
            device_id=device,
            device_id_type=MESH,
        )

    def z_copy(unit, step):
        rows = place(unit, dp, z)
        number = chunk_count * kinds + unit * (tensor_count - 1) + step - 1
        return remote(shards[unit], weights[unit].at[rows], number, (dp, peers[step - 1]))

    by_z = [unit * tensor_count + 1 for unit in Z_UNITS]

    def plane_copy(chunk, kind):
        unit, step = divmod(chunk, tensor_count)
        part = flipped(z, step)
        owner = (dp, dp, first, dp, first, second, both)[kind]
        device = ((first, second, second, other, other, other, other)[kind], z)
        if chunk in by_z and kind < 3:
            part, owner, device = z, (first, second, both)[kind], (dp, peers[0])
        rows = place(unit, owner, part)
        return remote(
            weights[unit].at[rows], weights[unit].at[rows], chunk * kinds + kind, device
        )

    def z_start(unit):
        for step in range(1, tensor_count):
            z_copy(unit, step).start()

    def stage0(chunk):
        unit, step = divmod(chunk, tensor_count)
        if step:
            z_copy(unit, step).wait_recv()
        for kind in (3,) if chunk in by_z else (0, 1, 3):
            plane_copy(chunk, kind).start()

    def pass_on(chunk, kind):
        if chunk + 1 in by_z:
            plane_copy(chunk + 1, kind).start()

    def stage1(chunk):
        plane_copy(chunk, 0).wait_recv()
        for kind in (4,) if chunk in by_z else (2, 4):
            plane_copy(chunk, kind).start()
        pass_on(chunk, 0)

    def stage2(chunk):
        plane_copy(chunk, 1).wait_recv()
        plane_copy(chunk, 5).start()
        pass_on(chunk, 1)
        plane_copy(chunk, 2).wait_recv()
        plane_copy(chunk, 6).start()
        pass_on(chunk, 2)

    def stage3(chunk):
        for kind in (3, 4, 5, 6):
            plane_copy(chunk, kind).wait_recv()

    def send_first(chunk):
        stage0(chunk)
        unit, step = divmod(chunk, tensor_count)
        if step == tensor_count - 2 and unit < 3:
            z_start(unit + 1)

    stages = (send_first, stage1, stage2, stage3)

    def run_at(name):
        for stage, chunk in GATHER_PLAN.get(name, ()):
            stages[stage](chunk)

    def run_each(name, index, count):
        for number in range(count):
            if GATHER_PLAN.get(name + str(number)):
                pl.when(index == number)(partial(run_at, name + str(number)))

    def vec_copy(hop):
        if hop < tensor_count - 1:
            source, device = vec_own, (dp, peers[hop])
        else:
            level = hop - (tensor_count - 1)
            source, device = vec_sum.at[level], ((first, second, other)[level], z)
        return pltpu.make_async_remote_copy(
            src_ref=source,
            dst_ref=vec_in.at[hop],
            send_sem=vec_ssem.at[hop],
            recv_sem=vec_rsem.at[hop],
            device_id=device,
            device_id_type=MESH,
        )

    def read_in(index):
        rows = inbuf.shape[1]
        start = pl.multiple_of(index * rows, rows)
        slot = lax.rem(index, 2)
        return pltpu.make_async_copy(
            inp.at[pl.ds(start, rows)], inbuf.at[slot], in_sem.at[slot]
        )

    def keep(source, target, number):
        return pltpu.make_async_copy(source, target, out_sem.at[number])

    width = vectors.shape[1]
    first_col = (dp * tensor_count + z) * width
    row = lax.broadcasted_iota(jnp.int32, (width, D), 0)
    col = lax.broadcasted_iota(jnp.int32, (width, D), 1)
    spot = jnp.where(col == row + first_col, 1.0, 0.0).astype(BF)
    vec_own[...] = jnp.zeros(vec_own.shape, BF)
    vec_own[0 : vectors.shape[0], :] = nn(vectors[...], spot).astype(BF)
    for hop in range(tensor_count - 1):
        vec_copy(hop).start()
    w_cross[place(0, dp, z), :] = cross_shard[...]
    z_start(0)
    read_in(0).start()
    keep(cot, gn3_o, 16).start()
    for unit in range(1, 4):
        weights[unit][place(unit, dp, z), :] = shards[unit][...]
    seg[...] = jnp.full(seg.shape, 2, jnp.int32)
    for row in range(seg_in.shape[0]):
        seg[:, PAD + row * LANES : PAD + (row + 1) * LANES] = seg_in[row : row + 1, :]
    run_at("start")
    run_at("vecz")
    for hop in range(tensor_count - 1):
        vec_copy(hop).wait_recv()
    total = vec_own[...].astype(F32)
    for hop in range(tensor_count - 1):
        total = total + vec_in[hop].astype(F32)
    for level in range(3):
        vec_sum[level] = total.astype(BF)
        hop = tensor_count - 1 + level
        vec_copy(hop).start()
        run_at(("veca", "vecb", "vecc")[level])
        vec_copy(hop).wait_recv()
        total = total + vec_in[hop].astype(F32)
    vec_o[...] = total

    def vec(row):
        return vec_o[row : row + 1, :]

    ctx[0:PAD, :] = jnp.zeros((PAD, D), BF)
    in_rows = inbuf.shape[1]
    reads = inp.shape[0] // in_rows

    def norm_inputs(index, carry):
        @pl.when(index + 1 < reads)
        def _():
            read_in(index + 1).start()

        read_in(index).wait()
        slot = lax.rem(index, 2)

        def rows_of(part, carry2):
            start = pl.multiple_of(part * 64, 64)
            values = inbuf[slot, pl.ds(start, 64), :].astype(F32)
            ctx[pl.ds(pl.multiple_of(PAD + index * in_rows + start, 64), 64), :] = ln_rows(
                values, vec(2), vec(3)
            ).astype(BF)
            return carry2

        lax.fori_loop(0, in_rows // 64, rows_of, 0)

        run_each("ln", index, reads)
        return carry

    lax.fori_loop(0, reads, norm_inputs, 0)
    run_at("post")
    normed = ln_rows(lat[...], vec(0), vec(1)).astype(BF)
    keep(cot, gn3_o, 16).wait()
    gy = gn3_o[...].astype(BF)
    gy_t[...] = gn3_o[...].T.astype(BF)
    run_at("q")
    keep(w_cross, wc_o, 0).start()
    mask = head_mask(GHEADS * LAT)

    query = (nn(normed, w_cross[0:D, :]) + vec(4)).astype(BF)
    scaled = (query.astype(F32) * HEAD_DIM ** (-0.5)).astype(BF)
    query_o[...] = scaled
    for slot in range(2):
        for group in range(GROUPS):
            block = scaled[slot * LAT : (slot + 1) * LAT, group * GROUP : (group + 1) * GROUP]
            qbd[slot * GROUPS + group] = spread_heads(block, mask)

    def project(index, carry):
        rows = pl.ds(pl.multiple_of(index * TILE, TILE), TILE)
        block = ctx[rows, :]
        keys[rows, :] = nn(block, w_cross[D : 2 * D, :]).astype(BF)
        vals[rows, :] = (nn(block, w_cross[2 * D : 3 * D, :]) + vec(5)).astype(BF)

        run_each("kv", index, tiles)
        return carry

    lax.fori_loop(0, tiles, project, 0)
    keep(ctx, ctx_o, 1).start()
    keep(keys, key_o, 2).start()
    keep(vals, val_o, 3).start()

    wide = 3 * TILE
    whole = tiles // 3
    rest = [
        (0, slice(whole * wide, tiles * TILE), slice(whole * wide, tiles * TILE)),
        (
            1,
            slice(SLOT1_FIRST * TILE, (SLOT1_FIRST + SLOT1_TILES) * TILE),
            slice(tiles * TILE, (tiles + SLOT1_TILES) * TILE),
        ),
    ]

    def wide_cols(index):
        return pl.ds(pl.multiple_of(index * wide, wide), wide)

    def fold(values, op):
        parts = [values[:, at : at + LANES] for at in range(0, values.shape[1], LANES)]
        while len(parts) > 1:
            parts = [
                op(parts[at], parts[at + 1]) if at + 1 < len(parts) else parts[at]
                for at in range(0, len(parts), 2)
            ]
        return parts[0]

    seen = []
    for slot in range(2):
        hit = jnp.where(seg[...] == slot, 1.0, 0.0)
        seen.append(jnp.max(hit, axis=1, keepdims=True))

    for group in range(GROUPS):
        gcols = slice(group * GROUP, (group + 1) * GROUP)
        peak[...] = jnp.full(peak.shape, HIDE, F32)
        denom[...] = jnp.zeros(denom.shape, F32)
        oacc[...] = jnp.zeros(oacc.shape, F32)

        def score_part(slot, rows, cols):
            values = nt(qbd[slot * GROUPS + group], keys[rows, gcols])
            values = jnp.where(seg[:, rows] == slot, values, HIDE)
            scores[:, cols] = values
            peak[slot] = jnp.maximum(peak[slot], fold(values, jnp.maximum))

        def score(index, carry):
            score_part(0, wide_cols(index), wide_cols(index))
            return carry

        run_at("s%d" % group)
        lax.fori_loop(0, whole, score, 0)
        for slot, rows, cols in rest:
            score_part(slot, rows, cols)
        for slot in range(2):
            top = jnp.max(peak[slot], axis=1, keepdims=True)
            top = jnp.where(seen[slot] > 0.0, top, 0.0)
            peak[slot] = jnp.broadcast_to(top, (GHEADS * LAT, LANES))
        if group:
            keep(probs, prob_o.at[group - 1], 4).wait()

        def spread_part(slot, rows, cols):
            for head in range(GHEADS):
                part = slice(head * LAT, (head + 1) * LAT)
                values = scores[part, cols]
                count = values.shape[1] // LANES
                top = jnp.concatenate([peak[slot, part, :]] * count, axis=1)
                values = jnp.exp(values - top)
                probs[part, cols] = values.astype(BF)
                denom[slot, part, :] += fold(values, jnp.add)
            oacc[slot] += nn(probs[:, cols], vals[rows, gcols])

        def spread(index, carry):
            run_each("p%d_" % group, index, whole)
            spread_part(0, wide_cols(index), wide_cols(index))
            return carry

        lax.fori_loop(0, whole, spread, 0)
        for slot, rows, cols in rest:
            spread_part(slot, rows, cols)
        keep(probs, prob_o.at[group], 4).start()
        run_at("t%d" % group)
        for slot in range(2):
            total = jnp.sum(denom[slot], axis=1, keepdims=True) + 1.0 - seen[slot]
            scale = 1.0 / total
            full = jnp.broadcast_to(scale, (GHEADS * LAT, GROUP))
            inv_o[slot * LAT : (slot + 1) * LAT, gcols] = pick_heads(full)
            read[slot * LAT : (slot + 1) * LAT, gcols] = pick_heads(oacc[slot] * scale)

    run_at("mid")
    mid = lat[...] + (nn(read[...].astype(BF), w_cross[3 * D :, :]) + vec(6))
    mid_o[...] = mid
    normed_two = ln_rows(mid, vec(7), vec(8)).astype(BF)
    run_at("self0")
    keep(w_self, ws_o, 5).start()
    query_two = (nn(normed_two, w_self[0:D, :]) + vec(9)).astype(BF)
    query2_o[...] = (query_two.astype(F32) * HEAD_DIM ** (-0.5)).astype(BF)
    key2_o[...] = nn(normed_two, w_self[D : 2 * D, :]).astype(BF)
    val2_o[...] = (nn(normed_two, w_self[2 * D : 3 * D, :]) + vec(10)).astype(BF)
    run_at("self1")
    for slot in range(2):
        srows = slice(slot * LAT, (slot + 1) * LAT)
        for group in range(GROUPS):
            gcols = slice(group * GROUP, (group + 1) * GROUP)
            wide = spread_heads(query2_o[srows, gcols], mask)
            values = nt(wide, key2_o[srows, gcols])
            values = jnp.exp(values - jnp.max(values, axis=1, keepdims=True))
            values = values / jnp.sum(values, axis=1, keepdims=True)
            values = values.astype(BF)
            prob2_o[slot, group] = values
            read2_o[srows, gcols] = pick_heads(nn(values, val2_o[srows, gcols]))
    late = mid_o[...] + (nn(read2_o[...].astype(BF), w_self[3 * D :, :]) + vec(11))
    late_o[...] = late
    normed_three = ln_rows(late, vec(12), vec(13))
    norm_t[...] = normed_three.T.astype(BF)
    normed_three = normed_three.astype(BF)
    keep(probs, prob_o.at[GROUPS - 1], 4).wait()
    keep(keys, key_o, 2).wait()
    keep(vals, val_o, 3).wait()

    small = [
        (query_o, query_h),
        (read, read_h),
        (mid_o, mid_h),
        (query2_o, query2_h),
        (key2_o, key2_h),
        (val2_o, val2_h),
        (prob2_o, prob2_h),
        (read2_o, read2_h),
        (late_o, late_h),
    ]
    for number, (source, target) in enumerate(small):
        keep(source, target, 17 + number).start()

    rows_all = slice(0, 2 * LAT)

    def quarter(step):
        part = flipped(z, step)
        return part, pl.ds(pl.multiple_of(part * D, D), D)

    def up_part(step):
        part, rows = quarter(step)
        cols = slice(step * D, (step + 1) * D)
        pre = nn(normed_three, w_up[rows, :]) + vec_o[pl.ds(15 + part, 1), :]
        half = 0.5 * (1.0 + lax.erf(pre * 0.5**0.5))
        slope = half + pre * jnp.exp(-0.5 * pre * pre) * 0.3989422804014327
        hidden = (pre * half).astype(BF)
        probs[rows_all, cols] = hidden
        scores[rows_all, cols] = slope
        vals[rows, :] = nn(gy_t[...], hidden).astype(BF)
        keep(vals.at[rows], gdn_o.at[rows], 6 + step).start()

    def down_part(step):
        part, rows = quarter(step)
        cols = slice(step * D, (step + 1) * D)
        down = w_down[rows, :]
        y_part = nt(probs[rows_all, cols], down)
        grad_pre = (scores[rows_all, cols] * nn(gy, down)).astype(BF)
        keys[rows, :] = nn(norm_t[...], grad_pre).astype(BF)
        keep(keys.at[rows], gup_o.at[rows], 6 + tensor_count + step).start()
        x_part = nt(grad_pre, w_up[rows, :])
        if step == 0:
            out_o[...] = late_o[...] + vec(14) + y_part
            gn3_o[...] = x_part
        else:
            out_o[...] += y_part
            gn3_o[...] += x_part
        gb1_o[pl.ds(part, 1), :] = jnp.sum(grad_pre.astype(F32), axis=0, keepdims=True)

    gb1_o[...] = jnp.zeros(gb1_o.shape, F32)
    for step in range(tensor_count):
        run_at("up%d" % step)
        up_part(step)
    for step in range(tensor_count):
        run_at("down%d" % step)
        down_part(step)
    for number, (source, target) in enumerate(small):
        keep(source, target, 17 + number).wait()
    keep(w_cross, wc_o, 0).wait()
    keep(ctx, ctx_o, 1).wait()
    keep(w_self, ws_o, 5).wait()
    for step in range(tensor_count):
        part, rows = quarter(step)
        keep(vals.at[rows], gdn_o.at[rows], 6 + step).wait()
        keep(keys.at[rows], gup_o.at[rows], 6 + tensor_count + step).wait()
    for hop in range(tensor_count + 2):
        vec_copy(hop).wait_send()
    for unit in range(4):
        for step in range(1, tensor_count):
            z_copy(unit, step).wait_send()
    for chunk in range(chunk_count):
        for kind in range(kinds):
            plane_copy(chunk, kind).wait_send()


def forward_call(tensor_count, lat, inp, seg, cross_w, self_w, up_w, down_w, vectors, cot):
    rows = lat.shape[0]
    tokens = inp.shape[0] + PAD
    virtual = (tokens // TILE + SLOT1_TILES) * TILE
    sds = jax.ShapeDtypeStruct
    hbm = pl.BlockSpec(memory_space=pl.ANY)
    vmem = pl.BlockSpec(memory_space=pltpu.VMEM)
    stacked = GHEADS * LAT
    copies = 4 * tensor_count * 7 + 4 * (tensor_count - 1)
    outs = [
        (sds((rows, D), F32), vmem),
        (sds((NROWS, D), BF), hbm),
        (sds((NROWS, D), BF), hbm),
        (sds((tokens, D), BF), hbm),
        (sds((tokens, D), BF), hbm),
        (sds((tokens, D), BF), hbm),
        (sds((GROUPS, stacked, virtual), BF), hbm),
        (sds((NROWS, D), BF), hbm),
        (sds((NROWS, D), BF), hbm),
        (sds((VEC_PAD, D), F32), vmem),
        (sds((rows, D), BF), hbm),
        (sds((rows, D), F32), hbm),
        (sds((rows, D), F32), hbm),
        (sds((rows, D), BF), hbm),
        (sds((rows, D), BF), hbm),
        (sds((rows, D), BF), hbm),
        (sds((2, GROUPS, stacked, LAT), BF), hbm),
        (sds((rows, D), F32), hbm),
        (sds((rows, D), F32), hbm),
        (sds((rows, D), F32), vmem),
        (sds((8, D), F32), vmem),
        (sds((rows, D), F32), vmem),
    ]
    return pl.pallas_call(
        partial(forward_kernel, tensor_count),
        out_shape=[shape for shape, spec in outs],
        out_specs=[spec for shape, spec in outs],
        in_specs=[vmem, hbm] + [vmem] * 6 + [hbm],
        scratch_shapes=[
            pltpu.VMEM((rows, D), BF),
            pltpu.VMEM((rows, D), F32),
            pltpu.VMEM((rows, D), F32),
            pltpu.VMEM((rows, D), BF),
            pltpu.VMEM((rows, D), BF),
            pltpu.VMEM((rows, D), BF),
            pltpu.VMEM((2, GROUPS, stacked, LAT), BF),
            pltpu.VMEM((rows, D), F32),
            pltpu.VMEM((rows, D), F32),
            pltpu.VMEM((1, tokens), jnp.int32),
            pltpu.VMEM((VEC_PAD, D), BF),
            pltpu.VMEM((NROWS, D), BF),
            pltpu.VMEM((NROWS, D), BF),
            pltpu.VMEM((NROWS, D), BF),
            pltpu.VMEM((NROWS, D), BF),
            pltpu.VMEM((tokens, D), BF),
            pltpu.VMEM((tokens, D), BF),
            pltpu.VMEM((tokens, D), BF),
            pltpu.VMEM((stacked, virtual), F32),
            pltpu.VMEM((stacked, virtual), BF),
            pltpu.VMEM((2, 320, D), BF),
            pltpu.VMEM((2 * GROUPS, stacked, GROUP), BF),
            pltpu.VMEM((2, stacked, LANES), F32),
            pltpu.VMEM((2, stacked, LANES), F32),
            pltpu.VMEM((2, stacked, GROUP), F32),
            pltpu.VMEM((D, rows), BF),
            pltpu.VMEM((D, rows), BF),
            pltpu.VMEM((tensor_count + 2, VEC_PAD, D), BF),
            pltpu.VMEM((3, VEC_PAD, D), BF),
            pltpu.SemaphoreType.DMA((copies,)),
            pltpu.SemaphoreType.DMA((copies,)),
            pltpu.SemaphoreType.DMA((tensor_count + 2,)),
            pltpu.SemaphoreType.DMA((tensor_count + 2,)),
            pltpu.SemaphoreType.DMA((2,)),
            pltpu.SemaphoreType.DMA((26,)),
        ],
        compiler_params=pltpu.CompilerParams(
            collective_id=0, has_side_effects=True, vmem_limit_bytes=VMEM_LIMIT
        ),
        name="gather_forward",
    )(lat, inp, seg, cross_w, self_w, up_w, down_w, vectors, cot)


def tn(left, right):
    return lax.dot_general(
        left, right, (((0,), (0,)), ((), ())), preferred_element_type=F32
    )


def ln_back(values, gain_row, incoming):
    unit, scale = ln_parts(values)
    scaled = incoming * gain_row
    inner = jnp.mean(scaled * unit, axis=-1, keepdims=True)
    outgoing = scale * (scaled - jnp.mean(scaled, axis=-1, keepdims=True) - unit * inner)
    gain = jnp.sum(incoming * unit, axis=0, keepdims=True)
    return outgoing, gain, jnp.sum(incoming, axis=0, keepdims=True)


def head_mask_t(rows):
    row_head = lax.broadcasted_iota(jnp.int32, (GROUP, rows), 0) // HEAD_DIM
    col_head = lax.broadcasted_iota(jnp.int32, (GROUP, rows), 1) // LAT
    return row_head == col_head


def spread_columns(block, mask):
    wide = jnp.concatenate([block.T] * GHEADS, axis=1)
    return jnp.where(mask, wide, 0.0).astype(BF)


def backward_kernel(
    tensor_count,
    lat_h,
    cot_h,
    mid_h,
    late_h,
    gn3_h,
    read_h,
    read2_h,
    query_h,
    query2_h,
    key2_h,
    val2_h,
    prob2_h,
    vecs,
    gb1,
    inv,
    wc_h,
    ws_h,
    ctx_h,
    key_h,
    val_h,
    prob_h,
    gup_h,
    gdn_h,
    inp,
    glat_o,
    ginp_o,
    gcross_o,
    gself_o,
    gvec_o,
    gup_o,
    gdn_o,
    dkv_h,
    w_cross,
    g_mlp,
    g_sc,
    rc,
    rb,
    ra,
    rz,
    rq,
    dwk,
    dwv,
    kt,
    vt,
    ct,
    it,
    pt,
    p1,
    ot,
    dkv,
    gbd,
    gbd_t,
    qbd_t,
    row_r,
    dqacc,
    gread,
    dq2,
    dk2,
    dv2,
    gbias,
    gvec,
    vec_in,
    vec_sum,
    c_ssem,
    c_rsem,
    b_ssem,
    b_rsem,
    a_ssem,
    a_rsem,
    z_ssem,
    z_rsem,
    v_ssem,
    v_rsem,
    tile_sem,
    load_sem,
    credit,
):
    dp, z, core, other, first, second, both, peers = neighbours(tensor_count)
    meet(dp, z, other, first, second, peers)
    shard = gcross_o.shape[0]
    quad = 4 * shard
    yy = dp // 4
    xx = lax.rem(dp // 2, 2)
    tiles = ctx_h.shape[0] // TILE
    chunk_count = 4 * tensor_count
    w_self_at = NROWS

    def mult(value, by):
        return pl.multiple_of(value, by)

    def chunk_part(chunk):
        step = chunk % tensor_count + 1
        return flipped(z, step) if step < tensor_count else z

    def own_ref(chunk):
        unit, part = chunk // tensor_count, chunk_part(chunk)
        if unit < 2:
            return g_mlp, (unit * tensor_count + part) * quad
        return g_sc, (((unit - 2) * 2 + core) * tensor_count + part) * quad

    def rows_at(start, count):
        return pl.ds(mult(start, shard), count)

    def remote(source, target, send, recv, device):
        return pltpu.make_async_remote_copy(
            src_ref=source,
            dst_ref=target,
            send_sem=send,
            recv_sem=recv,
            device_id=device,
            device_id_type=MESH,
        )

    def c_slot(chunk):
        return rc.at[chunk % 8]

    def c_whole(chunk):
        return remote(
            c_slot(chunk), c_slot(chunk), c_ssem.at[chunk], c_rsem.at[chunk], (other, z)
        )

    def c_start(chunk):
        unit, part = chunk // tensor_count, chunk_part(chunk)
        if unit < 2:
            source = (gdn_h, gup_h)[unit]
            for q in range(4):
                start = part * D + (2 * q + 1 - core) * shard
                remote(
                    source.at[rows_at(start, shard)],
                    c_slot(chunk).at[pl.ds(q * shard, shard)],
                    c_ssem.at[chunk],
                    c_rsem.at[chunk],
                    (other, z),
                ).start()
        else:
            start = (((unit - 2) * 2 + 1 - core) * tensor_count + part) * quad
            remote(
                g_sc.at[rows_at(start, quad)],
                c_slot(chunk),
                c_ssem.at[chunk],
                c_rsem.at[chunk],
                (other, z),
            ).start()

    by_z = [unit * tensor_count for unit in Z_UNITS_BACK]

    in_plane = [chunk for chunk in range(chunk_count) if chunk not in by_z]

    def b_copy(chunk, half):
        ref, base = own_ref(chunk)
        q = (1 - core) * ((1 - yy) * 2 + half) + core * (half * 2 + 1 - xx)
        number = chunk * 2 + half
        return remote(
            ref.at[rows_at(base + q * shard, shard)],
            rb.at[in_plane.index(chunk), half],
            b_ssem.at[number],
            b_rsem.at[number],
            (second, z),
        )

    def a_copy(chunk):
        ref, base = own_ref(chunk)
        q = (1 - core) * (yy * 2 + 1 - xx) + core * ((1 - yy) * 2 + xx)
        return remote(
            ref.at[rows_at(base + q * shard, shard)],
            ra.at[in_plane.index(chunk)],
            a_ssem.at[chunk],
            a_rsem.at[chunk],
            (first, z),
        )

    def z_copy(chunk):
        unit, step = divmod(chunk, tensor_count)
        ref, base = own_ref(chunk)
        number = unit * (tensor_count - 1) + step
        if chunk in by_z:
            return remote(
                ref.at[rows_at(base, quad)],
                rq.at[by_z.index(chunk)],
                z_ssem.at[number],
                z_rsem.at[number],
                (dp, peers[0]),
            )
        return remote(
            ref.at[rows_at(base + (yy * 2 + xx) * shard, shard)],
            rz.at[number],
            z_ssem.at[number],
            z_rsem.at[number],
            (dp, peers[step]),
        )

    piece = 32

    def add_rows(ref, start, source, count):
        def body(index, carry):
            rows = pl.ds(mult(start + index * piece, piece), piece)
            part = source[pl.ds(mult(index * piece, piece), piece), :]
            ref[rows, :] = (ref[rows, :].astype(F32) + part.astype(F32)).astype(BF)
            return carry

        lax.fori_loop(0, count // piece, body, 0)

    def stage1(chunk):
        c_whole(chunk).wait_recv()
        ref, base = own_ref(chunk)
        if chunk == tensor_count:
            own_up = g_mlp.at[pl.ds(tensor_count * quad, tensor_count * quad)]
            load(own_up, own_up, 2).wait()
        add_rows(ref, base, c_slot(chunk), quad)
        if chunk in (3, 7):
            pl.semaphore_signal(
                credit, inc=1, device_id=(other, z), device_id_type=MESH
            )
        if chunk in by_z:
            z_copy(chunk).start()
            return
        whole = chunk - (tensor_count - 1)
        if whole in by_z:
            z_copy(whole).wait_recv()
            add_rows(ref, base, rq.at[by_z.index(whole)], quad)
        for half in range(2):
            b_copy(chunk, half).start()

    def stage2(chunk):
        ref, base = own_ref(chunk)
        for half in range(2):
            b_copy(chunk, half).wait_recv()
            q = (1 - core) * (yy * 2 + half) + core * (half * 2 + xx)
            add_rows(ref, base + q * shard, rb.at[in_plane.index(chunk), half], shard)
        a_copy(chunk).start()

    def stage3(chunk):
        a_copy(chunk).wait_recv()
        ref, base = own_ref(chunk)
        add_rows(ref, base + (yy * 2 + xx) * shard, ra.at[in_plane.index(chunk)], shard)
        if chunk % tensor_count < tensor_count - 1:
            z_copy(chunk).start()

    def finish(unit):
        chunk = unit * tensor_count + tensor_count - 1
        ref, base = own_ref(chunk)
        target = (gdn_o, gup_o, gself_o, gcross_o)[unit]
        steps = range(1 if unit in Z_UNITS_BACK else 0, tensor_count - 1)
        for step in steps:
            z_copy(unit * tensor_count + step).wait_recv()

        def body(index, carry):
            rows = pl.ds(mult(index * piece, piece), piece)
            start = base + (yy * 2 + xx) * shard + index * piece
            total = ref[pl.ds(mult(start, piece), piece), :].astype(F32)
            for step in steps:
                total = total + rz[unit * (tensor_count - 1) + step, rows, :].astype(F32)
            target[rows, :] = total
            return carry

        lax.fori_loop(0, shard // piece, body, 0)

    def vec_copy(hop):
        if hop < 3:
            source, device = vec_sum.at[hop], ((other, second, first)[hop], z)
        else:
            source, device = vec_sum.at[3], (dp, peers[hop - 3])
        return remote(source, vec_in.at[hop], v_ssem.at[hop], v_rsem.at[hop], device)

    def vec_step(step):
        if step == 0:
            vec_sum[0] = gvec[...]
        elif step <= 3:
            vec_copy(step - 1).wait_recv()
            vec_sum[step] = vec_sum[step - 1] + vec_in[step - 1]
        if step < 3:
            vec_copy(step).start()
        elif step == 3:
            for hop in range(3, 2 + tensor_count):
                vec_copy(hop).start()
        else:
            total = vec_sum[3]
            for hop in range(3, 2 + tensor_count):
                vec_copy(hop).wait_recv()
                total = total + vec_in[hop]
            width = gvec_o.shape[1]
            turn = lax.rem(D - (dp * tensor_count + z) * width, D)
            gvec_o[...] = pltpu.roll(total, turn, 1)[0 : gvec_o.shape[0], 0:width]

    stages = (stage1, stage2, stage3, finish, vec_step)

    def run_at(name):
        for stage, chunk in SCATTER_PLAN.get(name, ()):
            stages[stage](chunk)

    def run_each(name, index, count):
        for number in range(count):
            if SCATTER_PLAN.get(name + str(number)):
                pl.when(index == number)(partial(run_at, name + str(number)))

    def send_unit(unit):
        pl.semaphore_wait(credit, 1)
        for chunk in range(unit * tensor_count, (unit + 1) * tensor_count):
            c_start(chunk)

    def store_grad(unit, block, values):
        for part in range(8):
            parity, zpart = divmod(part, tensor_count)
            start = (((unit * 2 + parity) * tensor_count + zpart) * 4 + block) * shard
            g_sc[start : start + shard, :] = values[part * shard : (part + 1) * shard].astype(BF)

    def load(source, target, number):
        return pltpu.make_async_copy(source, target, load_sem.at[number])

    w_self = g_sc.at[pl.ds(w_self_at, NROWS)]
    for chunk in range(2 * tensor_count):
        c_start(chunk)
    for unit in range(2):
        source = (gdn_h, gup_h)[unit]
        for part in range(tensor_count):
            for q in range(4):
                pltpu.make_async_copy(
                    source.at[rows_at(part * D + (2 * q + core) * shard, shard)],
                    g_mlp.at[pl.ds(((unit * tensor_count + part) * 4 + q) * shard, shard)],
                    load_sem.at[1 + unit],
                ).start()
    lat_rows = 2 * LAT
    late, gn3, read2 = (dwk.at[pl.ds(third * lat_rows, lat_rows)] for third in range(3))
    read, mid, lat = (dwv.at[pl.ds(third * lat_rows, lat_rows)] for third in range(3))
    prob2 = pt.at[:, :, :, pl.ds(0, LAT)]
    early = [
        (cot_h, glat_o),
        (late_h, late),
        (gn3_h, gn3),
        (read2_h, read2),
        (read_h, read),
        (mid_h, mid),
        (prob2_h, prob2),
        (query2_h, kt.at[0]),
        (key2_h, kt.at[1]),
        (val2_h, vt.at[0]),
        (query_h, vt.at[1]),
    ]
    query2, key2, val2, query = kt.at[0], kt.at[1], vt.at[0], vt.at[1]
    for number, (source, target) in enumerate(early):
        load(source, target, 5 + number).start()
    load(ws_h, w_self, 0).start()
    load(wc_h, w_cross, 3).start()

    def load_p1(extra):
        return load(prob_h.at[:, :, pl.ds((tiles + extra) * TILE, TILE)], p1, 4)

    load_p1(0).start()
    half_mlp = tensor_count * quad
    own_down = g_mlp.at[pl.ds(0, half_mlp)]
    load(own_down, own_down, 1).wait()

    def vec(row):
        return vecs[row : row + 1, :]

    mask = head_mask(GHEADS * LAT)
    mask_t = head_mask_t(GHEADS * LAT)
    gvec[...] = jnp.zeros(gvec.shape, F32)

    def note(row, values):
        gvec[row : row + 1, :] = values

    def col_sum(values):
        return jnp.sum(values.astype(F32), axis=0, keepdims=True)

    def row_terms(grad_block, read_block):
        wide = jnp.concatenate([grad_block.astype(F32) * read_block] * GHEADS, axis=0)
        return jnp.sum(jnp.where(mask, wide, 0.0), axis=1, keepdims=True)

    run_at("a")
    for number, (source, target) in enumerate(early):
        load(source, target, 5 + number).wait()
    note(14, col_sum(glat_o[...].astype(BF)))
    gvec[15 : 15 + tensor_count, :] = gb1[0:tensor_count, :]
    back, gain, shift = ln_back(late[...], vec(12), gn3[...])
    note(12, gain)
    note(13, shift)
    gas = glat_o[...] + back
    glat_o[...] = gas
    grad_out = gas.astype(BF)
    note(11, col_sum(grad_out))
    load(ws_h, w_self, 0).wait()

    def self_block(block):
        return g_sc[w_self_at + block * D : w_self_at + (block + 1) * D, :]

    run_at("b")
    store_grad(0, 3, nn(read2[...].T.astype(BF), grad_out))
    gread[...] = nt(grad_out, self_block(3)).astype(BF)
    run_at("c")
    for slot in range(2):
        srows = slice(slot * LAT, (slot + 1) * LAT)
        for group in range(GROUPS):
            gcols = slice(group * GROUP, (group + 1) * GROUP)
            grads = spread_heads(gread[srows, gcols], mask)
            inner = row_terms(gread[srows, gcols], read2[srows, gcols])
            chance = prob2[slot, group]
            dprob = nt(grads, val2[srows, gcols])
            dscore = (chance.astype(F32) * (dprob - inner)).astype(BF)
            dq2[srows, gcols] = (
                pick_heads(nn(dscore, key2[srows, gcols])) * HEAD_DIM ** (-0.5)
            ).astype(BF)
            wide = spread_heads(query2[srows, gcols], mask)
            dk2[srows, gcols] = tn(dscore, wide).astype(BF)
            dv2[srows, gcols] = tn(chance, grads).astype(BF)
    run_at("d")
    note(9, col_sum(dq2[...]))
    note(10, col_sum(dv2[...]))
    unit_two, scale_two = ln_parts(mid[...])
    norm_t = (unit_two * vec(7) + vec(8)).T.astype(BF)
    store_grad(0, 0, nn(norm_t, dq2[...]))
    store_grad(0, 1, nn(norm_t, dk2[...]))
    store_grad(0, 2, nn(norm_t, dv2[...]))
    incoming = nt(dq2[...], self_block(0)) + nt(dk2[...], self_block(1))
    incoming = incoming + nt(dv2[...], self_block(2))
    back, gain, shift = ln_back(mid[...], vec(7), incoming)
    note(7, gain)
    note(8, shift)
    total = glat_o[...] + back
    glat_o[...] = total
    run_at("CS2")
    send_unit(2)
    run_at("e")
    grad_out = total.astype(BF)
    note(6, col_sum(grad_out))
    load(wc_h, w_cross, 3).wait()
    store_grad(1, 3, nn(read[...].T.astype(BF), grad_out))
    gread[...] = nt(grad_out, w_cross[3 * D :, :]).astype(BF)
    run_at("f")
    for slot in range(2):
        srows = slice(slot * LAT, (slot + 1) * LAT)
        for group in range(GROUPS):
            gcols = slice(group * GROUP, (group + 1) * GROUP)
            at = slot * GROUPS + group
            grads = gread[srows, gcols].astype(F32) * inv[srows, gcols]
            gbd[at] = spread_heads(grads, mask)
            gbd_t[at] = spread_columns(grads, mask_t)
            qbd_t[at] = spread_columns(query[srows, gcols].astype(F32), mask_t)
            inner = row_terms(grads, read[srows, gcols])
            row_r[at] = jnp.broadcast_to(inner, (GHEADS * LAT, LANES))
    dqacc[...] = jnp.zeros(dqacc.shape, F32)
    dwk[...] = jnp.zeros(dwk.shape, F32)
    dwv[...] = jnp.zeros(dwv.shape, F32)
    gbias[...] = jnp.zeros(gbias.shape, F32)
    it[0] = jnp.zeros(it.shape[1:], BF)

    def fetches(index):
        slot = lax.rem(index, 2)
        rows = pl.ds(mult(index * TILE, TILE), TILE)
        copies = [
            (key_h.at[rows], kt.at[slot]),
            (val_h.at[rows], vt.at[slot]),
            (ctx_h.at[rows], ct.at[slot]),
            (prob_h.at[:, :, rows], pt.at[slot]),
        ]
        return [
            pltpu.make_async_copy(source, target, tile_sem.at[slot, number])
            for number, (source, target) in enumerate(copies)
        ]

    def spill(index):
        slot = lax.rem(index, 2)
        return pltpu.make_async_copy(dkv.at[slot], dkv_h.at[index], tile_sem.at[slot, 4])

    for copy in fetches(jnp.int32(0)):
        copy.start()

    def attend_back(slot, chance_of, buffer, first_time):
        for group in range(GROUPS):
            gcols = slice(group * GROUP, (group + 1) * GROUP)
            at = slot * GROUPS + group
            chance = chance_of(group)
            dprob = nt(gbd[at], vt[buffer, :, gcols])
            inner = row_r[at]
            dscore = chance.astype(F32) * (dprob - jnp.concatenate([inner, inner], axis=1))
            dscore = dscore.astype(BF)
            dk_part = nn(qbd_t[at], dscore)
            dv_part = nn(gbd_t[at], chance)
            if not first_time:
                dk_part = dk_part + dkv[buffer, 0, gcols, :].astype(F32)
                dv_part = dv_part + dkv[buffer, 1, gcols, :].astype(F32)
            dkv[buffer, 0, gcols, :] = dk_part.astype(BF)
            dkv[buffer, 1, gcols, :] = dv_part.astype(BF)
            dqacc[at] += nn(dscore, kt[buffer, :, gcols])

    def tile_body(index, carry):
        buffer = lax.rem(index, 2)

        @pl.when(index + 1 < tiles)
        def _():
            for copy in fetches(index + 1):
                copy.start()

        run_each("t", index, tiles)

        @pl.when(index > 1)
        def _():
            spill(index - 2).wait()

        for copy in fetches(index):
            copy.wait()
        attend_back(0, lambda group: pt[buffer, group], buffer, True)
        for extra in range(SLOT1_TILES):

            @pl.when(index == SLOT1_FIRST + extra)
            def _():
                load_p1(extra).wait()
                attend_back(1, lambda group: p1[group], buffer, False)
                if extra + 1 < SLOT1_TILES:
                    load_p1(extra + 1).start()

        spill(index).start()
        dk = dkv[buffer, 0]
        dv = dkv[buffer, 1]
        gbias[...] += dv[:, :LANES].astype(F32) + dv[:, LANES:].astype(F32)
        block = ct[buffer]
        dwk[...] += nn(dk, block)
        dwv[...] += nn(dv, block)

        return carry

    lax.fori_loop(0, tiles, tile_body, 0)
    run_at("g")
    row = lax.broadcasted_iota(jnp.int32, (D, D), 0)
    col = lax.broadcasted_iota(jnp.int32, (D, D), 1)
    unity = jnp.where(row == col, 1.0, 0.0).astype(BF)
    store_grad(1, 2, nt(unity, dwv[...].astype(BF)))
    load(lat_h, lat, 16).start()
    store_grad(1, 1, nt(unity, dwk[...].astype(BF)))
    for slot in range(2):
        srows = slice(slot * LAT, (slot + 1) * LAT)
        for group in range(GROUPS):
            gcols = slice(group * GROUP, (group + 1) * GROUP)
            dq2[srows, gcols] = (
                pick_heads(dqacc[slot * GROUPS + group]) * HEAD_DIM ** (-0.5)
            ).astype(BF)
    load(lat_h, lat, 16).wait()
    unit_one, scale_one = ln_parts(lat[...])
    norm_t = (unit_one * vec(0) + vec(1)).T.astype(BF)
    store_grad(1, 0, nn(norm_t, dq2[...]))
    run_at("CS3")
    send_unit(3)
    spill(tiles - 2).wait()
    spill(tiles - 1).wait()

    note(4, col_sum(dq2[...]))
    note(5, jnp.sum(gbias[...].T, axis=0, keepdims=True))
    incoming = nt(dq2[...], w_cross[0:D, :])
    back, gain, shift = ln_back(lat[...], vec(0), incoming)
    note(0, gain)
    note(1, shift)
    glat_o[...] = glat_o[...] + back

    def fetch_back(index, at_start):
        slot = 0 if at_start else lax.rem(index, 2)
        back_rows = inp.at[pl.ds(0, TILE - PAD)]
        target = it.at[0, pl.ds(PAD, TILE - PAD)]
        if not at_start:
            back_rows = inp.at[pl.ds(mult(index * TILE - PAD, PAD), TILE)]
            target = it.at[slot]
        tile = 0 if at_start else index
        return [
            pltpu.make_async_copy(back_rows, target, tile_sem.at[slot, 0]),
            pltpu.make_async_copy(dkv_h.at[tile], dkv.at[slot], tile_sem.at[slot, 1]),
        ]

    def put(index, at_start):
        slot = 0 if at_start else lax.rem(index, 2)
        if at_start:
            source, rows = ot.at[0, pl.ds(PAD, TILE - PAD)], pl.ds(0, TILE - PAD)
        else:
            source, rows = ot.at[slot], pl.ds(mult(index * TILE - PAD, PAD), TILE)
        return pltpu.make_async_copy(source, ginp_o.at[rows], tile_sem.at[slot, 5])

    for copy in fetch_back(0, True):
        copy.start()

    def token_body(index, carry):
        buffer = lax.rem(index, 2)

        @pl.when(index + 1 < tiles)
        def _():
            for copy in fetch_back(index + 1, False):
                copy.start()

        @pl.when(index == 0)
        def _():
            for copy in fetch_back(0, True):
                copy.wait()

        @pl.when(index > 0)
        def _():
            for copy in fetch_back(index, False):
                copy.wait()

        run_each("u", index, tiles)
        incoming = nn(w_cross[D : 2 * D, :], dkv[buffer, 0])
        incoming = incoming + nn(w_cross[2 * D : 3 * D, :], dkv[buffer, 1])
        back, gain, shift = ln_back(it[buffer].astype(F32), vec(2), incoming.T)
        gvec[2:3, :] += gain
        gvec[3:4, :] += shift

        @pl.when(index == 2)
        def _():
            put(0, True).wait()

        @pl.when(index > 2)
        def _():
            put(index - 2, False).wait()

        ot[buffer] = back.astype(BF)

        @pl.when(index == 0)
        def _():
            put(0, True).start()

        @pl.when(index > 0)
        def _():
            put(index, False).start()

        return carry

    lax.fori_loop(0, tiles, token_body, 0)
    run_at("h")
    run_at("end")
    put(tiles - 2, False).wait()
    put(tiles - 1, False).wait()
    for hop in range(2 + tensor_count):
        vec_copy(hop).wait_send()
    for chunk in range(chunk_count):
        c_whole(chunk).wait_send()
        if chunk not in by_z:
            b_copy(chunk, 0).wait_send()
            b_copy(chunk, 1).wait_send()
            a_copy(chunk).wait_send()
        if chunk % tensor_count < tensor_count - 1:
            z_copy(chunk).wait_send()


def backward_call(tensor_count, shard, vec_shape, operands):
    sds = jax.ShapeDtypeStruct
    hbm = pl.BlockSpec(memory_space=pl.ANY)
    vmem = pl.BlockSpec(memory_space=pltpu.VMEM)
    rows = operands[0].shape[0]
    inp = operands[-1]
    stacked = GHEADS * LAT
    chunks = 4 * tensor_count
    zs = 4 * (tensor_count - 1)
    at = 2 * GROUPS
    sem = pltpu.SemaphoreType.DMA
    outs = [
        (sds((rows, D), F32), vmem),
        (sds(inp.shape, BF), hbm),
        (sds((shard, D), F32), vmem),
        (sds((shard, D), F32), vmem),
        (sds(vec_shape, F32), vmem),
        (sds((shard, D), F32), vmem),
        (sds((shard, D), F32), vmem),
        (sds(((inp.shape[0] + PAD) // TILE, 2, D, TILE), BF), hbm),
    ]
    return pl.pallas_call(
        partial(backward_kernel, tensor_count),
        out_shape=[shape for shape, spec in outs],
        out_specs=[spec for shape, spec in outs],
        in_specs=[hbm] * 12 + [vmem] * 3 + [hbm] * 9,
        scratch_shapes=[
            pltpu.VMEM((NROWS, D), BF),
            pltpu.VMEM((NROWS, D), BF),
            pltpu.VMEM((2 * NROWS, D), BF),
            pltpu.VMEM((8, 4 * shard, D), BF),
            pltpu.VMEM((chunks - len(Z_UNITS_BACK), 2, shard, D), BF),
            pltpu.VMEM((chunks - len(Z_UNITS_BACK), shard, D), BF),
            pltpu.VMEM((zs, shard, D), BF),
            pltpu.VMEM((len(Z_UNITS_BACK), 4 * shard, D), BF),
            pltpu.VMEM((D, D), F32),
            pltpu.VMEM((D, D), F32),
            pltpu.VMEM((2, TILE, D), BF),
            pltpu.VMEM((2, TILE, D), BF),
            pltpu.VMEM((2, TILE, D), BF),
            pltpu.VMEM((2, TILE, D), BF),
            pltpu.VMEM((2, GROUPS, stacked, TILE), BF),
            pltpu.VMEM((GROUPS, stacked, TILE), BF),
            pltpu.VMEM((2, TILE, D), BF),
            pltpu.VMEM((2, 2, D, TILE), BF),
            pltpu.VMEM((at, stacked, GROUP), BF),
            pltpu.VMEM((at, GROUP, stacked), BF),
            pltpu.VMEM((at, GROUP, stacked), BF),
            pltpu.VMEM((at, stacked, LANES), F32),
            pltpu.VMEM((at, stacked, GROUP), F32),
            pltpu.VMEM((rows, D), BF),
            pltpu.VMEM((rows, D), BF),
            pltpu.VMEM((rows, D), BF),
            pltpu.VMEM((rows, D), BF),
            pltpu.VMEM((D, LANES), F32),
            pltpu.VMEM((VEC_TOP, D), F32),
            pltpu.VMEM((2 + tensor_count, VEC_TOP, D), F32),
            pltpu.VMEM((4, VEC_TOP, D), F32),
            sem((chunks,)),
            sem((chunks,)),
            sem((2 * chunks,)),
            sem((2 * chunks,)),
            sem((chunks,)),
            sem((chunks,)),
            sem((zs,)),
            sem((zs,)),
            sem((2 + tensor_count,)),
            sem((2 + tensor_count,)),
            sem((2, 6)),
            sem((17,)),
            pltpu.SemaphoreType.REGULAR,
        ],
        compiler_params=pltpu.CompilerParams(
            collective_id=1, has_side_effects=True, vmem_limit_bytes=VMEM_LIMIT
        ),
        name="backward_scatter",
    )(*operands)


def copy_kernel(count, *refs):
    sources, targets = refs[:count], refs[count : 2 * count]
    buffers, (load_sem, store_sem) = refs[2 * count : 3 * count], refs[3 * count :]
    loads, stores = [], []
    for source, target, buffer in zip(sources, targets, buffers):
        rows = source.shape[0]
        pieces = 10 if rows >= 1024 else 1
        for piece in range(pieces):
            part = pl.ds(piece * (rows // pieces), rows // pieces)
            number = len(loads)
            loads.append(
                pltpu.make_async_copy(source.at[part], buffer.at[part], load_sem.at[number])
            )
            stores.append(
                pltpu.make_async_copy(buffer.at[part], target.at[part], store_sem.at[number])
            )
    for copy in loads:
        copy.start()
    for load, store in zip(loads, stores):
        load.wait()
        store.start()
    for copy in stores:
        copy.wait()


def hand_out(arrays):
    count = len(arrays)
    hbm = pl.BlockSpec(memory_space=pl.ANY)
    return pl.pallas_call(
        partial(copy_kernel, count),
        out_shape=[jax.ShapeDtypeStruct(array.shape, array.dtype) for array in arrays],
        in_specs=[hbm] * count,
        out_specs=[hbm] * count,
        scratch_shapes=[pltpu.VMEM(array.shape, array.dtype) for array in arrays]
        + [pltpu.SemaphoreType.DMA((10 + count,))] * 2,
        name="hand_out",
    )(*arrays)


def local_fused(
    latents,
    inputs,
    segment,
    cross_weights,
    self_weights,
    vectors,
    up_weight,
    down_weight,
    cotangent,
):
    tensor_count = lax.axis_size("tensor")
    shard = cross_weights.shape[0]
    seg = segment.reshape(-1, LANES)
    (
        latents_out,
        wc,
        ws,
        ctx,
        keys,
        vals,
        prob,
        gup,
        gdn,
        vecs,
        query,
        read,
        mid,
        query2,
        key2,
        val2,
        prob2,
        read2,
        late,
        gn3,
        gb1,
        inv,
    ) = forward_call(
        tensor_count,
        latents,
        inputs,
        seg,
        cross_weights,
        self_weights,
        up_weight,
        down_weight.T,
        vectors,
        cotangent,
    )
    operands = [latents, cotangent, mid, late, gn3, read, read2, query, query2, key2, val2]
    operands += [prob2, vecs, gb1, inv, wc, ws, ctx, keys, vals, prob, gup, gdn, inputs]
    glat, ginp, gcross, gself, gvec, gup_sum, gdn_sum, unused = backward_call(
        tensor_count, shard, vectors.shape, operands
    )
    results = hand_out([latents_out, glat, ginp, gcross, gself, gvec, gup_sum, gdn_sum])
    return (*results[:7], results[7].T)


def solution(mesh):
    placed = (
        P(("dp", "tensor"), None),
        P(("dp", "tensor"), None),
        P(("dp", "tensor")),
        P(("dp", "tensor"), None),
        P(("dp", "tensor"), None),
        P(None, ("dp", "tensor")),
        P("dp", "tensor"),
        P("tensor", "dp"),
        P(("dp", "tensor"), None),
    )
    shards = mesh.shape["dp"] * mesh.shape["tensor"]
    fused = mesh.shape["dp"] == 8 and mesh.shape["tensor"] == 4 and 4 * D % (32 * shards) == 0
    return jax.shard_map(
        local_fused if fused else local,
        mesh=mesh,
        in_specs=placed,
        out_specs=(
            P(("dp", "tensor"), None),
            P(("dp", "tensor"), None),
            P(("dp", "tensor"), None),
            P(("dp", "tensor"), None),
            P(("dp", "tensor"), None),
            P(None, ("dp", "tensor")),
            P("dp", "tensor"),
            P("tensor", "dp"),
        ),
        check_vma=False,
    )
```
